32 devices in a mesh: row: 8 (over z, y), col: 4 (over x, core).
Axes of the slice: x: 2, y: 2, z: 4, core: 2. Of those that a mesh axis runs over, the one named last changes fastest.
Arguments:
- features: float32 [8192, 128], P(('col', 'row')), may hold values from -6 to 6
- weight: float32 [128, 128], replicated, may hold values from -4 to 4
- bias_vector: float32 [128], replicated, may hold values from -4 to 4
- out_grad: float32 [8192, 128], P(('row', 'col')), may hold values from -6 to 6
- adj_tiles: int32 [8, 4, 128, 128, 128], P('row', 'col'), may hold values 0 or 1
- tile_slots: int32 [8, 4, 128], P('row', 'col'), may hold values from 0 to 127, as said below
- tile_counts: int32 [8, 4], P('row', 'col'), may hold values from 17 to 128, as said below
Outputs:
- activated: float32 [8192, 128], P(('row', 'col'))
- feature_grad: float32 [8192, 128], P(('col', 'row'))
- weight_grad: float32 [128, 128], replicated
- bias_grad: float32 [128], replicated
The draws below stay inside these ranges and needn't reach their ends.
Inputs may be any that keep to these rules, and one draw needn't show every extreme that they name: `tile_slots`: each block's slots name distinct positions r * 16 + c of its 8 x 16 tiles. Some block is full in every draw; slots from tile_counts on are ignored.
All inputs are finite; a program needn't handle non-finite values. No bound on the sum of `adj_tiles` on one device may be relied on, other than what follows from the above.
Results may differ from the reference program's by a relative error of at most 0.0003.
Values sent between devices are 32-bit elements; how exact they have to be, the bound alone decides.
No kernel may reach another device: no remote copies, remote signals or barrier semaphores. Data moves between devices by JAX's collectives and lax.ppermute only.
A program may use at most 128 MiB of HBM per device.

```python
import jax
import jax.numpy as jnp
from jax import lax

H = 128
TILE = 128
KT = 128
GRID_ROWS = 8
GRID_COLS = 4
TILE_ROWS = 8
TILE_COLS = 16
NODES = 8192


def draw_tile_slots(key, part):
    block_keys = jax.random.split(jax.random.fold_in(key, 11), GRID_ROWS * GRID_COLS)

    def one_block(block_key):
        return jax.random.permutation(block_key, TILE_ROWS * TILE_COLS)[:KT]
    return jax.vmap(one_block)(block_keys).reshape(GRID_ROWS, GRID_COLS, KT).astype(jnp.int32)


def draw_tile_counts(key, part):
    first_key, second_key = jax.random.split(jax.random.fold_in(key, 23))
    counts = jax.random.randint(first_key, (GRID_ROWS * GRID_COLS,), KT // 8 + 1, KT // 2 + 1)
    busiest = jax.random.randint(second_key, (), 0, GRID_ROWS * GRID_COLS)
    counts = jnp.where(jnp.arange(GRID_ROWS * GRID_COLS) == busiest, KT, counts)
    return counts.reshape(GRID_ROWS, GRID_COLS).astype(jnp.int32)


def touch_ends(drawn, rng, least, top_value):
    extent = drawn.shape
    place = [jax.random.randint(jax.random.fold_in(rng, axis), (), 0, extent[axis]) for axis in range(len(extent))]
    drawn = drawn.at[tuple(place)].set(least)
    longest = extent.index(max(extent))
    place[longest] = (place[longest] + 1) % extent[longest]
    return drawn.at[tuple(place)].set(top_value)


def steps_of(stream_key, dims, pieces, least, largest):
    def one(position, parts):
        draws = jax.random.uniform(jax.random.fold_in(jax.random.fold_in(stream_key, 6), position), (parts,), jnp.float32, least / len(pieces), largest / len(pieces))
        return jnp.repeat(jnp.exp(draws), dims[position] // parts).reshape((-1,) + (1,) * (len(dims) - position - 1))

    level = one(*pieces[0])
    for cut in pieces[1:]:
        level = level * one(*cut)
    return level


def gaussian(rng, extent, scale, bound, cuts=(), held_as=jnp.bfloat16):
    level = steps_of(rng, extent, cuts, -0.22, 0.18) if cuts else 1.0
    entries = jax.random.normal(rng, extent, jnp.float32) * scale * level
    return jnp.minimum(jnp.maximum(entries, -bound), bound).astype(held_as)


def setup_inputs(seed: int = 0) -> dict:
    seeds = jax.random.split(jax.random.key(seed), 8)
    features = gaussian(seeds[0], (NODES, H), 1.0, 6.0, ((0, 32),), jnp.float32)
    weight = gaussian(seeds[1], (H, H), 1.0, 4.0, (), jnp.float32)
    bias_vector = gaussian(seeds[2], (H,), 1.0, 4.0, (), jnp.float32)
    out_grad = gaussian(seeds[3], (NODES, H), 1.0, 6.0, ((0, 32),), jnp.float32)
    adj_tiles = touch_ends((jax.random.randint(seeds[4], (GRID_ROWS, GRID_COLS, KT, TILE, TILE), 0, 8) < 1).astype(jnp.int32), jax.random.fold_in(seeds[4], 1), 0, 1)
    tile_slots = draw_tile_slots(jax.random.fold_in(seeds[7], 71), 0)
    tile_counts = draw_tile_counts(jax.random.fold_in(seeds[7], 71), 0)
    return {"features": features, "weight": weight, "bias_vector": bias_vector, "out_grad": out_grad, "adj_tiles": adj_tiles, "tile_slots": tile_slots, "tile_counts": tile_counts}


def selectors(slots, slot_count, tile_rows, tile_cols):
    live_mask = (jnp.arange(slots.shape[0]) < slot_count).astype(jnp.float32)
    tile_row = slots // tile_cols
    tile_col = slots % tile_cols
    row_select = (tile_row[:, None] == jnp.arange(tile_rows)[None, :]).astype(jnp.float32)
    col_select = (tile_col[:, None] == jnp.arange(tile_cols)[None, :]).astype(jnp.float32)
    return (live_mask, row_select, col_select)

def reference(features, weight, bias_vector, out_grad, adj_tiles, tile_slots, tile_counts):
    grid_rows = adj_tiles.shape[0]
    grid_cols = adj_tiles.shape[1]
    flat_tiles = adj_tiles.reshape(grid_rows * grid_cols, KT, TILE, TILE)
    flat_slots = tile_slots.reshape(grid_rows * grid_cols, KT)
    flat_counts = tile_counts.reshape(grid_rows * grid_cols)

    def degree_parts(item):
        tile_block, slots, slot_count = item
        adjacency = tile_block.astype(jnp.float32)
        live_mask, row_select, col_select = selectors(slots, slot_count, TILE_ROWS, TILE_COLS)
        dst_partial = jnp.dot((row_select * live_mask[:, None]).T, lax.optimization_barrier(jnp.sum(adjacency, axis=2)), precision=lax.Precision.HIGHEST)
        src_partial = jnp.dot((col_select * live_mask[:, None]).T, lax.optimization_barrier(jnp.sum(adjacency, axis=1)), precision=lax.Precision.HIGHEST)
        return (dst_partial.reshape(-1), src_partial.reshape(-1))
    dst_parts, src_parts = lax.map(degree_parts, (flat_tiles, flat_slots, flat_counts))
    dst_degree = 1.0 + lax.optimization_barrier(jnp.sum(dst_parts.reshape(grid_rows, grid_cols, -1), axis=1)).reshape(-1)
    src_degree = 1.0 + lax.optimization_barrier(jnp.sum(src_parts.reshape(grid_rows, grid_cols, -1), axis=0)).reshape(-1)
    dst_scale = lax.rsqrt(dst_degree)
    src_scale = lax.rsqrt(src_degree)
    scaled = features * src_scale[:, None]
    scaled_blocks = scaled.reshape(grid_cols, TILE_COLS, TILE, H)

    def forward_row(row_index):

        def add_block(total, col_index):
            adjacency = adj_tiles[row_index, col_index].astype(jnp.float32)
            live_mask, row_select, col_select = selectors(tile_slots[row_index, col_index], tile_counts[row_index, col_index], TILE_ROWS, TILE_COLS)
            taken = jnp.einsum('kc,cbh->kbh', col_select, scaled_blocks[col_index], precision=lax.Precision.HIGHEST)
            product = jnp.einsum('kab,kbh->kah', adjacency, taken, precision=lax.Precision.HIGHEST)
            return (total + jnp.einsum('kr,kah->rah', row_select * live_mask[:, None], product, precision=lax.Precision.HIGHEST), None)
        total, unused = lax.scan(add_block, jnp.zeros((TILE_ROWS, TILE, H), jnp.float32), jnp.arange(grid_cols))
        return total
    aggregated = lax.map(forward_row, jnp.arange(grid_rows)).reshape(NODES, H) * dst_scale[:, None]
    preact = jnp.dot(aggregated, weight, precision=lax.Precision.HIGHEST) + bias_vector
    logistic = jax.nn.sigmoid(preact)
    activated = preact * logistic
    pre_grad = out_grad * logistic * (1.0 + preact * (1.0 - logistic))
    weight_grad = jnp.dot(aggregated.T, pre_grad, precision=lax.Precision.HIGHEST)
    bias_grad = lax.optimization_barrier(jnp.sum(pre_grad, axis=0))
    row_grads = jnp.dot(pre_grad, weight.T, precision=lax.Precision.HIGHEST) * dst_scale[:, None]
    row_blocks = row_grads.reshape(grid_rows, TILE_ROWS, TILE, H)

    def backward_col(col_index):

        def add_block(total, row_index):
            adjacency = adj_tiles[row_index, col_index].astype(jnp.float32)
            live_mask, row_select, col_select = selectors(tile_slots[row_index, col_index], tile_counts[row_index, col_index], TILE_ROWS, TILE_COLS)
            taken = jnp.einsum('kr,rah->kah', row_select, row_blocks[row_index], precision=lax.Precision.HIGHEST)
            product = jnp.einsum('kab,kah->kbh', adjacency, taken, precision=lax.Precision.HIGHEST)
            return (total + jnp.einsum('kc,kbh->cbh', col_select * live_mask[:, None], product, precision=lax.Precision.HIGHEST), None)
        total, unused = lax.scan(add_block, jnp.zeros((TILE_COLS, TILE, H), jnp.float32), jnp.arange(grid_rows))
        return total
    feature_grad = lax.map(backward_col, jnp.arange(grid_cols)).reshape(NODES, H) * src_scale[:, None]
    return (activated, feature_grad, weight_grad, bias_grad)
```

```python
import functools

import jax
import jax.numpy as jnp
from jax import lax
from jax.experimental import pallas as pl
from jax.experimental.pallas import tpu as pltpu
from jax.sharding import PartitionSpec as P

TILE = 128
PAD = 8
F32 = jnp.float32
BF16 = jnp.bfloat16
HIGHEST = lax.Precision.HIGHEST
VMEM_LIMIT = 56 * 1024 * 1024


def nt_dot(lhs, rhs, **kw):
    return lax.dot_general(lhs, rhs, (((1,), (1,)), ((), ())), preferred_element_type=F32, **kw)


def tn_dot(lhs, rhs, **kw):
    return lax.dot_general(lhs, rhs, (((0,), (0,)), ((), ())), preferred_element_type=F32, **kw)


def split(value):
    high = value.astype(BF16)
    low = (value - high.astype(F32)).astype(BF16)
    return high, low


def vmem_specs(count):
    return [pl.BlockSpec(memory_space=pltpu.VMEM)] * count


def params():
    return pltpu.CompilerParams(vmem_limit_bytes=VMEM_LIMIT)


def cost(flops, moved):
    return pl.CostEstimate(flops=int(flops), bytes_accessed=int(moved), transcendentals=0)


def densify_kernel(
    tile_rows, tile_cols, pieces, slots_ref, counts_ref, tiles_hbm,
    dense_ref, col_ref, row_ref, tiles, col_acc, row_acc, sems,
):
    slot_total = tiles.shape[0]
    piece = slot_total // pieces
    copies = [
        pltpu.make_async_copy(
            tiles_hbm.at[pl.ds(p * piece, piece)], tiles.at[pl.ds(p * piece, piece)], sems.at[p]
        )
        for p in range(pieces)
    ]
    for copy in copies:
        copy.start()
    if slot_total < tile_rows * tile_cols:
        dense_ref[...] = jnp.zeros_like(dense_ref)
    col_acc[...] = jnp.zeros_like(col_acc)
    row_acc[...] = jnp.zeros_like(row_acc)
    live = counts_ref[0]

    def place(k, carry):
        slot = slots_ref[k]
        r = slot // tile_cols
        c = slot % tile_cols
        keep = jnp.where(k < live, 1, 0)
        tile = tiles[k] * keep
        dense_ref[
            pl.ds(pl.multiple_of(r * TILE, TILE), TILE), pl.ds(pl.multiple_of(c * TILE, TILE), TILE)
        ] = tile.astype(F32).astype(BF16)
        col_acc[c] += jnp.sum(tile.reshape(TILE // 8, 8, TILE), axis=0)
        row_acc[r] += tile
        return carry

    for p in range(pieces):
        copies[p].wait()
        lax.fori_loop(p * piece, (p + 1) * piece, place, 0, unroll=4)
    col_ref[...] = jnp.sum(col_acc[...], axis=1).astype(F32)
    ones = jnp.ones((8, TILE), BF16)
    for r in range(tile_rows):
        sums = nt_dot(ones, row_acc[r].astype(F32).astype(BF16))
        row_ref[pl.ds(r, 1), :] = sums[0:1, :]


def densify(slots, counts, tiles, tile_rows, tile_cols):
    slot_total = tiles.shape[0]
    pieces = 8
    rows, cols = tile_rows * TILE, tile_cols * TILE
    return pl.pallas_call(
        functools.partial(densify_kernel, tile_rows, tile_cols, pieces),
        out_shape=(
            jax.ShapeDtypeStruct((rows, cols), BF16),
            jax.ShapeDtypeStruct((tile_cols, TILE), F32),
            jax.ShapeDtypeStruct((tile_rows, TILE), F32),
        ),
        in_specs=[
            pl.BlockSpec(memory_space=pltpu.SMEM),
            pl.BlockSpec(memory_space=pltpu.SMEM),
            pl.BlockSpec(memory_space=pl.ANY),
        ],
        out_specs=tuple(vmem_specs(3)),
        scratch_shapes=[
            pltpu.VMEM(tiles.shape, jnp.int32),
            pltpu.VMEM((tile_cols, 8, TILE), jnp.int32),
            pltpu.VMEM((tile_rows, TILE, TILE), jnp.int32),
            pltpu.SemaphoreType.DMA((pieces,)),
        ],
        compiler_params=params(),
        cost_estimate=cost(0, slot_total * TILE * TILE * 4 + rows * cols * 2),
        name="densify",
    )(slots, counts, tiles)


def scales_kernel(parts, own_tiles, *refs):
    sums, (wide_ref, own_ref) = refs[:parts], refs[parts:]
    total = sums[0][...]
    for ref in sums[1:]:
        total = total + ref[...]
    scale = lax.rsqrt(1.0 + total)
    tile_cols = scale.shape[0]
    for c in range(tile_cols):
        wide_ref[pl.ds(c * TILE, TILE), :] = jnp.broadcast_to(scale[c : c + 1, :], (TILE, TILE)).T
    own_ref[...] = scale


def source_scales(sums, own_tiles):
    tile_cols = sums[0].shape[0]
    return pl.pallas_call(
        functools.partial(scales_kernel, len(sums), own_tiles),
        out_shape=(
            jax.ShapeDtypeStruct((tile_cols * TILE, TILE), F32),
            jax.ShapeDtypeStruct((tile_cols, TILE), F32),
        ),
        in_specs=vmem_specs(len(sums)),
        out_specs=tuple(vmem_specs(2)),
        compiler_params=params(),
        cost_estimate=cost(0, tile_cols * TILE * TILE * 8),
        name="source_scales",
    )(*sums)


def forward_kernel(row_count, col_count, *refs):
    dense_ref, wide_ref, row_ref = refs[:3]
    blocks = refs[3 : 3 + row_count]
    outs = refs[3 + row_count : 3 + row_count + col_count]
    rhs = refs[-1]
    row = lax.axis_index("row")
    col = lax.axis_index("col")
    node_rows, width = blocks[0].shape
    for m in range(row_count):
        start = pl.multiple_of((row ^ m) * node_rows, node_rows)
        high, low = split(blocks[m][...] * wide_ref[pl.ds(start, node_rows), :])
        rhs[pl.ds(start, node_rows), :width] = high
        rhs[pl.ds(start, node_rows), width:] = low
    own_tiles = node_rows // TILE
    for m in list(range(1, col_count)) + [0]:
        peer = col ^ m
        start = pl.multiple_of(peer * node_rows, node_rows)
        both = jnp.dot(dense_ref[pl.ds(start, node_rows), :], rhs[...], preferred_element_type=F32)
        outs[m][pl.ds(0, node_rows), :] = both[:, :width] + both[:, width:]
        outs[m][pl.ds(node_rows, PAD), :] = jnp.zeros((PAD, width), F32)
        for t in range(own_tiles):
            outs[m][pl.ds(node_rows + t, 1), :] = row_ref[pl.ds(peer * own_tiles + t, 1), :]


def forward(dense, wide, row_sums, blocks, row_count, col_count):
    node_rows, width = blocks[0].shape
    rows, cols = dense.shape
    return pl.pallas_call(
        functools.partial(forward_kernel, row_count, col_count),
        out_shape=tuple(
            jax.ShapeDtypeStruct((node_rows + PAD, width), F32) for _ in range(col_count)
        ),
        in_specs=vmem_specs(3 + row_count),
        out_specs=tuple(vmem_specs(col_count)),
        scratch_shapes=[pltpu.VMEM((cols, 2 * width), BF16)],
        compiler_params=params(),
        cost_estimate=cost(4 * rows * cols * width, rows * cols * 2),
        name="forward",
    )(dense, wide, row_sums, *blocks)


def node_kernel(parts, *refs):
    pieces = refs[:parts]
    cot_ref, weight_ref, bias_ref, act_ref, back_ref, grad_ref = refs[parts:]
    node_rows, width = cot_ref.shape
    total = pieces[0][...]
    for ref in pieces[1:]:
        total = total + ref[...]
    own_tiles = node_rows // TILE
    scale = lax.rsqrt(1.0 + total[node_rows:, :])
    wide = jnp.concatenate(
        [jnp.broadcast_to(scale[t : t + 1, :], (TILE, TILE)).T for t in range(own_tiles)], axis=0
    )
    flat = jnp.concatenate([scale[t : t + 1, :] for t in range(own_tiles)], axis=1)
    weight = weight_ref[...]
    aggregated = total[:node_rows, :] * wide
    preact = (
        jnp.dot(aggregated, weight, precision=HIGHEST, preferred_element_type=F32) + bias_ref[...]
    )
    logistic = jax.nn.sigmoid(preact)
    act_ref[...] = preact * logistic
    pre_grad = cot_ref[...] * logistic * (1.0 + preact * (1.0 - logistic))
    back_ref[...] = nt_dot(weight, pre_grad, precision=HIGHEST) * flat
    grad_ref[pl.ds(0, width), :] = tn_dot(aggregated, pre_grad, precision=HIGHEST)
    grad_ref[pl.ds(width, PAD), :] = jnp.broadcast_to(
        jnp.sum(pre_grad, axis=0, keepdims=True), (PAD, width)
    )


def node_step(pieces, cotangent, weight, bias):
    node_rows, width = cotangent.shape
    return pl.pallas_call(
        functools.partial(node_kernel, len(pieces)),
        out_shape=(
            jax.ShapeDtypeStruct((node_rows, width), F32),
            jax.ShapeDtypeStruct((width, node_rows), F32),
            jax.ShapeDtypeStruct((width + PAD, width), F32),
        ),
        in_specs=vmem_specs(len(pieces) + 3),
        out_specs=tuple(vmem_specs(3)),
        compiler_params=params(),
        cost_estimate=cost(6 * 6 * node_rows * width * width, 4 * 8 * node_rows * width),
        name="node_step",
    )(*pieces, cotangent, weight, bias)


def backward_kernel(row_count, col_count, grad_parts, *refs):
    dense_ref = refs[0]
    blocks = refs[1 : 1 + col_count]
    grads = refs[1 + col_count : 1 + col_count + grad_parts]
    rest = refs[1 + col_count + grad_parts :]
    outs, sum_ref, lhs = rest[:row_count], rest[row_count], rest[row_count + 1]
    row = lax.axis_index("row")
    col = lax.axis_index("col")
    width, node_rows = blocks[0].shape
    for m in range(col_count):
        start = pl.multiple_of((col ^ m) * node_rows, node_rows)
        high, low = split(blocks[m][...])
        lhs[:width, pl.ds(start, node_rows)] = high
        lhs[width:, pl.ds(start, node_rows)] = low
    for m in list(range(1, row_count)) + [0]:
        start = pl.multiple_of((row ^ m) * node_rows, node_rows)
        both = jnp.dot(lhs[...], dense_ref[:, pl.ds(start, node_rows)], preferred_element_type=F32)
        outs[m][...] = both[:width, :] + both[width:, :]
    total = grads[0][...]
    for ref in grads[1:]:
        total = total + ref[...]
    sum_ref[...] = total


def backward(dense, blocks, grads, row_count):
    width, node_rows = blocks[0].shape
    rows, cols = dense.shape
    return pl.pallas_call(
        functools.partial(backward_kernel, row_count, len(blocks), len(grads)),
        out_shape=tuple(jax.ShapeDtypeStruct((width, node_rows), F32) for _ in range(row_count))
        + (jax.ShapeDtypeStruct(grads[0].shape, F32),),
        in_specs=vmem_specs(1 + len(blocks) + len(grads)),
        out_specs=tuple(vmem_specs(row_count + 1)),
        scratch_shapes=[pltpu.VMEM((2 * width, rows), BF16)],
        compiler_params=params(),
        cost_estimate=cost(4 * rows * cols * width, rows * cols * 2),
        name="backward",
    )(dense, *blocks, *grads)


def sums_kernel(counts, *refs):
    outs = refs[sum(counts) :]
    at = 0
    for out_ref, count in zip(outs, counts):
        total = refs[at][...]
        for ref in refs[at + 1 : at + count]:
            total = total + ref[...]
        out_ref[...] = total
        at += count


def sums(*groups):
    flat = [array for group in groups for array in group]
    return pl.pallas_call(
        functools.partial(sums_kernel, tuple(len(group) for group in groups)),
        out_shape=tuple(jax.ShapeDtypeStruct(group[0].shape, F32) for group in groups),
        in_specs=vmem_specs(len(flat)),
        out_specs=tuple(vmem_specs(len(groups))),
        compiler_params=params(),
        cost_estimate=cost(0, sum(4 * array.size for array in flat)),
        name="sums",
    )(*flat)


def finish_kernel(parts, grad_parts, *refs):
    pieces = refs[:parts]
    grads = refs[parts : parts + grad_parts]
    scale_ref, out_ref, weight_ref, bias_ref = refs[parts + grad_parts :]
    row = lax.axis_index("row")
    total = pieces[0][...]
    for ref in pieces[1:]:
        total = total + ref[...]
    width, node_rows = total.shape
    own_tiles = node_rows // TILE
    for t in range(own_tiles):
        part = total[:, t * TILE : (t + 1) * TILE] * scale_ref[pl.ds(row * own_tiles + t, 1), :]
        out_ref[pl.ds(t * TILE, TILE), :] = part.T
    total = grads[0][...]
    for ref in grads[1:]:
        total = total + ref[...]
    weight_ref[...] = total[:width, :]
    bias_ref[...] = total[width : width + 1, :]


def finish(pieces, grads, scale):
    width, node_rows = pieces[0].shape
    return pl.pallas_call(
        functools.partial(finish_kernel, len(pieces), len(grads)),
        out_shape=(
            jax.ShapeDtypeStruct((node_rows, width), F32),
            jax.ShapeDtypeStruct((width, width), F32),
            jax.ShapeDtypeStruct((1, width), F32),
        ),
        in_specs=vmem_specs(len(pieces) + len(grads) + 1),
        out_specs=tuple(vmem_specs(3)),
        compiler_params=params(),
        cost_estimate=cost(0, 4 * 6 * node_rows * width),
        name="finish",
    )(*pieces, *grads, scale)


def swap(value, axis, mask):
    count = lax.axis_size(axis)
    return lax.ppermute(value, axis, [(i, i ^ mask) for i in range(count)])


def local(features, weight, bias_vector, out_grad, adj_tiles, tile_slots, tile_counts):
    row_count = lax.axis_size("row")
    col_count = lax.axis_size("col")
    node_rows, width = features.shape
    tile_rows = node_rows * col_count // TILE
    tile_cols = node_rows * row_count // TILE
    top = row_count // 2

    blocks = [None] * row_count
    blocks[0] = features
    blocks[top] = swap(features, "row", top)
    for m in range(1, top):
        blocks[m] = swap(features, "row", m)
    for m in range(1, top):
        blocks[top | m] = swap(blocks[top], "row", m)

    dense, col_sums, row_sums = densify(
        tile_slots[0, 0], tile_counts[0], adj_tiles[0, 0], tile_rows, tile_cols
    )
    col_parts = [col_sums] + [swap(col_sums, "row", m) for m in range(1, row_count)]
    wide, scale = source_scales(col_parts, node_rows // TILE)
    partial = forward(dense, wide, row_sums, blocks, row_count, col_count)
    pieces = [partial[0]] + [swap(partial[m], "col", m) for m in range(1, col_count)]
    activated, back, grads = node_step(pieces, out_grad, weight, bias_vector[None, :])

    backs = [back] + [swap(back, "col", m) for m in range(1, col_count)]
    late = 2
    early = [m for m in range(1, row_count) if not m & late]
    grad_parts = [grads] + [swap(grads, "row", m) for m in early]
    out = backward(dense, backs, grad_parts, row_count)
    chunks, grads = out[:row_count], out[row_count]

    ahead = [chunks[top]] + [swap(chunks[top | m], "row", m) for m in range(1, top)]
    mine = [chunks[0]] + [swap(chunks[m], "row", m) for m in range(1, top)]
    grad_parts = [grads] + [swap(grads, "col", m) for m in range(1, col_count)]
    passed, grads = sums(ahead, grad_parts)
    mine.append(swap(passed, "row", top))
    grad_parts = [grads, swap(grads, "row", late)]
    feature_grad, weight_grad, bias_grad = finish(mine, grad_parts, scale)
    return activated, feature_grad, weight_grad, bias_grad[0]


def solution(mesh):
    return jax.shard_map(
        local,
        mesh=mesh,
        in_specs=(
            P(("col", "row"), None),
            P(),
            P(),
            P(("row", "col"), None),
            P("row", "col", None, None, None),
            P("row", "col", None),
            P("row", "col"),
        ),
        out_specs=(P(("row", "col"), None), P(("col", "row"), None), P(), P()),
        check_vma=False,
    )
```

```python
import functools

import jax
import jax.numpy as jnp
from jax import lax
from jax.experimental import pallas as pl
from jax.experimental.pallas import tpu as pltpu
from jax.sharding import PartitionSpec as P

TILE = 128
PAD = 8
F32 = jnp.float32
BF16 = jnp.bfloat16
HIGHEST = lax.Precision.HIGHEST
MIB = 1024 * 1024


def nt_dot(lhs, rhs, **kw):
    return lax.dot_general(lhs, rhs, (((1,), (1,)), ((), ())), preferred_element_type=F32, **kw)


def tn_dot(lhs, rhs, **kw):
    return lax.dot_general(lhs, rhs, (((0,), (0,)), ((), ())), preferred_element_type=F32, **kw)


def split(value):
    high = value.astype(BF16)
    low = (value - high.astype(F32)).astype(BF16)
    return high, low


def total_of(refs):
    total = refs[0][...]
    for ref in refs[1:]:
        total = total + ref[...]
    return total


def vmem(*shape, dtype=F32):
    return pltpu.VMEM(shape, dtype)


def hbm(*shape, dtype=F32):
    return jax.ShapeDtypeStruct(shape, dtype)


def call(kernel, name, args, outs, flops=0, room=4, scratch=(), before=(), before_specs=()):
    spec = pl.BlockSpec(memory_space=pltpu.VMEM)
    return pl.pallas_call(
        kernel,
        out_shape=tuple(outs),
        in_specs=list(before_specs) + [spec] * len(args),
        out_specs=(spec,) * len(outs),
        scratch_shapes=list(scratch),
        compiler_params=pltpu.CompilerParams(vmem_limit_bytes=room * MIB),
        cost_estimate=pl.CostEstimate(
            flops=int(flops), bytes_accessed=sum(4 * arg.size for arg in args), transcendentals=0
        ),
        name=name,
    )(*before, *[pltpu.with_memory_space_constraint(arg, pltpu.VMEM) for arg in args])


def densify_kernel(
    tile_rows, tile_cols, pieces, slots_ref, counts_ref, tiles_hbm,
    dense_ref, col_ref, row_ref, tiles, col_acc, row_acc, sems,
):
    slot_total = tiles.shape[0]
    piece = slot_total // pieces
    copies = [
        pltpu.make_async_copy(
            tiles_hbm.at[pl.ds(p * piece, piece)], tiles.at[pl.ds(p * piece, piece)], sems.at[p]
        )
        for p in range(pieces)
    ]
    for copy in copies:
        copy.start()
    if slot_total < tile_rows * tile_cols:
        dense_ref[...] = jnp.zeros_like(dense_ref)
    col_acc[...] = jnp.zeros_like(col_acc)
    row_acc[...] = jnp.zeros_like(row_acc)
    live = counts_ref[0]

    def place(k, carry):
        slot = slots_ref[k]
        r = slot // tile_cols
        c = slot % tile_cols
        keep = jnp.where(k < live, 1, 0)
        tile = tiles[k] * keep
        dense_ref[
            pl.ds(pl.multiple_of(r * TILE, TILE), TILE), pl.ds(pl.multiple_of(c * TILE, TILE), TILE)
        ] = tile.astype(F32).astype(BF16)
        col_acc[c] += jnp.sum(tile.reshape(TILE // 8, 8, TILE), axis=0)
        row_acc[r] += tile
        return carry

    for p in range(pieces):
        copies[p].wait()
        lax.fori_loop(p * piece, (p + 1) * piece, place, 0, unroll=4)
    col_ref[...] = jnp.sum(col_acc[...], axis=1).astype(F32)
    ones = jnp.ones((8, TILE), BF16)
    for r in range(tile_rows):
        sums = nt_dot(ones, row_acc[r].astype(F32).astype(BF16))
        row_ref[pl.ds(r, 1), :] = sums[0:1, :]


def densify(slots, counts, tiles, tile_rows, tile_cols):
    pieces = 8
    return call(
        functools.partial(densify_kernel, tile_rows, tile_cols, pieces),
        "densify",
        (),
        (
            vmem(tile_rows * TILE, tile_cols * TILE, dtype=BF16),
            vmem(tile_cols, TILE),
            vmem(tile_rows, TILE),
        ),
        flops=tiles.size * 400,
        room=16,
        scratch=(
            vmem(*tiles.shape, dtype=jnp.int32),
            vmem(tile_cols, 8, TILE, dtype=jnp.int32),
            vmem(tile_rows, TILE, TILE, dtype=jnp.int32),
            pltpu.SemaphoreType.DMA((pieces,)),
        ),
        before=(slots, counts, pltpu.with_memory_space_constraint(tiles, pltpu.HBM)),
        before_specs=(
            pl.BlockSpec(memory_space=pltpu.SMEM),
            pl.BlockSpec(memory_space=pltpu.SMEM),
            pl.BlockSpec(memory_space=pl.ANY),
        ),
    )


def scales_kernel(*refs):
    parts, (wide_ref, scale_ref) = refs[:-2], refs[-2:]
    scale = lax.rsqrt(1.0 + total_of(parts))
    for c in range(scale.shape[0]):
        wide_ref[pl.ds(c * TILE, TILE), :] = jnp.broadcast_to(scale[c : c + 1, :], (TILE, TILE)).T
    scale_ref[...] = scale


def source_scales(parts):
    tile_cols = parts[0].shape[0]
    return call(
        scales_kernel,
        "source_scales",
        parts,
        (vmem(tile_cols * TILE, TILE), vmem(tile_cols, TILE)),
    )


def forward_chunks(peers, dense_ref, row_ref, rhs, out_ref):
    col = lax.axis_index("col")
    node_rows, width = out_ref.shape[1] - PAD, out_ref.shape[2]
    own_tiles = node_rows // TILE
    for h, m in enumerate(peers):
        peer = col ^ m
        start = pl.multiple_of(peer * node_rows, node_rows)
        both = jnp.dot(dense_ref[pl.ds(start, node_rows), :], rhs[...], preferred_element_type=F32)
        out_ref[h, pl.ds(0, node_rows), :] = both[:, :width] + both[:, width:]
        out_ref[h, pl.ds(node_rows, PAD), :] = jnp.zeros((PAD, width), F32)
        for t in range(own_tiles):
            out_ref[h, pl.ds(node_rows + t, 1), :] = row_ref[pl.ds(peer * own_tiles + t, 1), :]


def forward_first_kernel(peers, row_count, *refs):
    dense_ref, row_ref, wide_ref = refs[:3]
    blocks = refs[3 : 3 + row_count]
    out_ref, rhs = refs[3 + row_count :]
    row = lax.axis_index("row")
    node_rows, width = blocks[0].shape
    for m in range(row_count):
        start = pl.multiple_of((row ^ m) * node_rows, node_rows)
        high, low = split(blocks[m][...] * wide_ref[pl.ds(start, node_rows), :])
        rhs[pl.ds(start, node_rows), :width] = high
        rhs[pl.ds(start, node_rows), width:] = low
    forward_chunks(peers, dense_ref, row_ref, rhs, out_ref)


def forward_second_kernel(peers, dense_ref, row_ref, rhs, out_ref):
    forward_chunks(peers, dense_ref, row_ref, rhs, out_ref)


def forward_first(peers, dense, row_sums, wide, blocks):
    node_rows, width = blocks[0].shape
    cols = dense.shape[1]
    return call(
        functools.partial(forward_first_kernel, peers, len(blocks)),
        "forward_first",
        (dense, row_sums, wide, *blocks),
        (vmem(len(peers), node_rows + PAD, width), vmem(cols, 2 * width, dtype=BF16)),
        flops=4 * len(peers) * node_rows * cols * width,
    )


def forward_second(peers, dense, row_sums, rhs, node_rows):
    cols = dense.shape[1]
    width = rhs.shape[1] // 2
    return call(
        functools.partial(forward_second_kernel, peers),
        "forward_second",
        (dense, row_sums, rhs),
        (vmem(len(peers), node_rows + PAD, width),),
        flops=4 * len(peers) * node_rows * cols * width,
    )[0]


def pair_kernel(kept_ref, got_ref, *outs):
    for h, out_ref in enumerate(outs):
        out_ref[...] = kept_ref[h + 1] + got_ref[h + 1]


def pair_sums(kept, got):
    return call(
        pair_kernel, "pair_sums", (kept, got), [vmem(*kept.shape[1:])] * (kept.shape[0] - 1)
    )


def node_kernel(*refs):
    kept_ref, got_ref = refs[:2]
    others = refs[2:-7]
    cot_ref, weight_ref, bias_ref, act_ref, back_ref, agg_ref, pre_ref = refs[-7:]
    node_rows, width = cot_ref.shape
    total = kept_ref[0] + got_ref[0]
    for ref in others:
        total = total + ref[...]
    own_tiles = node_rows // TILE
    scale = lax.rsqrt(1.0 + total[node_rows:, :])
    wide = jnp.concatenate(
        [jnp.broadcast_to(scale[t : t + 1, :], (TILE, TILE)).T for t in range(own_tiles)], axis=0
    )
    flat = jnp.concatenate([scale[t : t + 1, :] for t in range(own_tiles)], axis=1)
    weight = weight_ref[...]
    aggregated = total[:node_rows, :] * wide
    preact = (
        jnp.dot(aggregated, weight, precision=HIGHEST, preferred_element_type=F32) + bias_ref[...]
    )
    logistic = jax.nn.sigmoid(preact)
    act_ref[...] = preact * logistic
    pre_grad = cot_ref[...] * logistic * (1.0 + preact * (1.0 - logistic))
    back_ref[...] = nt_dot(weight, pre_grad, precision=HIGHEST) * flat
    agg_ref[...] = aggregated
    pre_ref[...] = pre_grad


def node_step(kept, got, others, cotangent, weight, bias):
    node_rows, width = cotangent.shape
    return call(
        node_kernel,
        "node_step",
        (kept, got, *others, cotangent, weight, bias),
        (
            vmem(node_rows, width),
            vmem(width, node_rows),
            vmem(node_rows, width),
            vmem(node_rows, width),
        ),
        flops=24 * node_rows * width * width,
    )


def grads_kernel(agg_ref, pre_ref, out_ref):
    width = agg_ref.shape[1]
    pre_grad = pre_ref[...]
    out_ref[pl.ds(0, width), :] = tn_dot(agg_ref[...], pre_grad, precision=HIGHEST)
    out_ref[pl.ds(width, PAD), :] = jnp.broadcast_to(
        jnp.sum(pre_grad, axis=0, keepdims=True), (PAD, width)
    )


def weight_parts(aggregated, pre_grad):
    node_rows, width = aggregated.shape
    return call(
        grads_kernel,
        "weight_parts",
        (aggregated, pre_grad),
        (vmem(width + PAD, width),),
        flops=12 * node_rows * width * width,
    )[0]


def backward_chunks(peers, dense_ref, lhs, outs):
    row = lax.axis_index("row")
    width, node_rows = outs[0].shape
    for m, out_ref in zip(peers, outs):
        start = pl.multiple_of((row ^ m) * node_rows, node_rows)
        both = jnp.dot(lhs[...], dense_ref[:, pl.ds(start, node_rows)], preferred_element_type=F32)
        out_ref[...] = both[:width, :] + both[width:, :]


def backward_first_kernel(peers, col_count, *refs):
    dense_ref = refs[0]
    blocks = refs[1 : 1 + col_count]
    outs, lhs = refs[1 + col_count : -1], refs[-1]
    col = lax.axis_index("col")
    width, node_rows = blocks[0].shape
    for m in range(col_count):
        start = pl.multiple_of((col ^ m) * node_rows, node_rows)
        high, low = split(blocks[m][...])
        lhs[:width, pl.ds(start, node_rows)] = high
        lhs[width:, pl.ds(start, node_rows)] = low
    backward_chunks(peers, dense_ref, lhs, outs)


def backward_second_kernel(peers, dense_ref, lhs, *outs):
    backward_chunks(peers, dense_ref, lhs, outs)


def backward_first(peers, dense, blocks):
    width, node_rows = blocks[0].shape
    rows = dense.shape[0]
    out = call(
        functools.partial(backward_first_kernel, peers, len(blocks)),
        "backward_first",
        (dense, *blocks),
        [vmem(width, node_rows)] * len(peers) + [vmem(2 * width, rows, dtype=BF16)],
        flops=4 * len(peers) * node_rows * rows * width,
    )
    return dict(zip(peers, out)), out[-1]


def backward_second(peers, dense, lhs, node_rows):
    rows = dense.shape[0]
    width = lhs.shape[0] // 2
    out = call(
        functools.partial(backward_second_kernel, peers),
        "backward_second",
        (dense, lhs),
        [vmem(width, node_rows)] * len(peers),
        flops=4 * len(peers) * node_rows * rows * width,
    )
    return dict(zip(peers, out))


def sum_kernel(*refs):
    refs[-1][...] = total_of(refs[:-1])


def sum_all(parts, name):
    return call(sum_kernel, name, parts, (vmem(*parts[0].shape),))[0]


def finish_kernel(parts, *refs):
    total = total_of(refs[:parts])
    grads = total_of(refs[parts:-4])
    scale_ref, out_ref, weight_ref, bias_ref = refs[-4:]
    row = lax.axis_index("row")
    width, node_rows = total.shape
    own_tiles = node_rows // TILE
    for t in range(own_tiles):
        part = total[:, t * TILE : (t + 1) * TILE] * scale_ref[pl.ds(row * own_tiles + t, 1), :]
        out_ref[pl.ds(t * TILE, TILE), :] = part.T
    weight_ref[...] = grads[:width, :]
    bias_ref[...] = grads[width : width + 1, :]


def finish(parts, grads, scale):
    width, node_rows = parts[0].shape
    return call(
        functools.partial(finish_kernel, len(parts)),
        "finish",
        (*parts, *grads, scale),
        (hbm(node_rows, width), hbm(width, width), hbm(1, width)),
    )


def swap(value, axis, mask):
    count = lax.axis_size(axis)
    return lax.ppermute(value, axis, [(i, i ^ mask) for i in range(count)])


def local(features, weight, bias_vector, out_grad, adj_tiles, tile_slots, tile_counts):
    row_count = lax.axis_size("row")
    col_count = lax.axis_size("col")
    node_rows, width = features.shape
    tile_rows = node_rows * col_count // TILE
    tile_cols = node_rows * row_count // TILE
    top = row_count // 2
    near, far = list(range(top)), list(range(top, row_count))
    even, odd = list(range(0, col_count, 2)), list(range(1, col_count, 2))

    blocks = [None] * row_count
    blocks[0] = features
    blocks[top] = swap(features, "row", top)
    for m in near[1:]:
        blocks[m] = swap(features, "row", m)
    for m in near[1:]:
        blocks[top | m] = swap(blocks[top], "row", m)

    dense, col_sums, row_sums = densify(
        tile_slots[0, 0], tile_counts[0], adj_tiles[0, 0], tile_rows, tile_cols
    )
    col_sums = sum_all([col_sums] + [swap(col_sums, "row", m) for m in near[1:]], "near_sums")
    wide, scale = source_scales([col_sums, swap(col_sums, "row", top)])

    given, rhs = forward_first(odd, dense, row_sums, wide, blocks)
    got = swap(given, "col", 1)
    kept = forward_second(even, dense, row_sums, rhs, node_rows)
    paired = pair_sums(kept, got)
    others = [swap(part, "col", m) for m, part in zip(even[1:], paired)]
    activated, back, aggregated, pre_grad = node_step(
        kept, got, others, out_grad, weight, bias_vector[None, :]
    )

    backs = [None] * col_count
    backs[0] = back
    for m in even[1:]:
        backs[m] = swap(back, "col", m)
    for m in even:
        backs[m | 1] = swap(backs[m], "col", 1)
    grads = weight_parts(aggregated, pre_grad)
    late = 2
    early = [m for m in range(1, row_count) if not m & late]
    grads = sum_all([grads] + [swap(grads, "row", m) for m in early], "early_grads")

    chunks, lhs = backward_first(far, dense, backs)
    ahead = [chunks[top]] + [swap(chunks[top | m], "row", m) for m in near[1:]]
    chunks = backward_second(near, dense, lhs, node_rows)
    mine = [chunks[0]] + [swap(chunks[m], "row", m) for m in near[1:]]
    grads = sum_all([grads] + [swap(grads, "col", m) for m in range(1, col_count)], "col_grads")
    mine.append(swap(sum_all(ahead, "ahead_sums"), "row", top))
    feature_grad, weight_grad, bias_grad = finish(
        mine, [grads, swap(grads, "row", late)], scale
    )
    return activated, feature_grad, weight_grad, bias_grad[0]


def solution(mesh):
    return jax.shard_map(
        local,
        mesh=mesh,
        in_specs=(
            P(("col", "row"), None),
            P(),
            P(),
            P(("row", "col"), None),
            P("row", "col", None, None, None),
            P("row", "col", None),
            P("row", "col"),
        ),
        out_specs=(P(("row", "col"), None), P(("col", "row"), None), P(), P()),
        check_vma=False,
    )
```

```python
import functools

import jax
import jax.numpy as jnp
from jax import lax
from jax.experimental import pallas as pl
from jax.experimental.pallas import tpu as pltpu
from jax.sharding import PartitionSpec as P

TILE = 128
PAD = 8
F32 = jnp.float32
BF16 = jnp.bfloat16
HIGHEST = lax.Precision.HIGHEST
MIB = 1024 * 1024
HINT = 2 * 10**9


def nt_dot(lhs, rhs, **kw):
    return lax.dot_general(lhs, rhs, (((1,), (1,)), ((), ())), preferred_element_type=F32, **kw)


def tn_dot(lhs, rhs, **kw):
    return lax.dot_general(lhs, rhs, (((0,), (0,)), ((), ())), preferred_element_type=F32, **kw)


def split(value):
    high = value.astype(BF16)
    low = (value - high.astype(F32)).astype(BF16)
    return high, low


def total_of(refs):
    total = refs[0][...]
    for ref in refs[1:]:
        total = total + ref[...]
    return total


def vmem(*shape, dtype=F32):
    return pltpu.VMEM(shape, dtype)


def hbm(*shape, dtype=F32):
    return jax.ShapeDtypeStruct(shape, dtype)


def call(kernel, name, args, outs, flops=0, room=4, scratch=(), before=(), before_specs=()):
    spec = pl.BlockSpec(memory_space=pltpu.VMEM)
    return pl.pallas_call(
        kernel,
        out_shape=tuple(outs),
        in_specs=list(before_specs) + [spec] * len(args),
        out_specs=(spec,) * len(outs),
        scratch_shapes=list(scratch),
        compiler_params=pltpu.CompilerParams(vmem_limit_bytes=room * MIB),
        cost_estimate=pl.CostEstimate(
            flops=int(flops), bytes_accessed=sum(4 * arg.size for arg in args), transcendentals=0
        ),
        name=name,
    )(*before, *[pltpu.with_memory_space_constraint(arg, pltpu.VMEM) for arg in args])


def densify_kernel(
    tile_cols, pieces, slots_hbm, counts_hbm, tiles_hbm, dense_ref, col_ref,
    tiles, col_acc, slots, counts, sems, slot_sem, count_sem,
):
    slot_total = tiles.shape[0]
    piece = slot_total // pieces
    slot_copy = pltpu.make_async_copy(slots_hbm.at[0], slots, slot_sem)
    count_copy = pltpu.make_async_copy(counts_hbm, counts, count_sem)
    slot_copy.start()
    count_copy.start()
    copies = [
        pltpu.make_async_copy(
            tiles_hbm.at[pl.ds(p * piece, piece)], tiles.at[pl.ds(p * piece, piece)], sems.at[p]
        )
        for p in range(pieces)
    ]
    for copy in copies:
        copy.start()
    if slot_total * TILE * TILE < dense_ref.shape[0] * dense_ref.shape[1]:
        dense_ref[...] = jnp.zeros_like(dense_ref)
    col_acc[...] = jnp.zeros_like(col_acc)
    slot_copy.wait()
    count_copy.wait()
    live = counts[0, 0]

    def place(k, carry):
        slot = slots[k]
        r = slot // tile_cols
        c = slot % tile_cols
        keep = jnp.where(k < live, 1.0, 0.0)
        tile = (tiles[k].astype(F32) * keep).astype(BF16)
        dense_ref[
            pl.ds(pl.multiple_of(r * TILE, TILE), TILE), pl.ds(pl.multiple_of(c * TILE, TILE), TILE)
        ] = tile
        col_acc[c] += jnp.sum(tile.reshape(TILE // 16, 16, TILE), axis=0, dtype=BF16).astype(F32)
        return carry

    for p in range(pieces):
        copies[p].wait()
        lax.fori_loop(p * piece, (p + 1) * piece, place, 0, unroll=4)
    col_ref[...] = jnp.sum(col_acc[...], axis=1)


def densify(slots, counts, tiles, tile_rows, tile_cols):
    pieces = 8
    return call(
        functools.partial(densify_kernel, tile_cols, pieces),
        "densify",
        (),
        (vmem(tile_rows * TILE, tile_cols * TILE, dtype=BF16), vmem(tile_cols, TILE)),
        flops=tiles.size * 400,
        room=16,
        scratch=(
            vmem(*tiles.shape, dtype=jnp.int32),
            vmem(tile_cols, 16, TILE),
            pltpu.SMEM(slots.shape[1:], jnp.int32),
            pltpu.SMEM(counts.shape, jnp.int32),
            pltpu.SemaphoreType.DMA((pieces,)),
            pltpu.SemaphoreType.DMA,
            pltpu.SemaphoreType.DMA,
        ),
        before=(slots, counts, pltpu.with_memory_space_constraint(tiles, pltpu.HBM)),
        before_specs=[pl.BlockSpec(memory_space=pl.ANY)] * 3,
    )


def row_kernel(dense_ref, row_ref):
    ones = jnp.ones((8, TILE), BF16)
    tile_rows = row_ref.shape[0]
    for r in range(tile_rows):
        total = dense_ref[pl.ds(r * TILE, TILE), pl.ds(0, TILE)].astype(F32)
        for c in range(1, dense_ref.shape[1] // TILE):
            total += dense_ref[pl.ds(r * TILE, TILE), pl.ds(c * TILE, TILE)].astype(F32)
        row_ref[pl.ds(r, 1), :] = nt_dot(ones, total.astype(BF16))[0:1, :]


def row_totals(dense):
    return call(row_kernel, "row_totals", (dense,), (vmem(dense.shape[0] // TILE, TILE),))[0]


def message_kernel(block_ref, own_ref, got_ref, *refs):
    out_ref = refs[-1]
    node_rows = block_ref.shape[0]
    out_ref[pl.ds(0, node_rows), :] = block_ref[...]
    out_ref[pl.ds(node_rows, own_ref.shape[0]), :] = own_ref[...] + got_ref[...]


def message(block, own, got, after):
    rows = block.shape[0] + own.shape[0]
    return call(
        message_kernel, "message", (block, own, got, *after), (vmem(rows, block.shape[1]),)
    )[0]


def scales_kernel(skip, *refs):
    parts, (wide_ref, scale_ref) = refs[:-2], refs[-2:]
    total = parts[0][skip:, :]
    for ref in parts[1:]:
        total = total + ref[skip:, :]
    scale = lax.rsqrt(1.0 + total)
    for c in range(scale.shape[0]):
        wide_ref[pl.ds(c * TILE, TILE), :] = jnp.broadcast_to(scale[c : c + 1, :], (TILE, TILE)).T
    scale_ref[...] = scale


def source_scales(parts, skip):
    tile_cols = parts[0].shape[0] - skip
    return call(
        functools.partial(scales_kernel, skip),
        "source_scales",
        parts,
        (vmem(tile_cols * TILE, TILE), vmem(tile_cols, TILE)),
    )


def forward_chunks(peers, dense_ref, row_ref, rhs, out_ref):
    col = lax.axis_index("col")
    node_rows, width = out_ref.shape[1] - PAD, out_ref.shape[2]
    own_tiles = node_rows // TILE
    for h, m in enumerate(peers):
        peer = col ^ m
        start = pl.multiple_of(peer * node_rows, node_rows)
        both = jnp.dot(dense_ref[pl.ds(start, node_rows), :], rhs[...], preferred_element_type=F32)
        out_ref[h, pl.ds(0, node_rows), :] = both[:, :width] + both[:, width:]
        out_ref[h, pl.ds(node_rows, PAD), :] = jnp.zeros((PAD, width), F32)
        for t in range(own_tiles):
            out_ref[h, pl.ds(node_rows + t, 1), :] = row_ref[pl.ds(peer * own_tiles + t, 1), :]


def forward_first_kernel(peers, row_count, *refs):
    dense_ref, row_ref, wide_ref = refs[:3]
    blocks = refs[3 : 3 + row_count]
    out_ref, rhs = refs[3 + row_count :]
    row = lax.axis_index("row")
    node_rows, width = blocks[0].shape
    for m in range(row_count):
        start = pl.multiple_of((row ^ m) * node_rows, node_rows)
        block = blocks[m][pl.ds(0, node_rows), :]
        high, low = split(block * wide_ref[pl.ds(start, node_rows), :])
        rhs[pl.ds(start, node_rows), :width] = high
        rhs[pl.ds(start, node_rows), width:] = low
    forward_chunks(peers, dense_ref, row_ref, rhs, out_ref)


def forward_second_kernel(peers, dense_ref, row_ref, rhs, out_ref):
    forward_chunks(peers, dense_ref, row_ref, rhs, out_ref)


def forward_first(peers, dense, row_sums, wide, blocks):
    node_rows, width = blocks[0].shape
    cols = dense.shape[1]
    return call(
        functools.partial(forward_first_kernel, peers, len(blocks)),
        "forward_first",
        (dense, row_sums, wide, *blocks),
        (vmem(len(peers), node_rows + PAD, width), vmem(cols, 2 * width, dtype=BF16)),
        flops=4 * len(peers) * node_rows * cols * width,
    )


def forward_second(peers, dense, row_sums, rhs, node_rows):
    cols = dense.shape[1]
    width = rhs.shape[1] // 2
    return call(
        functools.partial(forward_second_kernel, peers),
        "forward_second",
        (dense, row_sums, rhs),
        (vmem(len(peers), node_rows + PAD, width),),
        flops=4 * len(peers) * node_rows * cols * width,
    )[0]


def pair_kernel(kept_ref, got_ref, *outs):
    for h, out_ref in enumerate(outs):
        out_ref[...] = kept_ref[h + 1] + got_ref[h + 1]


def pair_sums(kept, got):
    return call(
        pair_kernel, "pair_sums", (kept, got), [vmem(*kept.shape[1:])] * (kept.shape[0] - 1)
    )


def node_kernel(*refs):
    kept_ref, got_ref = refs[:2]
    others = refs[2:-7]
    cot_ref, weight_ref, bias_ref, act_ref, back_ref, agg_ref, pre_ref = refs[-7:]
    node_rows, width = cot_ref.shape
    total = kept_ref[0] + got_ref[0]
    for ref in others:
        total = total + ref[...]
    own_tiles = node_rows // TILE
    scale = lax.rsqrt(1.0 + total[node_rows:, :])
    wide = jnp.concatenate(
        [jnp.broadcast_to(scale[t : t + 1, :], (TILE, TILE)).T for t in range(own_tiles)], axis=0
    )
    flat = jnp.concatenate([scale[t : t + 1, :] for t in range(own_tiles)], axis=1)
    weight = weight_ref[...]
    aggregated = total[:node_rows, :] * wide
    preact = (
        jnp.dot(aggregated, weight, precision=HIGHEST, preferred_element_type=F32) + bias_ref[...]
    )
    logistic = jax.nn.sigmoid(preact)
    act_ref[...] = preact * logistic
    pre_grad = cot_ref[...] * logistic * (1.0 + preact * (1.0 - logistic))
    back_ref[...] = nt_dot(weight, pre_grad, precision=HIGHEST) * flat
    agg_ref[...] = aggregated
    pre_ref[...] = pre_grad


def node_step(kept, got, others, cotangent, weight, bias):
    node_rows, width = cotangent.shape
    return call(
        node_kernel,
        "node_step",
        (kept, got, *others, cotangent, weight, bias),
        (
            vmem(node_rows, width),
            vmem(width, node_rows),
            vmem(node_rows, width),
            vmem(node_rows, width),
        ),
        flops=24 * node_rows * width * width,
    )


def grads_kernel(agg_ref, pre_ref, out_ref):
    width = agg_ref.shape[1]
    pre_grad = pre_ref[...]
    out_ref[pl.ds(0, width), :] = tn_dot(agg_ref[...], pre_grad, precision=HIGHEST)
    out_ref[pl.ds(width, PAD), :] = jnp.broadcast_to(
        jnp.sum(pre_grad, axis=0, keepdims=True), (PAD, width)
    )


def weight_parts(aggregated, pre_grad):
    node_rows, width = aggregated.shape
    return call(
        grads_kernel,
        "weight_parts",
        (aggregated, pre_grad),
        (vmem(width + PAD, width),),
        flops=12 * node_rows * width * width,
    )[0]


def backward_chunks(peers, dense_ref, lhs, outs):
    row = lax.axis_index("row")
    width, node_rows = outs[0].shape
    for m, out_ref in zip(peers, outs):
        start = pl.multiple_of((row ^ m) * node_rows, node_rows)
        both = jnp.dot(lhs[...], dense_ref[:, pl.ds(start, node_rows)], preferred_element_type=F32)
        out_ref[...] = both[:width, :] + both[width:, :]


def backward_first_kernel(peers, col_count, *refs):
    dense_ref = refs[0]
    blocks = refs[1 : 1 + col_count]
    outs, lhs = refs[1 + col_count : -1], refs[-1]
    col = lax.axis_index("col")
    width, node_rows = blocks[0].shape
    for m in range(col_count):
        start = pl.multiple_of((col ^ m) * node_rows, node_rows)
        high, low = split(blocks[m][...])
        lhs[:width, pl.ds(start, node_rows)] = high
        lhs[width:, pl.ds(start, node_rows)] = low
    backward_chunks(peers, dense_ref, lhs, outs)


def backward_second_kernel(peers, dense_ref, lhs, *outs):
    backward_chunks(peers, dense_ref, lhs, outs)


def backward_first(peers, dense, blocks):
    width, node_rows = blocks[0].shape
    rows = dense.shape[0]
    out = call(
        functools.partial(backward_first_kernel, peers, len(blocks)),
        "backward_first",
        (dense, *blocks),
        [vmem(width, node_rows)] * len(peers) + [vmem(2 * width, rows, dtype=BF16)],
        flops=4 * len(peers) * node_rows * rows * width,
    )
    return dict(zip(peers, out)), out[-1]


def backward_second(peers, dense, lhs, node_rows):
    rows = dense.shape[0]
    width = lhs.shape[0] // 2
    out = call(
        functools.partial(backward_second_kernel, peers),
        "backward_second",
        (dense, lhs),
        [vmem(width, node_rows)] * len(peers),
        flops=4 * len(peers) * node_rows * rows * width,
    )
    return dict(zip(peers, out))


def sum_kernel(count, *refs):
    refs[-1][...] = total_of(refs[:count])


def sum_all(parts, name, after=(), flops=0):
    kernel = functools.partial(sum_kernel, len(parts))
    return call(kernel, name, (*parts, *after), (vmem(*parts[0].shape),), flops=flops)[0]


def finish_kernel(parts, *refs):
    total = total_of(refs[:parts])
    grads = total_of(refs[parts:-4])
    scale_ref, out_ref, weight_ref, bias_ref = refs[-4:]
    row = lax.axis_index("row")
    width, node_rows = total.shape
    own_tiles = node_rows // TILE
    for t in range(own_tiles):
        part = total[:, t * TILE : (t + 1) * TILE] * scale_ref[pl.ds(row * own_tiles + t, 1), :]
        out_ref[pl.ds(t * TILE, TILE), :] = part.T
    weight_ref[...] = grads[:width, :]
    bias_ref[...] = grads[width : width + 1, :]


def finish(parts, grads, scale):
    width, node_rows = parts[0].shape
    return call(
        functools.partial(finish_kernel, len(parts)),
        "finish",
        (*parts, *grads, scale),
        (hbm(node_rows, width), hbm(width, width), hbm(1, width)),
    )


def swap(value, axis, mask):
    count = lax.axis_size(axis)
    return lax.ppermute(value, axis, [(i, i ^ mask) for i in range(count)])


def local(features, weight, bias_vector, out_grad, adj_tiles, tile_slots, tile_counts):
    row_count = lax.axis_size("row")
    col_count = lax.axis_size("col")
    node_rows, width = features.shape
    tile_rows = node_rows * col_count // TILE
    tile_cols = node_rows * row_count // TILE
    top = row_count // 2
    near, far = list(range(top)), list(range(top, row_count))
    even, odd = list(range(0, col_count, 2)), list(range(1, col_count, 2))

    blocks = [None] * row_count
    blocks[0] = features
    blocks[top] = swap(features, "row", top)
    for m in near[1:]:
        blocks[m] = swap(features, "row", m)
    dense, col_sums = densify(tile_slots[0], tile_counts, adj_tiles[0, 0], tile_rows, tile_cols)
    sent = message(blocks[top], col_sums, swap(col_sums, "row", top), blocks[1:top])
    row_sums = row_totals(dense)
    blocks[top:] = [sent] + [swap(sent, "row", m) for m in near[1:]]
    wide, scale = source_scales(blocks[top:], node_rows)

    given, rhs = forward_first(odd, dense, row_sums, wide, blocks)
    got = swap(given, "col", 1)
    kept = forward_second(even, dense, row_sums, rhs, node_rows)
    paired = pair_sums(kept, got)
    others = [swap(part, "col", m) for m, part in zip(even[1:], paired)]
    activated, back, aggregated, pre_grad = node_step(
        kept, got, others, out_grad, weight, bias_vector[None, :]
    )

    backs = [None] * col_count
    backs[0] = back
    for m in even[1:]:
        backs[m] = swap(back, "col", m)
    for m in even:
        backs[m | 1] = swap(backs[m], "col", 1)
    grads = weight_parts(aggregated, pre_grad)

    chunks, lhs = backward_first(far, dense, backs)
    ahead = [chunks[top]] + [swap(chunks[top | m], "row", m) for m in near[1:]]
    chunks = backward_second(near, dense, lhs, node_rows)
    mine = [chunks[0]] + [swap(chunks[m], "row", m) for m in near[1:]]
    ahead = sum_all(ahead, "ahead_sums")
    passed = swap(ahead, "row", top)

    rounds = [("row", top), ("row", 1)] if top > 1 else [("row", 1)]
    rounds += [("col", 1 << b) for b in range(col_count.bit_length() - 1)]
    rounds += [("row", 1 << b) for b in range(1, top.bit_length() - 1)]
    behind = [(chunks[0],), ()] + [(ahead,)] * (len(rounds) - 2)
    for (axis, mask), after in zip(rounds[:-1], behind):
        grads = sum_all([grads, swap(grads, axis, mask)], f"{axis}{mask}_grads", after)
    mine = sum_all(mine, "mine_sums", (grads,), HINT)
    axis, mask = rounds[-1]
    feature_grad, weight_grad, bias_grad = finish(
        [mine, passed], [grads, swap(grads, axis, mask)], scale
    )
    return activated, feature_grad, weight_grad, bias_grad[0]


def solution(mesh):
    return jax.shard_map(
        local,
        mesh=mesh,
        in_specs=(
            P(("col", "row"), None),
            P(),
            P(),
            P(("row", "col"), None),
            P("row", "col", None, None, None),
            P("row", "col", None),
            P("row", "col"),
        ),
        out_specs=(P(("row", "col"), None), P(("col", "row"), None), P(), P()),
        check_vma=False,
    )
```

```python
import functools

import jax
import jax.numpy as jnp
from jax import lax
from jax.experimental import pallas as pl
from jax.experimental.pallas import tpu as pltpu
from jax.sharding import PartitionSpec as P

TILE = 128
PAD = 8
F32 = jnp.float32
BF16 = jnp.bfloat16
HIGHEST = lax.Precision.HIGHEST
MIB = 1024 * 1024
HINT = 2 * 10**9


def nt_dot(lhs, rhs, **kw):
    return lax.dot_general(lhs, rhs, (((1,), (1,)), ((), ())), preferred_element_type=F32, **kw)


def tn_dot(lhs, rhs, **kw):
    return lax.dot_general(lhs, rhs, (((0,), (0,)), ((), ())), preferred_element_type=F32, **kw)


def split(value):
    high = value.astype(BF16)
    low = (value - high.astype(F32)).astype(BF16)
    return high, low


def total_of(refs):
    total = refs[0][...]
    for ref in refs[1:]:
        total = total + ref[...]
    return total


def vmem(*shape, dtype=F32):
    return pltpu.VMEM(shape, dtype)


def hbm(*shape, dtype=F32):
    return jax.ShapeDtypeStruct(shape, dtype)


def call(kernel, name, args, outs, flops=0, room=4, scratch=(), before=(), before_specs=()):
    spec = pl.BlockSpec(memory_space=pltpu.VMEM)
    return pl.pallas_call(
        kernel,
        out_shape=tuple(outs),
        in_specs=list(before_specs) + [spec] * len(args),
        out_specs=(spec,) * len(outs),
        scratch_shapes=list(scratch),
        compiler_params=pltpu.CompilerParams(vmem_limit_bytes=room * MIB),
        cost_estimate=pl.CostEstimate(
            flops=int(flops), bytes_accessed=sum(4 * arg.size for arg in args), transcendentals=0
        ),
        name=name,
    )(*before, *[pltpu.with_memory_space_constraint(arg, pltpu.VMEM) for arg in args])


def densify_kernel(
    tile_cols, pieces, slots_hbm, counts_hbm, tiles_hbm, dense_ref, col_ref,
    tiles, col_acc, slots, counts, sems, slot_sem, count_sem,
):
    slot_total = tiles.shape[0]
    piece = slot_total // pieces
    slot_copy = pltpu.make_async_copy(slots_hbm.at[0], slots, slot_sem)
    count_copy = pltpu.make_async_copy(counts_hbm, counts, count_sem)
    slot_copy.start()
    count_copy.start()
    copies = [
        pltpu.make_async_copy(
            tiles_hbm.at[pl.ds(p * piece, piece)], tiles.at[pl.ds(p * piece, piece)], sems.at[p]
        )
        for p in range(pieces)
    ]
    for copy in copies:
        copy.start()
    if slot_total * TILE * TILE < dense_ref.shape[0] * dense_ref.shape[1]:
        dense_ref[...] = jnp.zeros_like(dense_ref)
    col_acc[...] = jnp.zeros_like(col_acc)
    slot_copy.wait()
    count_copy.wait()
    live = counts[0, 0]

    def place(k, carry):
        slot = slots[k]
        r = slot // tile_cols
        c = slot % tile_cols
        keep = jnp.where(k < live, 1.0, 0.0)
        tile = (tiles[k].astype(F32) * keep).astype(BF16)
        dense_ref[
            pl.ds(pl.multiple_of(r * TILE, TILE), TILE), pl.ds(pl.multiple_of(c * TILE, TILE), TILE)
        ] = tile
        col_acc[c] += jnp.sum(tile.reshape(TILE // 16, 16, TILE), axis=0, dtype=BF16).astype(F32)
        return carry

    for p in range(pieces):
        copies[p].wait()
        lax.fori_loop(p * piece, (p + 1) * piece, place, 0, unroll=4)
    col_ref[...] = jnp.sum(col_acc[...], axis=1)


def densify(slots, counts, tiles, tile_rows, tile_cols):
    pieces = 8
    return call(
        functools.partial(densify_kernel, tile_cols, pieces),
        "densify",
        (),
        (vmem(tile_rows * TILE, tile_cols * TILE, dtype=BF16), vmem(tile_cols, TILE)),
        flops=tiles.size * 400,
        room=16,
        scratch=(
            vmem(*tiles.shape, dtype=jnp.int32),
            vmem(tile_cols, 16, TILE),
            pltpu.SMEM(slots.shape[1:], jnp.int32),
            pltpu.SMEM(counts.shape, jnp.int32),
            pltpu.SemaphoreType.DMA((pieces,)),
            pltpu.SemaphoreType.DMA,
            pltpu.SemaphoreType.DMA,
        ),
        before=(
            pltpu.with_memory_space_constraint(slots, pltpu.HBM),
            counts,
            pltpu.with_memory_space_constraint(tiles, pltpu.HBM),
        ),
        before_specs=[pl.BlockSpec(memory_space=pl.ANY)] * 3,
    )


def row_kernel(dense_ref, row_ref):
    ones = jnp.ones((8, TILE), BF16)
    tile_rows = row_ref.shape[0]
    for r in range(tile_rows):
        total = dense_ref[pl.ds(r * TILE, TILE), pl.ds(0, TILE)].astype(F32)
        for c in range(1, dense_ref.shape[1] // TILE):
            total += dense_ref[pl.ds(r * TILE, TILE), pl.ds(c * TILE, TILE)].astype(F32)
        row_ref[pl.ds(r, 1), :] = nt_dot(ones, total.astype(BF16))[0:1, :]


def row_totals(dense):
    return call(row_kernel, "row_totals", (dense,), (vmem(dense.shape[0] // TILE, TILE),))[0]


def message_kernel(block_ref, own_ref, got_ref, *refs):
    out_ref = refs[-1]
    node_rows = block_ref.shape[0]
    out_ref[pl.ds(0, node_rows), :] = block_ref[...]
    out_ref[pl.ds(node_rows, own_ref.shape[0]), :] = own_ref[...] + got_ref[...]


def message(block, own, got, after):
    rows = block.shape[0] + own.shape[0]
    return call(
        message_kernel, "message", (block, own, got, *after), (vmem(rows, block.shape[1]),)
    )[0]


def scales_kernel(skip, *refs):
    parts, (wide_ref, scale_ref) = refs[:-2], refs[-2:]
    total = parts[0][skip:, :]
    for ref in parts[1:]:
        total = total + ref[skip:, :]
    scale = lax.rsqrt(1.0 + total)
    for c in range(scale.shape[0]):
        wide_ref[pl.ds(c * TILE, TILE), :] = jnp.broadcast_to(scale[c : c + 1, :], (TILE, TILE)).T
    scale_ref[...] = scale


def source_scales(parts, skip):
    tile_cols = parts[0].shape[0] - skip
    return call(
        functools.partial(scales_kernel, skip),
        "source_scales",
        parts,
        (vmem(tile_cols * TILE, TILE), vmem(tile_cols, TILE)),
    )


def forward_chunks(peers, dense_ref, row_ref, rhs, out_ref):
    col = lax.axis_index("col")
    node_rows, width = out_ref.shape[1] - PAD, out_ref.shape[2]
    own_tiles = node_rows // TILE
    for h, m in enumerate(peers):
        peer = col ^ m
        start = pl.multiple_of(peer * node_rows, node_rows)
        both = jnp.dot(dense_ref[pl.ds(start, node_rows), :], rhs[...], preferred_element_type=F32)
        out_ref[h, pl.ds(0, node_rows), :] = both[:, :width] + both[:, width:]
        out_ref[h, pl.ds(node_rows, PAD), :] = jnp.zeros((PAD, width), F32)
        for t in range(own_tiles):
            out_ref[h, pl.ds(node_rows + t, 1), :] = row_ref[pl.ds(peer * own_tiles + t, 1), :]


def forward_first_kernel(peers, row_count, *refs):
    dense_ref, row_ref, wide_ref = refs[:3]
    blocks = refs[3 : 3 + row_count]
    out_ref, rhs = refs[3 + row_count :]
    row = lax.axis_index("row")
    node_rows, width = blocks[0].shape
    for m in range(row_count):
        start = pl.multiple_of((row ^ m) * node_rows, node_rows)
        block = blocks[m][pl.ds(0, node_rows), :]
        high, low = split(block * wide_ref[pl.ds(start, node_rows), :])
        rhs[pl.ds(start, node_rows), :width] = high
        rhs[pl.ds(start, node_rows), width:] = low
    forward_chunks(peers, dense_ref, row_ref, rhs, out_ref)


def forward_second_kernel(peers, dense_ref, row_ref, rhs, out_ref):
    forward_chunks(peers, dense_ref, row_ref, rhs, out_ref)


def forward_first(peers, dense, row_sums, wide, blocks):
    node_rows, width = blocks[0].shape
    cols = dense.shape[1]
    return call(
        functools.partial(forward_first_kernel, peers, len(blocks)),
        "forward_first",
        (dense, row_sums, wide, *blocks),
        (vmem(len(peers), node_rows + PAD, width), vmem(cols, 2 * width, dtype=BF16)),
        flops=4 * len(peers) * node_rows * cols * width,
    )


def forward_second(peers, dense, row_sums, rhs, node_rows):
    cols = dense.shape[1]
    width = rhs.shape[1] // 2
    return call(
        functools.partial(forward_second_kernel, peers),
        "forward_second",
        (dense, row_sums, rhs),
        (vmem(len(peers), node_rows + PAD, width),),
        flops=4 * len(peers) * node_rows * cols * width,
    )[0]


def pair_kernel(kept_ref, got_ref, *outs):
    for h, out_ref in enumerate(outs):
        out_ref[...] = kept_ref[h + 1] + got_ref[h + 1]


def pair_sums(kept, got):
    return call(
        pair_kernel, "pair_sums", (kept, got), [vmem(*kept.shape[1:])] * (kept.shape[0] - 1)
    )


def node_kernel(*refs):
    kept_ref, got_ref = refs[:2]
    others = refs[2:-7]
    cot_ref, weight_ref, bias_ref, act_ref, back_ref, agg_ref, pre_ref = refs[-7:]
    node_rows, width = cot_ref.shape
    total = kept_ref[0] + got_ref[0]
    for ref in others:
        total = total + ref[...]
    own_tiles = node_rows // TILE
    scale = lax.rsqrt(1.0 + total[node_rows:, :])
    wide = jnp.concatenate(
        [jnp.broadcast_to(scale[t : t + 1, :], (TILE, TILE)).T for t in range(own_tiles)], axis=0
    )
    flat = jnp.concatenate([scale[t : t + 1, :] for t in range(own_tiles)], axis=1)
    weight = weight_ref[...]
    aggregated = total[:node_rows, :] * wide
    preact = (
        jnp.dot(aggregated, weight, precision=HIGHEST, preferred_element_type=F32) + bias_ref[...]
    )
    logistic = jax.nn.sigmoid(preact)
    act_ref[...] = preact * logistic
    pre_grad = cot_ref[...] * logistic * (1.0 + preact * (1.0 - logistic))
    back_ref[...] = nt_dot(weight, pre_grad, precision=HIGHEST) * flat
    agg_ref[...] = aggregated
    pre_ref[...] = pre_grad


def node_step(kept, got, others, cotangent, weight, bias):
    node_rows, width = cotangent.shape
    return call(
        node_kernel,
        "node_step",
        (kept, got, *others, cotangent, weight, bias),
        (
            vmem(node_rows, width),
            vmem(width, node_rows),
            vmem(node_rows, width),
            vmem(node_rows, width),
        ),
        flops=24 * node_rows * width * width,
    )


def grads_kernel(agg_ref, pre_ref, out_ref):
    width = agg_ref.shape[1]
    pre_grad = pre_ref[...]
    out_ref[pl.ds(0, width), :] = tn_dot(agg_ref[...], pre_grad, precision=HIGHEST)
    out_ref[pl.ds(width, PAD), :] = jnp.broadcast_to(
        jnp.sum(pre_grad, axis=0, keepdims=True), (PAD, width)
    )


def weight_parts(aggregated, pre_grad):
    node_rows, width = aggregated.shape
    return call(
        grads_kernel,
        "weight_parts",
        (aggregated, pre_grad),
        (vmem(width + PAD, width),),
        flops=12 * node_rows * width * width,
    )[0]


def folds(rows, width, node_rows):
    step = -(-rows * width // node_rows // 8) * 8
    return [(at, min(step, rows - at)) for at in range(0, rows, step)], step


def carried_kernel(block_ref, own_ref, got_ref, out_ref):
    width, node_rows = block_ref.shape
    parts, step = folds(own_ref.shape[0], width, node_rows)
    out_ref[pl.ds(0, width), :] = block_ref[...]
    for j, (at, size) in enumerate(parts):
        out_ref[pl.ds(width, size), pl.ds(j * width, width)] = (
            own_ref[pl.ds(at, size), :] + got_ref[pl.ds(at, size), :]
        )
        if size < step:
            out_ref[pl.ds(width + size, step - size), pl.ds(j * width, width)] = jnp.zeros(
                (step - size, width), F32
            )


def carried(block, own, got):
    width, node_rows = block.shape
    step = folds(own.shape[0], width, node_rows)[1]
    return call(
        carried_kernel, "carried", (block, own, got), (vmem(width + step, node_rows),)
    )[0]


def backward_chunks(peers, dense_ref, lhs, outs):
    row = lax.axis_index("row")
    width, node_rows = outs[0].shape
    for m, out_ref in zip(peers, outs):
        start = pl.multiple_of((row ^ m) * node_rows, node_rows)
        both = jnp.dot(lhs[...], dense_ref[:, pl.ds(start, node_rows)], preferred_element_type=F32)
        out_ref[...] = both[:width, :] + both[width:, :]


def backward_first_kernel(peers, carrier, *refs):
    outs, lhs, grad_ref = refs[-2 - len(peers) : -2], refs[-2], refs[-1]
    dense_ref, blocks = refs[0], refs[1 : -2 - len(peers)]
    col = lax.axis_index("col")
    width, node_rows = blocks[0].shape
    for m, block in enumerate(blocks):
        start = pl.multiple_of((col ^ m) * node_rows, node_rows)
        high, low = split(block[pl.ds(0, width), :])
        lhs[:width, pl.ds(start, node_rows)] = high
        lhs[width:, pl.ds(start, node_rows)] = low
    backward_chunks(peers, dense_ref, lhs, outs)
    parts, step = folds(grad_ref.shape[0], width, node_rows)
    for j, (at, size) in enumerate(parts):
        rows, cols = pl.ds(width, size), pl.ds(j * width, width)
        grad_ref[pl.ds(at, size), :] = blocks[carrier][rows, cols] + blocks[carrier | 1][rows, cols]


def backward_second_kernel(peers, dense_ref, lhs, *outs):
    backward_chunks(peers, dense_ref, lhs, outs)


def backward_first(peers, dense, blocks):
    width, node_rows = blocks[0].shape
    rows = dense.shape[0]
    out = call(
        functools.partial(backward_first_kernel, peers, len(blocks) - 2),
        "backward_first",
        (dense, *blocks),
        [vmem(width, node_rows)] * len(peers)
        + [vmem(2 * width, rows, dtype=BF16), vmem(width + PAD, width)],
        flops=4 * len(peers) * node_rows * rows * width,
    )
    return dict(zip(peers, out)), out[-2], out[-1]


def backward_second(peers, dense, lhs, node_rows):
    rows = dense.shape[0]
    width = lhs.shape[0] // 2
    out = call(
        functools.partial(backward_second_kernel, peers),
        "backward_second",
        (dense, lhs),
        [vmem(width, node_rows)] * len(peers),
        flops=4 * len(peers) * node_rows * rows * width,
    )
    return dict(zip(peers, out))


def sum_kernel(count, *refs):
    refs[-1][...] = total_of(refs[:count])


def sum_all(parts, name, after=(), flops=0):
    kernel = functools.partial(sum_kernel, len(parts))
    return call(kernel, name, (*parts, *after), (vmem(*parts[0].shape),), flops=flops)[0]


def hand_over_kernel(value_ref, *refs):
    refs[-1][...] = value_ref[...]


def hand_over(value, after):
    return call(hand_over_kernel, "hand_over", (value, *after), (hbm(*value.shape),))[0]


def finish_kernel(parts, *refs):
    total = total_of(refs[:parts])
    grads = total_of(refs[parts:-4])
    scale_ref, out_ref, weight_ref, bias_ref = refs[-4:]
    row = lax.axis_index("row")
    width, node_rows = total.shape
    own_tiles = node_rows // TILE
    for t in range(own_tiles):
        part = total[:, t * TILE : (t + 1) * TILE] * scale_ref[pl.ds(row * own_tiles + t, 1), :]
        out_ref[pl.ds(t * TILE, TILE), :] = part.T
    weight_ref[...] = grads[:width, :]
    bias_ref[...] = grads[width : width + 1, :]


def finish(parts, grads, scale):
    width, node_rows = parts[0].shape
    return call(
        functools.partial(finish_kernel, len(parts)),
        "finish",
        (*parts, *grads, scale),
        (hbm(node_rows, width), hbm(width, width), hbm(1, width)),
    )


def swap(value, axis, mask):
    count = lax.axis_size(axis)
    return lax.ppermute(value, axis, [(i, i ^ mask) for i in range(count)])


def local(features, weight, bias_vector, out_grad, adj_tiles, tile_slots, tile_counts):
    row_count = lax.axis_size("row")
    col_count = lax.axis_size("col")
    node_rows, width = features.shape
    tile_rows = node_rows * col_count // TILE
    tile_cols = node_rows * row_count // TILE
    top = row_count // 2
    near, far = list(range(top)), list(range(top, row_count))
    even, odd = list(range(0, col_count, 2)), list(range(1, col_count, 2))

    blocks = [None] * row_count
    blocks[0] = features
    blocks[top] = swap(features, "row", top)
    for m in near[1:]:
        blocks[m] = swap(features, "row", m)
    dense, col_sums = densify(tile_slots[0], tile_counts, adj_tiles[0, 0], tile_rows, tile_cols)
    sent = message(blocks[top], col_sums, swap(col_sums, "row", top), blocks[1:top])
    row_sums = row_totals(dense)
    blocks[top:] = [sent] + [swap(sent, "row", m) for m in near[1:]]
    wide, scale = source_scales(blocks[top:], node_rows)

    given, rhs = forward_first(odd, dense, row_sums, wide, blocks)
    got = swap(given, "col", 1)
    kept = forward_second(even, dense, row_sums, rhs, node_rows)
    paired = pair_sums(kept, got)
    others = [swap(part, "col", m) for m, part in zip(even[1:], paired)]
    activated, back, aggregated, pre_grad = node_step(
        kept, got, others, out_grad, weight, bias_vector[None, :]
    )

    backs = [None] * col_count
    backs[0] = back
    for m in even[1:]:
        backs[m] = swap(back, "col", m)
    grads = weight_parts(aggregated, pre_grad)
    carrier = even[-1]
    backs[carrier] = carried(backs[carrier], grads, swap(grads, "row", top))
    for m in even:
        backs[m | 1] = swap(backs[m], "col", 1)
    rounds = [("row", 1)] if top > 1 else []
    rounds += [("col", 1 << b) for b in range(1, col_count.bit_length() - 1)]
    rounds += [("row", 1 << b) for b in range(1, top.bit_length() - 1)]

    chunks, lhs, grads = backward_first(far, dense, backs)
    ahead = [chunks[top]] + [swap(chunks[top | m], "row", m) for m in near[1:]]
    chunks = backward_second(near, dense, lhs, node_rows)
    mine = [chunks[0]] + [swap(chunks[m], "row", m) for m in near[1:]]
    ahead = sum_all(ahead, "ahead_sums")
    passed = swap(ahead, "row", top)
    for axis, mask in rounds[:-1]:
        grads = sum_all([grads, swap(grads, axis, mask)], f"{axis}{mask}_grads")
    activated = hand_over(activated, (grads,))
    mine = sum_all(mine, "mine_sums", (grads,), 2 * HINT)
    mine = sum_all([mine, passed], "last_sums", (), HINT // 2)
    axis, mask = rounds[-1]
    feature_grad, weight_grad, bias_grad = finish(
        [mine], [grads, swap(grads, axis, mask)], scale
    )
    return activated, feature_grad, weight_grad, bias_grad[0]


def solution(mesh):
    return jax.shard_map(
        local,
        mesh=mesh,
        in_specs=(
            P(("col", "row"), None),
            P(),
            P(),
            P(("row", "col"), None),
            P("row", "col", None, None, None),
            P("row", "col", None),
            P("row", "col"),
        ),
        out_specs=(P(("row", "col"), None), P(("col", "row"), None), P(), P()),
        check_vma=False,
    )
```

```python
import functools

import jax
import jax.numpy as jnp
from jax import lax
from jax.experimental import pallas as pl
from jax.experimental.pallas import tpu as pltpu
from jax.sharding import PartitionSpec as P

TILE = 128
PAD = 8
F32 = jnp.float32
BF16 = jnp.bfloat16
HIGHEST = lax.Precision.HIGHEST
MIB = 1024 * 1024
HINT = 2 * 10**9


def nt_dot(lhs, rhs, **kw):
    return lax.dot_general(lhs, rhs, (((1,), (1,)), ((), ())), preferred_element_type=F32, **kw)


def tn_dot(lhs, rhs, **kw):
    return lax.dot_general(lhs, rhs, (((0,), (0,)), ((), ())), preferred_element_type=F32, **kw)


def split(value):
    high = value.astype(BF16)
    low = (value - high.astype(F32)).astype(BF16)
    return high, low


def total_of(refs):
    total = refs[0][...]
    for ref in refs[1:]:
        total = total + ref[...]
    return total


def vmem(*shape, dtype=F32):
    return pltpu.VMEM(shape, dtype)


def hbm(*shape, dtype=F32):
    return jax.ShapeDtypeStruct(shape, dtype)


def call(kernel, name, args, outs, flops=0, room=4, scratch=(), before=(), before_specs=()):
    spec = pl.BlockSpec(memory_space=pltpu.VMEM)
    return pl.pallas_call(
        kernel,
        out_shape=tuple(outs),
        in_specs=list(before_specs) + [spec] * len(args),
        out_specs=(spec,) * len(outs),
        scratch_shapes=list(scratch),
        compiler_params=pltpu.CompilerParams(vmem_limit_bytes=room * MIB),
        cost_estimate=pl.CostEstimate(
            flops=int(flops), bytes_accessed=sum(4 * arg.size for arg in args), transcendentals=0
        ),
        name=name,
    )(*before, *[pltpu.with_memory_space_constraint(arg, pltpu.VMEM) for arg in args])


def densify_kernel(
    tile_cols, pieces, slots_hbm, counts_hbm, tiles_hbm, dense_ref, col_ref,
    tiles, col_acc, slots, counts, sems, slot_sem, count_sem,
):
    slot_total = tiles.shape[0]
    piece = slot_total // pieces
    slot_copy = pltpu.make_async_copy(slots_hbm.at[0], slots, slot_sem)
    count_copy = pltpu.make_async_copy(counts_hbm, counts, count_sem)
    slot_copy.start()
    count_copy.start()
    copies = [
        pltpu.make_async_copy(
            tiles_hbm.at[pl.ds(p * piece, piece)], tiles.at[pl.ds(p * piece, piece)], sems.at[p]
        )
        for p in range(pieces)
    ]
    for copy in copies:
        copy.start()
    if slot_total * TILE * TILE < dense_ref.shape[0] * dense_ref.shape[1]:
        dense_ref[...] = jnp.zeros_like(dense_ref)
    col_acc[...] = jnp.zeros_like(col_acc)
    slot_copy.wait()
    count_copy.wait()
    live = counts[0, 0]

    def place(k, carry):
        slot = slots[k]
        r = slot // tile_cols
        c = slot % tile_cols
        keep = jnp.where(k < live, 1.0, 0.0)
        tile = (tiles[k].astype(F32) * keep).astype(BF16)
        dense_ref[
            pl.ds(pl.multiple_of(r * TILE, TILE), TILE), pl.ds(pl.multiple_of(c * TILE, TILE), TILE)
        ] = tile
        col_acc[c] += jnp.sum(tile.reshape(TILE // 16, 16, TILE), axis=0, dtype=BF16).astype(F32)
        return carry

    for p in range(pieces):
        copies[p].wait()
        lax.fori_loop(p * piece, (p + 1) * piece, place, 0, unroll=4)
    col_ref[...] = jnp.sum(col_acc[...], axis=1)


def densify(slots, counts, tiles, tile_rows, tile_cols):
    pieces = 8
    return call(
        functools.partial(densify_kernel, tile_cols, pieces),
        "densify",
        (),
        (vmem(tile_rows * TILE, tile_cols * TILE, dtype=BF16), vmem(tile_cols, TILE)),
        flops=tiles.size * 400,
        room=16,
        scratch=(
            vmem(*tiles.shape, dtype=jnp.int32),
            vmem(tile_cols, 16, TILE),
            pltpu.SMEM(slots.shape[1:], jnp.int32),
            pltpu.SMEM(counts.shape, jnp.int32),
            pltpu.SemaphoreType.DMA((pieces,)),
            pltpu.SemaphoreType.DMA,
            pltpu.SemaphoreType.DMA,
        ),
        before=(
            pltpu.with_memory_space_constraint(slots, pltpu.HBM),
            counts,
            pltpu.with_memory_space_constraint(tiles, pltpu.HBM),
        ),
        before_specs=[pl.BlockSpec(memory_space=pl.ANY)] * 3,
    )


def row_kernel(dense_ref, row_ref):
    ones = jnp.ones((8, TILE), BF16)
    tile_rows = row_ref.shape[0]
    for r in range(tile_rows):
        total = dense_ref[pl.ds(r * TILE, TILE), pl.ds(0, TILE)].astype(F32)
        for c in range(1, dense_ref.shape[1] // TILE):
            total += dense_ref[pl.ds(r * TILE, TILE), pl.ds(c * TILE, TILE)].astype(F32)
        row_ref[pl.ds(r, 1), :] = nt_dot(ones, total.astype(BF16))[0:1, :]


def row_totals(dense):
    return call(row_kernel, "row_totals", (dense,), (vmem(dense.shape[0] // TILE, TILE),))[0]


def message_kernel(block_ref, own_ref, got_ref, *refs):
    out_ref = refs[-1]
    node_rows = block_ref.shape[0]
    out_ref[pl.ds(0, node_rows), :] = block_ref[...]
    out_ref[pl.ds(node_rows, own_ref.shape[0]), :] = own_ref[...] + got_ref[...]


def message(block, own, got, after):
    rows = block.shape[0] + own.shape[0]
    return call(
        message_kernel, "message", (block, own, got, *after), (vmem(rows, block.shape[1]),)
    )[0]


def scales_kernel(skip, *refs):
    parts, (wide_ref, scale_ref) = refs[:-2], refs[-2:]
    total = parts[0][skip:, :]
    for ref in parts[1:]:
        total = total + ref[skip:, :]
    scale = lax.rsqrt(1.0 + total)
    for c in range(scale.shape[0]):
        wide_ref[pl.ds(c * TILE, TILE), :] = jnp.broadcast_to(scale[c : c + 1, :], (TILE, TILE)).T
    scale_ref[...] = scale


def source_scales(parts, skip):
    tile_cols = parts[0].shape[0] - skip
    return call(
        functools.partial(scales_kernel, skip),
        "source_scales",
        parts,
        (vmem(tile_cols * TILE, TILE), vmem(tile_cols, TILE)),
    )


def forward_chunks(peers, dense_ref, row_ref, rhs, out_ref):
    col = lax.axis_index("col")
    node_rows, width = out_ref.shape[1] - PAD, out_ref.shape[2]
    own_tiles = node_rows // TILE
    for h, m in enumerate(peers):
        peer = col ^ m
        start = pl.multiple_of(peer * node_rows, node_rows)
        both = jnp.dot(dense_ref[pl.ds(start, node_rows), :], rhs[...], preferred_element_type=F32)
        out_ref[h, pl.ds(0, node_rows), :] = both[:, :width] + both[:, width:]
        out_ref[h, pl.ds(node_rows, PAD), :] = jnp.zeros((PAD, width), F32)
        for t in range(own_tiles):
            out_ref[h, pl.ds(node_rows + t, 1), :] = row_ref[pl.ds(peer * own_tiles + t, 1), :]


def forward_first_kernel(peers, row_count, *refs):
    dense_ref, row_ref, wide_ref = refs[:3]
    blocks = refs[3 : 3 + row_count]
    out_ref, rhs = refs[3 + row_count :]
    row = lax.axis_index("row")
    node_rows, width = blocks[0].shape
    for m in range(row_count):
        start = pl.multiple_of((row ^ m) * node_rows, node_rows)
        block = blocks[m][pl.ds(0, node_rows), :]
        high, low = split(block * wide_ref[pl.ds(start, node_rows), :])
        rhs[pl.ds(start, node_rows), :width] = high
        rhs[pl.ds(start, node_rows), width:] = low
    forward_chunks(peers, dense_ref, row_ref, rhs, out_ref)


def forward_second_kernel(peers, dense_ref, row_ref, rhs, out_ref):
    forward_chunks(peers, dense_ref, row_ref, rhs, out_ref)


def forward_first(peers, dense, row_sums, wide, blocks):
    node_rows, width = blocks[0].shape
    cols = dense.shape[1]
    return call(
        functools.partial(forward_first_kernel, peers, len(blocks)),
        "forward_first",
        (dense, row_sums, wide, *blocks),
        (vmem(len(peers), node_rows + PAD, width), vmem(cols, 2 * width, dtype=BF16)),
        flops=4 * len(peers) * node_rows * cols * width,
    )


def forward_second(peers, dense, row_sums, rhs, node_rows):
    cols = dense.shape[1]
    width = rhs.shape[1] // 2
    return call(
        functools.partial(forward_second_kernel, peers),
        "forward_second",
        (dense, row_sums, rhs),
        (vmem(len(peers), node_rows + PAD, width),),
        flops=4 * len(peers) * node_rows * cols * width,
    )[0]


def pair_kernel(kept_ref, got_ref, *outs):
    for h, out_ref in enumerate(outs):
        out_ref[...] = kept_ref[h + 1] + got_ref[h + 1]


def pair_sums(kept, got):
    return call(
        pair_kernel, "pair_sums", (kept, got), [vmem(*kept.shape[1:])] * (kept.shape[0] - 1)
    )


def node_kernel(*refs):
    kept_ref, got_ref = refs[:2]
    others = refs[2:-7]
    cot_ref, weight_ref, bias_ref, act_ref, back_ref, agg_ref, pre_ref = refs[-7:]
    node_rows, width = cot_ref.shape
    total = kept_ref[0] + got_ref[0]
    for ref in others:
        total = total + ref[...]
    own_tiles = node_rows // TILE
    scale = lax.rsqrt(1.0 + total[node_rows:, :])
    wide = jnp.concatenate(
        [jnp.broadcast_to(scale[t : t + 1, :], (TILE, TILE)).T for t in range(own_tiles)], axis=0
    )
    flat = jnp.concatenate([scale[t : t + 1, :] for t in range(own_tiles)], axis=1)
    weight = weight_ref[...]
    aggregated = total[:node_rows, :] * wide
    preact = (
        jnp.dot(aggregated, weight, precision=HIGHEST, preferred_element_type=F32) + bias_ref[...]
    )
    logistic = jax.nn.sigmoid(preact)
    act_ref[...] = preact * logistic
    pre_grad = cot_ref[...] * logistic * (1.0 + preact * (1.0 - logistic))
    back_ref[...] = nt_dot(weight, pre_grad, precision=HIGHEST) * flat
    agg_ref[...] = aggregated
    pre_ref[...] = pre_grad


def node_step(kept, got, others, cotangent, weight, bias):
    node_rows, width = cotangent.shape
    return call(
        node_kernel,
        "node_step",
        (kept, got, *others, cotangent, weight, bias),
        (
            vmem(node_rows, width),
            vmem(width, node_rows),
            vmem(node_rows, width),
            vmem(node_rows, width),
        ),
        flops=24 * node_rows * width * width,
    )


def grads_kernel(agg_ref, pre_ref, out_ref):
    width = agg_ref.shape[1]
    pre_grad = pre_ref[...]
    out_ref[pl.ds(0, width), :] = tn_dot(agg_ref[...], pre_grad, precision=HIGHEST)
    out_ref[pl.ds(width, PAD), :] = jnp.broadcast_to(
        jnp.sum(pre_grad, axis=0, keepdims=True), (PAD, width)
    )


def weight_parts(aggregated, pre_grad):
    node_rows, width = aggregated.shape
    return call(
        grads_kernel,
        "weight_parts",
        (aggregated, pre_grad),
        (vmem(width + PAD, width),),
        flops=12 * node_rows * width * width,
    )[0]


def backward_chunks(peers, dense_ref, lhs, outs):
    row = lax.axis_index("row")
    width, node_rows = outs[0].shape
    for m, out_ref in zip(peers, outs):
        start = pl.multiple_of((row ^ m) * node_rows, node_rows)
        both = jnp.dot(lhs[...], dense_ref[:, pl.ds(start, node_rows)], preferred_element_type=F32)
        out_ref[...] = both[:width, :] + both[width:, :]


def backward_first_kernel(peers, col_count, *refs):
    outs, lhs = refs[-1 - len(peers) : -1], refs[-1]
    dense_ref, blocks = refs[0], refs[1 : 1 + col_count]
    col = lax.axis_index("col")
    width, node_rows = blocks[0].shape
    for m, block in enumerate(blocks):
        start = pl.multiple_of((col ^ m) * node_rows, node_rows)
        high, low = split(block[...])
        lhs[:width, pl.ds(start, node_rows)] = high
        lhs[width:, pl.ds(start, node_rows)] = low
    backward_chunks(peers, dense_ref, lhs, outs)


def backward_second_kernel(peers, dense_ref, lhs, *outs):
    backward_chunks(peers, dense_ref, lhs, outs)


def backward_first(peers, dense, blocks, after):
    width, node_rows = blocks[0].shape
    rows = dense.shape[0]
    out = call(
        functools.partial(backward_first_kernel, peers, len(blocks)),
        "backward_first",
        (dense, *blocks, *after),
        [vmem(width, node_rows)] * len(peers) + [vmem(2 * width, rows, dtype=BF16)],
        flops=4 * len(peers) * node_rows * rows * width,
    )
    return dict(zip(peers, out)), out[-1]


def backward_second(peers, dense, lhs, node_rows):
    rows = dense.shape[0]
    width = lhs.shape[0] // 2
    out = call(
        functools.partial(backward_second_kernel, peers),
        "backward_second",
        (dense, lhs),
        [vmem(width, node_rows)] * len(peers),
        flops=4 * len(peers) * node_rows * rows * width,
    )
    return dict(zip(peers, out))


def sum_kernel(count, *refs):
    refs[-1][...] = total_of(refs[:count])


def sum_all(parts, name, after=(), flops=0):
    kernel = functools.partial(sum_kernel, len(parts))
    return call(kernel, name, (*parts, *after), (vmem(*parts[0].shape),), flops=flops)[0]


def hand_over_kernel(value_ref, *refs):
    refs[-1][...] = value_ref[...]


def hand_over(value, after):
    return call(hand_over_kernel, "hand_over", (value, *after), (hbm(*value.shape),))[0]


def finish_kernel(parts, *refs):
    total = total_of(refs[:parts])
    grads = total_of(refs[parts:-4])
    scale_ref, out_ref, weight_ref, bias_ref = refs[-4:]
    row = lax.axis_index("row")
    width, node_rows = total.shape
    own_tiles = node_rows // TILE
    for t in range(own_tiles):
        part = total[:, t * TILE : (t + 1) * TILE] * scale_ref[pl.ds(row * own_tiles + t, 1), :]
        out_ref[pl.ds(t * TILE, TILE), :] = part.T
    weight_ref[...] = grads[:width, :]
    bias_ref[...] = grads[width : width + 1, :]


def finish(parts, grads, scale):
    width, node_rows = parts[0].shape
    return call(
        functools.partial(finish_kernel, len(parts)),
        "finish",
        (*parts, *grads, scale),
        (hbm(node_rows, width), hbm(width, width), hbm(1, width)),
    )


def swap(value, axis, mask):
    count = lax.axis_size(axis)
    return lax.ppermute(value, axis, [(i, i ^ mask) for i in range(count)])


def local(features, weight, bias_vector, out_grad, adj_tiles, tile_slots, tile_counts):
    row_count = lax.axis_size("row")
    col_count = lax.axis_size("col")
    node_rows, width = features.shape
    tile_rows = node_rows * col_count // TILE
    tile_cols = node_rows * row_count // TILE
    top = row_count // 2
    near, far = list(range(top)), list(range(top, row_count))
    even, odd = list(range(0, col_count, 2)), list(range(1, col_count, 2))

    blocks = [None] * row_count
    blocks[0] = features
    blocks[top] = swap(features, "row", top)
    for m in near[1:]:
        blocks[m] = swap(features, "row", m)
    dense, col_sums = densify(tile_slots[0], tile_counts, adj_tiles[0, 0], tile_rows, tile_cols)
    sent = message(blocks[top], col_sums, swap(col_sums, "row", top), blocks[1:top])
    row_sums = row_totals(dense)
    blocks[top:] = [sent] + [swap(sent, "row", m) for m in near[1:]]
    wide, scale = source_scales(blocks[top:], node_rows)

    given, rhs = forward_first(odd, dense, row_sums, wide, blocks)
    got = swap(given, "col", 1)
    kept = forward_second(even, dense, row_sums, rhs, node_rows)
    paired = pair_sums(kept, got)
    others = [swap(part, "col", m) for m, part in zip(even[1:], paired)]
    activated, back, aggregated, pre_grad = node_step(
        kept, got, others, out_grad, weight, bias_vector[None, :]
    )

    backs = [None] * col_count
    backs[0] = back
    for m in even[1:]:
        backs[m] = swap(back, "col", m)
    for m in even:
        backs[m | 1] = swap(backs[m], "col", 1)
    grads = weight_parts(aggregated, pre_grad)
    grads = sum_all([grads, swap(grads, "row", top)], "top_grads", (), HINT)
    chunks, lhs = backward_first(far, dense, backs, (grads,))
    ahead = [chunks[top]] + [swap(chunks[top | m], "row", m) for m in near[1:]]
    chunks = backward_second(near, dense, lhs, node_rows)
    mine = [chunks[0]] + [swap(chunks[m], "row", m) for m in near[1:]]
    ahead = sum_all(ahead, "ahead_sums", (), HINT)
    passed = swap(ahead, "row", top)

    rounds = [("col", 1 << b) for b in range(col_count.bit_length() - 1)]
    rounds += [("row", 1 << b) for b in range(top.bit_length() - 1)]
    grads = sum_all([grads], "held_grads", (chunks[0],))
    for step, (axis, mask) in enumerate(rounds[:-1]):
        after = (ahead,) if axis == "col" and mask * 2 == col_count else ()
        grads = sum_all([grads, swap(grads, axis, mask)], f"{axis}{mask}_grads", after)
    activated = hand_over(activated, (grads,))
    mine = sum_all(mine, "mine_sums", (grads,), 3 * HINT)
    mine = sum_all([mine, passed], "last_sums", (), HINT // 2)
    axis, mask = rounds[-1]
    feature_grad, weight_grad, bias_grad = finish(
        [mine], [grads, swap(grads, axis, mask)], scale
    )
    return activated, feature_grad, weight_grad, bias_grad[0]


def solution(mesh):
    return jax.shard_map(
        local,
        mesh=mesh,
        in_specs=(
            P(("col", "row"), None),
            P(),
            P(),
            P(("row", "col"), None),
            P("row", "col", None, None, None),
            P("row", "col", None),
            P("row", "col"),
        ),
        out_specs=(P(("row", "col"), None), P(("col", "row"), None), P(), P()),
        check_vma=False,
    )
```

```python
import functools

import jax
import jax.numpy as jnp
from jax import lax
from jax.experimental import pallas as pl
from jax.experimental.pallas import tpu as pltpu
from jax.sharding import PartitionSpec as P

TILE = 128
PAD = 8
F32 = jnp.float32
BF16 = jnp.bfloat16
HIGHEST = lax.Precision.HIGHEST
MIB = 1024 * 1024
HINT = 2 * 10**9


def nt_dot(lhs, rhs, **kw):
    return lax.dot_general(lhs, rhs, (((1,), (1,)), ((), ())), preferred_element_type=F32, **kw)


def tn_dot(lhs, rhs, **kw):
    return lax.dot_general(lhs, rhs, (((0,), (0,)), ((), ())), preferred_element_type=F32, **kw)


def split(value):
    high = value.astype(BF16)
    low = (value - high.astype(F32)).astype(BF16)
    return high, low


def total_of(refs):
    total = refs[0][...]
    for ref in refs[1:]:
        total = total + ref[...]
    return total


def vmem(*shape, dtype=F32):
    return pltpu.VMEM(shape, dtype)


def hbm(*shape, dtype=F32):
    return jax.ShapeDtypeStruct(shape, dtype)


def call(kernel, name, args, outs, flops=0, room=4, scratch=(), before=(), before_specs=()):
    spec = pl.BlockSpec(memory_space=pltpu.VMEM)
    return pl.pallas_call(
        kernel,
        out_shape=tuple(outs),
        in_specs=list(before_specs) + [spec] * len(args),
        out_specs=(spec,) * len(outs),
        scratch_shapes=list(scratch),
        compiler_params=pltpu.CompilerParams(vmem_limit_bytes=room * MIB),
        cost_estimate=pl.CostEstimate(
            flops=int(flops), bytes_accessed=sum(4 * arg.size for arg in args), transcendentals=0
        ),
        name=name,
    )(*before, *[pltpu.with_memory_space_constraint(arg, pltpu.VMEM) for arg in args])


def densify_kernel(
    tile_cols, pieces, slots_hbm, counts_hbm, tiles_hbm, dense_ref, col_ref,
    tiles, col_acc, slots, counts, sems, slot_sem, count_sem,
):
    slot_total = tiles.shape[0]
    piece = slot_total // pieces
    slot_copy = pltpu.make_async_copy(slots_hbm.at[0], slots, slot_sem)
    count_copy = pltpu.make_async_copy(counts_hbm, counts, count_sem)
    slot_copy.start()
    count_copy.start()
    copies = [
        pltpu.make_async_copy(
            tiles_hbm.at[pl.ds(p * piece, piece)], tiles.at[pl.ds(p * piece, piece)], sems.at[p]
        )
        for p in range(pieces)
    ]
    for copy in copies:
        copy.start()
    if slot_total * TILE * TILE < dense_ref.shape[0] * dense_ref.shape[1]:
        dense_ref[...] = jnp.zeros_like(dense_ref)
    col_acc[...] = jnp.zeros_like(col_acc)
    slot_copy.wait()
    count_copy.wait()
    live = counts[0, 0]

    def place(k, carry):
        slot = slots[k]
        r = slot // tile_cols
        c = slot % tile_cols
        keep = jnp.where(k < live, 1.0, 0.0)
        tile = (tiles[k].astype(F32) * keep).astype(BF16)
        dense_ref[
            pl.ds(pl.multiple_of(r * TILE, TILE), TILE), pl.ds(pl.multiple_of(c * TILE, TILE), TILE)
        ] = tile
        col_acc[c] += jnp.sum(tile.reshape(TILE // 16, 16, TILE), axis=0, dtype=BF16).astype(F32)
        return carry

    for p in range(pieces):
        copies[p].wait()
        lax.fori_loop(p * piece, (p + 1) * piece, place, 0, unroll=4)
    col_ref[...] = jnp.sum(col_acc[...], axis=1)


def densify(slots, counts, tiles, tile_rows, tile_cols):
    pieces = 8
    return call(
        functools.partial(densify_kernel, tile_cols, pieces),
        "densify",
        (),
        (vmem(tile_rows * TILE, tile_cols * TILE, dtype=BF16), vmem(tile_cols, TILE)),
        flops=tiles.size * 400,
        room=16,
        scratch=(
            vmem(*tiles.shape, dtype=jnp.int32),
            vmem(tile_cols, 16, TILE),
            pltpu.SMEM(slots.shape[1:], jnp.int32),
            pltpu.SMEM(counts.shape, jnp.int32),
            pltpu.SemaphoreType.DMA((pieces,)),
            pltpu.SemaphoreType.DMA,
            pltpu.SemaphoreType.DMA,
        ),
        before=(
            pltpu.with_memory_space_constraint(slots, pltpu.HBM),
            counts,
            pltpu.with_memory_space_constraint(tiles, pltpu.HBM),
        ),
        before_specs=[pl.BlockSpec(memory_space=pl.ANY)] * 3,
    )


def row_kernel(dense_ref, row_ref):
    ones = jnp.ones((8, TILE), BF16)
    tile_rows = row_ref.shape[0]
    for r in range(tile_rows):
        total = dense_ref[pl.ds(r * TILE, TILE), pl.ds(0, TILE)].astype(F32)
        for c in range(1, dense_ref.shape[1] // TILE):
            total += dense_ref[pl.ds(r * TILE, TILE), pl.ds(c * TILE, TILE)].astype(F32)
        row_ref[pl.ds(r, 1), :] = nt_dot(ones, total.astype(BF16))[0:1, :]


def row_totals(dense):
    return call(row_kernel, "row_totals", (dense,), (vmem(dense.shape[0] // TILE, TILE),))[0]


def message_kernel(block_ref, own_ref, got_ref, *refs):
    out_ref = refs[-1]
    node_rows = block_ref.shape[0]
    out_ref[pl.ds(0, node_rows), :] = block_ref[...]
    out_ref[pl.ds(node_rows, own_ref.shape[0]), :] = own_ref[...] + got_ref[...]


def message(block, own, got, after):
    rows = block.shape[0] + own.shape[0]
    return call(
        message_kernel, "message", (block, own, got, *after), (vmem(rows, block.shape[1]),)
    )[0]


def scales_kernel(skip, *refs):
    parts, (wide_ref, scale_ref) = refs[:-2], refs[-2:]
    total = parts[0][skip:, :]
    for ref in parts[1:]:
        total = total + ref[skip:, :]
    scale = lax.rsqrt(1.0 + total)
    for c in range(scale.shape[0]):
        wide_ref[pl.ds(c * TILE, TILE), :] = jnp.broadcast_to(scale[c : c + 1, :], (TILE, TILE)).T
    scale_ref[...] = scale


def source_scales(parts, skip):
    tile_cols = parts[0].shape[0] - skip
    return call(
        functools.partial(scales_kernel, skip),
        "source_scales",
        parts,
        (vmem(tile_cols * TILE, TILE), vmem(tile_cols, TILE)),
    )


def forward_chunks(peers, dense_ref, row_ref, rhs, out_ref):
    col = lax.axis_index("col")
    node_rows, width = out_ref.shape[1] - PAD, out_ref.shape[2]
    own_tiles = node_rows // TILE
    for h, m in enumerate(peers):
        peer = col ^ m
        start = pl.multiple_of(peer * node_rows, node_rows)
        both = jnp.dot(dense_ref[pl.ds(start, node_rows), :], rhs[...], preferred_element_type=F32)
        out_ref[h, pl.ds(0, node_rows), :] = both[:, :width] + both[:, width:]
        out_ref[h, pl.ds(node_rows, PAD), :] = jnp.zeros((PAD, width), F32)
        for t in range(own_tiles):
            out_ref[h, pl.ds(node_rows + t, 1), :] = row_ref[pl.ds(peer * own_tiles + t, 1), :]


def forward_first_kernel(peers, row_count, *refs):
    dense_ref, row_ref, wide_ref = refs[:3]
    blocks = refs[3 : 3 + row_count]
    out_ref, rhs = refs[3 + row_count :]
    row = lax.axis_index("row")
    node_rows, width = blocks[0].shape
    for m in range(row_count):
        start = pl.multiple_of((row ^ m) * node_rows, node_rows)
        block = blocks[m][pl.ds(0, node_rows), :]
        high, low = split(block * wide_ref[pl.ds(start, node_rows), :])
        rhs[pl.ds(start, node_rows), :width] = high
        rhs[pl.ds(start, node_rows), width:] = low
    forward_chunks(peers, dense_ref, row_ref, rhs, out_ref)


def forward_second_kernel(peers, dense_ref, row_ref, rhs, out_ref):
    forward_chunks(peers, dense_ref, row_ref, rhs, out_ref)


def forward_first(peers, dense, row_sums, wide, blocks):
    node_rows, width = blocks[0].shape
    cols = dense.shape[1]
    return call(
        functools.partial(forward_first_kernel, peers, len(blocks)),
        "forward_first",
        (dense, row_sums, wide, *blocks),
        (vmem(len(peers), node_rows + PAD, width), vmem(cols, 2 * width, dtype=BF16)),
        flops=4 * len(peers) * node_rows * cols * width,
    )


def forward_second(peers, dense, row_sums, rhs, node_rows):
    cols = dense.shape[1]
    width = rhs.shape[1] // 2
    return call(
        functools.partial(forward_second_kernel, peers),
        "forward_second",
        (dense, row_sums, rhs),
        (vmem(len(peers), node_rows + PAD, width),),
        flops=4 * len(peers) * node_rows * cols * width,
    )[0]


def pair_kernel(kept_ref, got_ref, *outs):
    for h, out_ref in enumerate(outs):
        out_ref[...] = kept_ref[h + 1] + got_ref[h + 1]


def pair_sums(kept, got):
    return call(
        pair_kernel, "pair_sums", (kept, got), [vmem(*kept.shape[1:])] * (kept.shape[0] - 1)
    )


def node_kernel(*refs):
    kept_ref, got_ref = refs[:2]
    others = refs[2:-7]
    cot_ref, weight_ref, bias_ref, act_ref, back_ref, agg_ref, pre_ref = refs[-7:]
    node_rows, width = cot_ref.shape
    total = kept_ref[0] + got_ref[0]
    for ref in others:
        total = total + ref[...]
    own_tiles = node_rows // TILE
    scale = lax.rsqrt(1.0 + total[node_rows:, :])
    wide = jnp.concatenate(
        [jnp.broadcast_to(scale[t : t + 1, :], (TILE, TILE)).T for t in range(own_tiles)], axis=0
    )
    flat = jnp.concatenate([scale[t : t + 1, :] for t in range(own_tiles)], axis=1)
    weight = weight_ref[...]
    aggregated = total[:node_rows, :] * wide
    preact = (
        jnp.dot(aggregated, weight, precision=HIGHEST, preferred_element_type=F32) + bias_ref[...]
    )
    logistic = jax.nn.sigmoid(preact)
    act_ref[...] = preact * logistic
    pre_grad = cot_ref[...] * logistic * (1.0 + preact * (1.0 - logistic))
    back_ref[...] = nt_dot(weight, pre_grad, precision=HIGHEST) * flat
    agg_ref[...] = aggregated
    pre_ref[...] = pre_grad


def node_step(kept, got, others, cotangent, weight, bias):
    node_rows, width = cotangent.shape
    return call(
        node_kernel,
        "node_step",
        (kept, got, *others, cotangent, weight, bias),
        (
            vmem(node_rows, width),
            vmem(width, node_rows),
            vmem(node_rows, width),
            vmem(node_rows, width),
        ),
        flops=24 * node_rows * width * width,
    )


def grads_kernel(agg_ref, pre_ref, out_ref):
    width = agg_ref.shape[1]
    pre_grad = pre_ref[...]
    out_ref[pl.ds(0, width), :] = tn_dot(agg_ref[...], pre_grad, precision=HIGHEST)
    out_ref[pl.ds(width, PAD), :] = jnp.broadcast_to(
        jnp.sum(pre_grad, axis=0, keepdims=True), (PAD, width)
    )


def weight_parts(aggregated, pre_grad):
    node_rows, width = aggregated.shape
    return call(
        grads_kernel,
        "weight_parts",
        (aggregated, pre_grad),
        (vmem(width + PAD, width),),
        flops=12 * node_rows * width * width,
    )[0]


def backward_chunks(peers, dense_ref, lhs, outs):
    row = lax.axis_index("row")
    width, node_rows = outs[0].shape
    for m, out_ref in zip(peers, outs):
        start = pl.multiple_of((row ^ m) * node_rows, node_rows)
        both = jnp.dot(lhs[...], dense_ref[:, pl.ds(start, node_rows)], preferred_element_type=F32)
        out_ref[...] = both[:width, :] + both[width:, :]


def backward_first_kernel(peers, col_count, *refs):
    outs, lhs = refs[-1 - len(peers) : -1], refs[-1]
    dense_ref, blocks = refs[0], refs[1 : 1 + col_count]
    col = lax.axis_index("col")
    width, node_rows = blocks[0].shape
    for m, block in enumerate(blocks):
        start = pl.multiple_of((col ^ m) * node_rows, node_rows)
        high, low = split(block[...])
        lhs[:width, pl.ds(start, node_rows)] = high
        lhs[width:, pl.ds(start, node_rows)] = low
    backward_chunks(peers, dense_ref, lhs, outs)


def backward_second_kernel(peers, dense_ref, lhs, *outs):
    backward_chunks(peers, dense_ref, lhs, outs)


def backward_first(peers, dense, blocks, after):
    width, node_rows = blocks[0].shape
    rows = dense.shape[0]
    out = call(
        functools.partial(backward_first_kernel, peers, len(blocks)),
        "backward_first",
        (dense, *blocks, *after),
        [vmem(width, node_rows)] * len(peers) + [vmem(2 * width, rows, dtype=BF16)],
        flops=4 * len(peers) * node_rows * rows * width,
    )
    return dict(zip(peers, out)), out[-1]


def backward_second(peers, dense, lhs, node_rows):
    rows = dense.shape[0]
    width = lhs.shape[0] // 2
    out = call(
        functools.partial(backward_second_kernel, peers),
        "backward_second",
        (dense, lhs),
        [vmem(width, node_rows)] * len(peers),
        flops=4 * len(peers) * node_rows * rows * width,
    )
    return dict(zip(peers, out))


def sum_kernel(count, *refs):
    refs[-1][...] = total_of(refs[:count])


def sum_all(parts, name, after=(), flops=0):
    kernel = functools.partial(sum_kernel, len(parts))
    return call(kernel, name, (*parts, *after), (vmem(*parts[0].shape),), flops=flops)[0]


def hand_over_kernel(value_ref, *refs):
    refs[-1][...] = value_ref[...]


def hand_over(value, after):
    return call(hand_over_kernel, "hand_over", (value, *after), (hbm(*value.shape),))[0]


def finish_kernel(parts, *refs):
    total = total_of(refs[:parts])
    grads = total_of(refs[parts:-4])
    scale_ref, out_ref, weight_ref, bias_ref = refs[-4:]
    row = lax.axis_index("row")
    width, node_rows = total.shape
    own_tiles = node_rows // TILE
    for t in range(own_tiles):
        part = total[:, t * TILE : (t + 1) * TILE] * scale_ref[pl.ds(row * own_tiles + t, 1), :]
        out_ref[pl.ds(t * TILE, TILE), :] = part.T
    weight_ref[...] = grads[:width, :]
    bias_ref[...] = grads[width : width + 1, :]


def finish(parts, grads, scale):
    width, node_rows = parts[0].shape
    return call(
        functools.partial(finish_kernel, len(parts)),
        "finish",
        (*parts, *grads, scale),
        (hbm(node_rows, width), hbm(width, width), hbm(1, width)),
    )


def swap(value, axis, mask):
    count = lax.axis_size(axis)
    return lax.ppermute(value, axis, [(i, i ^ mask) for i in range(count)])


def local(features, weight, bias_vector, out_grad, adj_tiles, tile_slots, tile_counts):
    row_count = lax.axis_size("row")
    col_count = lax.axis_size("col")
    node_rows, width = features.shape
    tile_rows = node_rows * col_count // TILE
    tile_cols = node_rows * row_count // TILE
    top = row_count // 2
    near, far = list(range(top)), list(range(top, row_count))
    even, odd = list(range(0, col_count, 2)), list(range(1, col_count, 2))

    blocks = [None] * row_count
    blocks[0] = features
    blocks[top] = swap(features, "row", top)
    for m in near[1:]:
        blocks[m] = swap(features, "row", m)
    dense, col_sums = densify(tile_slots[0], tile_counts, adj_tiles[0, 0], tile_rows, tile_cols)
    sent = message(blocks[top], col_sums, swap(col_sums, "row", top), blocks[1:top])
    row_sums = row_totals(dense)
    blocks[top:] = [sent] + [swap(sent, "row", m) for m in near[1:]]
    wide, scale = source_scales(blocks[top:], node_rows)

    given, rhs = forward_first(odd, dense, row_sums, wide, blocks)
    got = swap(given, "col", 1)
    kept = forward_second(even, dense, row_sums, rhs, node_rows)
    paired = pair_sums(kept, got)
    others = [swap(part, "col", m) for m, part in zip(even[1:], paired)]
    activated, back, aggregated, pre_grad = node_step(
        kept, got, others, out_grad, weight, bias_vector[None, :]
    )

    backs = [None] * col_count
    backs[0] = back
    for m in even[1:]:
        backs[m] = swap(back, "col", m)
    for m in even:
        backs[m | 1] = swap(backs[m], "col", 1)
    grads = weight_parts(aggregated, pre_grad)
    grads = sum_all([grads, swap(grads, "row", top)], "top_grads", (), HINT)
    chunks, lhs = backward_first(far, dense, backs, (grads,))
    ahead = [chunks[top]] + [swap(chunks[top | m], "row", m) for m in near[1:]]
    chunks = backward_second(near, dense, lhs, node_rows)
    mine = [chunks[0]] + [swap(chunks[m], "row", m) for m in near[1:]]
    ahead = sum_all(ahead, "ahead_sums", (), HINT)
    passed = swap(ahead, "row", top)

    rounds = [("col", 1 << b) for b in range(col_count.bit_length() - 1)]
    rounds += [("row", 1 << b) for b in range(top.bit_length() - 1)]
    grads = sum_all([grads], "held_grads", (chunks[0],))
    for step, (axis, mask) in enumerate(rounds[:-1]):
        after = (ahead,) if axis == "col" and mask * 2 == col_count else ()
        grads = sum_all([grads, swap(grads, axis, mask)], f"{axis}{mask}_grads", after)
    activated = hand_over(activated, (grads,))
    mine = sum_all(mine, "mine_sums", (grads,), HINT // 4)
    mine = sum_all([mine, passed], "last_sums", (), HINT)
    axis, mask = rounds[-1]
    feature_grad, weight_grad, bias_grad = finish(
        [mine], [grads, swap(grads, axis, mask)], scale
    )
    return activated, feature_grad, weight_grad, bias_grad[0]


def solution(mesh):
    return jax.shard_map(
        local,
        mesh=mesh,
        in_specs=(
            P(("col", "row"), None),
            P(),
            P(),
            P(("row", "col"), None),
            P("row", "col", None, None, None),
            P("row", "col", None),
            P("row", "col"),
        ),
        out_specs=(P(("row", "col"), None), P(("col", "row"), None), P(), P()),
        check_vma=False,
    )
```

```python
import functools

import jax
import jax.numpy as jnp
from jax import lax
from jax.experimental import pallas as pl
from jax.experimental.pallas import tpu as pltpu
from jax.sharding import PartitionSpec as P

TILE = 128
PAD = 8
F32 = jnp.float32
BF16 = jnp.bfloat16
HIGHEST = lax.Precision.HIGHEST
MIB = 1024 * 1024
HINT = 2 * 10**9


def nt_dot(lhs, rhs, **kw):
    return lax.dot_general(lhs, rhs, (((1,), (1,)), ((), ())), preferred_element_type=F32, **kw)


def tn_dot(lhs, rhs, **kw):
    return lax.dot_general(lhs, rhs, (((0,), (0,)), ((), ())), preferred_element_type=F32, **kw)


def split(value):
    high = value.astype(BF16)
    low = (value - high.astype(F32)).astype(BF16)
    return high, low


def total_of(refs):
    total = refs[0][...]
    for ref in refs[1:]:
        total = total + ref[...]
    return total


def vmem(*shape, dtype=F32):
    return pltpu.VMEM(shape, dtype)


def hbm(*shape, dtype=F32):
    return jax.ShapeDtypeStruct(shape, dtype)


def call(kernel, name, args, outs, flops=0, room=4, scratch=(), before=(), before_specs=()):
    spec = pl.BlockSpec(memory_space=pltpu.VMEM)
    return pl.pallas_call(
        kernel,
        out_shape=tuple(outs),
        in_specs=list(before_specs) + [spec] * len(args),
        out_specs=(spec,) * len(outs),
        scratch_shapes=list(scratch),
        compiler_params=pltpu.CompilerParams(vmem_limit_bytes=room * MIB),
        cost_estimate=pl.CostEstimate(
            flops=int(flops), bytes_accessed=sum(4 * arg.size for arg in args), transcendentals=0
        ),
        name=name,
    )(*before, *[pltpu.with_memory_space_constraint(arg, pltpu.VMEM) for arg in args])


def densify_kernel(
    tile_cols, pieces, slots_hbm, counts_hbm, tiles_hbm, dense_ref, col_ref,
    tiles, col_acc, slots, counts, sems, slot_sem, count_sem,
):
    slot_total = tiles.shape[0]
    piece = slot_total // pieces
    slot_copy = pltpu.make_async_copy(slots_hbm.at[0], slots, slot_sem)
    count_copy = pltpu.make_async_copy(counts_hbm, counts, count_sem)
    slot_copy.start()
    count_copy.start()
    copies = [
        pltpu.make_async_copy(
            tiles_hbm.at[pl.ds(p * piece, piece)], tiles.at[pl.ds(p * piece, piece)], sems.at[p]
        )
        for p in range(pieces)
    ]
    for copy in copies:
        copy.start()
    if slot_total * TILE * TILE < dense_ref.shape[0] * dense_ref.shape[1]:
        dense_ref[...] = jnp.zeros_like(dense_ref)
    col_acc[...] = jnp.zeros_like(col_acc)
    slot_copy.wait()
    count_copy.wait()
    live = counts[0, 0]

    def place(k, carry):
        slot = slots[k]
        r = slot // tile_cols
        c = slot % tile_cols
        keep = jnp.where(k < live, 1.0, 0.0)
        tile = (tiles[k].astype(F32) * keep).astype(BF16)
        dense_ref[
            pl.ds(pl.multiple_of(r * TILE, TILE), TILE), pl.ds(pl.multiple_of(c * TILE, TILE), TILE)
        ] = tile
        col_acc[c] += jnp.sum(tile.reshape(TILE // 16, 16, TILE), axis=0, dtype=BF16).astype(F32)
        return carry

    for p in range(pieces):
        copies[p].wait()
        lax.fori_loop(p * piece, (p + 1) * piece, place, 0, unroll=4)
    col_ref[...] = jnp.sum(col_acc[...], axis=1)


def densify(slots, counts, tiles, tile_rows, tile_cols):
    pieces = 8
    return call(
        functools.partial(densify_kernel, tile_cols, pieces),
        "densify",
        (),
        (vmem(tile_rows * TILE, tile_cols * TILE, dtype=BF16), vmem(tile_cols, TILE)),
        flops=tiles.size * 400,
        room=16,
        scratch=(
            vmem(*tiles.shape, dtype=jnp.int32),
            vmem(tile_cols, 16, TILE),
            pltpu.SMEM(slots.shape[1:], jnp.int32),
            pltpu.SMEM(counts.shape, jnp.int32),
            pltpu.SemaphoreType.DMA((pieces,)),
            pltpu.SemaphoreType.DMA,
            pltpu.SemaphoreType.DMA,
        ),
        before=(
            pltpu.with_memory_space_constraint(slots, pltpu.HBM),
            counts,
            pltpu.with_memory_space_constraint(tiles, pltpu.HBM),
        ),
        before_specs=[pl.BlockSpec(memory_space=pl.ANY)] * 3,
    )


def row_kernel(dense_ref, row_ref):
    ones = jnp.ones((8, TILE), BF16)
    tile_rows = row_ref.shape[0]
    for r in range(tile_rows):
        total = dense_ref[pl.ds(r * TILE, TILE), pl.ds(0, TILE)].astype(F32)
        for c in range(1, dense_ref.shape[1] // TILE):
            total += dense_ref[pl.ds(r * TILE, TILE), pl.ds(c * TILE, TILE)].astype(F32)
        row_ref[pl.ds(r, 1), :] = nt_dot(ones, total.astype(BF16))[0:1, :]


def row_totals(dense):
    return call(row_kernel, "row_totals", (dense,), (vmem(dense.shape[0] // TILE, TILE),))[0]


def message_kernel(block_ref, own_ref, got_ref, *refs):
    out_ref = refs[-1]
    node_rows = block_ref.shape[0]
    out_ref[pl.ds(0, node_rows), :] = block_ref[...]
    out_ref[pl.ds(node_rows, own_ref.shape[0]), :] = own_ref[...] + got_ref[...]


def message(block, own, got, after):
    rows = block.shape[0] + own.shape[0]
    return call(
        message_kernel, "message", (block, own, got, *after), (vmem(rows, block.shape[1]),)
    )[0]


def scales_kernel(skip, *refs):
    parts, (wide_ref, scale_ref) = refs[:-2], refs[-2:]
    total = parts[0][skip:, :]
    for ref in parts[1:]:
        total = total + ref[skip:, :]
    scale = lax.rsqrt(1.0 + total)
    for c in range(scale.shape[0]):
        wide_ref[pl.ds(c * TILE, TILE), :] = jnp.broadcast_to(scale[c : c + 1, :], (TILE, TILE)).T
    scale_ref[...] = scale


def source_scales(parts, skip):
    tile_cols = parts[0].shape[0] - skip
    return call(
        functools.partial(scales_kernel, skip),
        "source_scales",
        parts,
        (vmem(tile_cols * TILE, TILE), vmem(tile_cols, TILE)),
    )


def forward_chunks(peers, dense_ref, row_ref, rhs, out_ref):
    col = lax.axis_index("col")
    node_rows, width = out_ref.shape[1] - PAD, out_ref.shape[2]
    own_tiles = node_rows // TILE
    for h, m in enumerate(peers):
        peer = col ^ m
        start = pl.multiple_of(peer * node_rows, node_rows)
        both = jnp.dot(dense_ref[pl.ds(start, node_rows), :], rhs[...], preferred_element_type=F32)
        out_ref[h, pl.ds(0, node_rows), :] = both[:, :width] + both[:, width:]
        out_ref[h, pl.ds(node_rows, PAD), :] = jnp.zeros((PAD, width), F32)
        for t in range(own_tiles):
            out_ref[h, pl.ds(node_rows + t, 1), :] = row_ref[pl.ds(peer * own_tiles + t, 1), :]


def forward_first_kernel(peers, row_count, *refs):
    dense_ref, row_ref, wide_ref = refs[:3]
    blocks = refs[3 : 3 + row_count]
    out_ref, rhs = refs[3 + row_count :]
    row = lax.axis_index("row")
    node_rows, width = blocks[0].shape
    for m in range(row_count):
        start = pl.multiple_of((row ^ m) * node_rows, node_rows)
        block = blocks[m][pl.ds(0, node_rows), :]
        high, low = split(block * wide_ref[pl.ds(start, node_rows), :])
        rhs[pl.ds(start, node_rows), :width] = high
        rhs[pl.ds(start, node_rows), width:] = low
    forward_chunks(peers, dense_ref, row_ref, rhs, out_ref)


def forward_second_kernel(peers, dense_ref, row_ref, rhs, out_ref):
    forward_chunks(peers, dense_ref, row_ref, rhs, out_ref)


def forward_first(peers, dense, row_sums, wide, blocks):
    node_rows, width = blocks[0].shape
    cols = dense.shape[1]
    return call(
        functools.partial(forward_first_kernel, peers, len(blocks)),
        "forward_first",
        (dense, row_sums, wide, *blocks),
        (vmem(len(peers), node_rows + PAD, width), vmem(cols, 2 * width, dtype=BF16)),
        flops=4 * len(peers) * node_rows * cols * width,
    )


def forward_second(peers, dense, row_sums, rhs, node_rows):
    cols = dense.shape[1]
    width = rhs.shape[1] // 2
    return call(
        functools.partial(forward_second_kernel, peers),
        "forward_second",
        (dense, row_sums, rhs),
        (vmem(len(peers), node_rows + PAD, width),),
        flops=4 * len(peers) * node_rows * cols * width,
    )[0]


def pair_kernel(kept_ref, got_ref, *outs):
    for h, out_ref in enumerate(outs):
        out_ref[...] = kept_ref[h + 1] + got_ref[h + 1]


def pair_sums(kept, got):
    return call(
        pair_kernel, "pair_sums", (kept, got), [vmem(*kept.shape[1:])] * (kept.shape[0] - 1)
    )


def node_kernel(*refs):
    kept_ref, got_ref = refs[:2]
    others = refs[2:-7]
    cot_ref, weight_ref, bias_ref, act_ref, back_ref, agg_ref, pre_ref = refs[-7:]
    node_rows, width = cot_ref.shape
    total = kept_ref[0] + got_ref[0]
    for ref in others:
        total = total + ref[...]
    own_tiles = node_rows // TILE
    scale = lax.rsqrt(1.0 + total[node_rows:, :])
    wide = jnp.concatenate(
        [jnp.broadcast_to(scale[t : t + 1, :], (TILE, TILE)).T for t in range(own_tiles)], axis=0
    )
    flat = jnp.concatenate([scale[t : t + 1, :] for t in range(own_tiles)], axis=1)
    weight = weight_ref[...]
    aggregated = total[:node_rows, :] * wide
    preact = (
        jnp.dot(aggregated, weight, precision=HIGHEST, preferred_element_type=F32) + bias_ref[...]
    )
    logistic = jax.nn.sigmoid(preact)
    act_ref[...] = preact * logistic
    pre_grad = cot_ref[...] * logistic * (1.0 + preact * (1.0 - logistic))
    back_ref[...] = nt_dot(weight, pre_grad, precision=HIGHEST) * flat
    agg_ref[...] = aggregated
    pre_ref[...] = pre_grad


def node_step(kept, got, others, cotangent, weight, bias):
    node_rows, width = cotangent.shape
    return call(
        node_kernel,
        "node_step",
        (kept, got, *others, cotangent, weight, bias),
        (
            vmem(node_rows, width),
            vmem(width, node_rows),
            vmem(node_rows, width),
            vmem(node_rows, width),
        ),
        flops=24 * node_rows * width * width,
    )


def folds(rows, width, node_rows):
    step = -(-rows * width // node_rows // 8) * 8
    return [(at, min(step, rows - at)) for at in range(0, rows, step)], step


def grads_kernel(back_ref, agg_ref, pre_ref, out_ref, sums):
    width, node_rows = back_ref.shape
    pre_grad = pre_ref[...]
    out_ref[pl.ds(0, width), :] = back_ref[...]
    sums[pl.ds(0, width), :] = tn_dot(agg_ref[...], pre_grad, precision=HIGHEST)
    sums[pl.ds(width, PAD), :] = jnp.broadcast_to(
        jnp.sum(pre_grad, axis=0, keepdims=True), (PAD, width)
    )
    parts, step = folds(width + PAD, width, node_rows)
    out_ref[pl.ds(width, step), :] = jnp.zeros((step, node_rows), F32)
    for j, (at, size) in enumerate(parts):
        out_ref[pl.ds(width, size), pl.ds(j * width, width)] = sums[pl.ds(at, size), :]


def weight_parts(back, aggregated, pre_grad):
    node_rows, width = aggregated.shape
    step = folds(width + PAD, width, node_rows)[1]
    return call(
        grads_kernel,
        "weight_parts",
        (back, aggregated, pre_grad),
        (vmem(width + step, node_rows),),
        flops=12 * node_rows * width * width,
        scratch=(vmem(width + PAD, width),),
    )[0]


def backward_chunks(peers, dense_ref, lhs, outs):
    row = lax.axis_index("row")
    width, node_rows = outs[0].shape
    for m, out_ref in zip(peers, outs):
        start = pl.multiple_of((row ^ m) * node_rows, node_rows)
        both = jnp.dot(lhs[...], dense_ref[:, pl.ds(start, node_rows)], preferred_element_type=F32)
        out_ref[...] = both[:width, :] + both[width:, :]


def backward_first_kernel(peers, *refs):
    outs, lhs, grad_ref = refs[-2 - len(peers) : -2], refs[-2], refs[-1]
    dense_ref, blocks = refs[0], refs[1 : -2 - len(peers)]
    col = lax.axis_index("col")
    width, node_rows = outs[0].shape
    for m, block in enumerate(blocks):
        start = pl.multiple_of((col ^ m) * node_rows, node_rows)
        high, low = split(block[pl.ds(0, width), :])
        lhs[:width, pl.ds(start, node_rows)] = high
        lhs[width:, pl.ds(start, node_rows)] = low
    backward_chunks(peers, dense_ref, lhs, outs)
    for j, (at, size) in enumerate(folds(grad_ref.shape[0], width, node_rows)[0]):
        rows, cols = pl.ds(width, size), pl.ds(j * width, width)
        grad_ref[pl.ds(at, size), :] = blocks[0][rows, cols] + blocks[1][rows, cols]


def backward_second_kernel(peers, dense_ref, lhs, *outs):
    backward_chunks(peers, dense_ref, lhs, outs)


def backward_first(peers, dense, blocks, width):
    rows = dense.shape[0]
    node_rows = blocks[0].shape[1]
    out = call(
        functools.partial(backward_first_kernel, peers),
        "backward_first",
        (dense, *blocks),
        [vmem(width, node_rows)] * len(peers)
        + [vmem(2 * width, rows, dtype=BF16), vmem(width + PAD, width)],
        flops=4 * len(peers) * node_rows * rows * width,
    )
    return dict(zip(peers, out)), out[-2], out[-1]


def backward_second(peers, dense, lhs, node_rows):
    rows = dense.shape[0]
    width = lhs.shape[0] // 2
    out = call(
        functools.partial(backward_second_kernel, peers),
        "backward_second",
        (dense, lhs),
        [vmem(width, node_rows)] * len(peers),
        flops=4 * len(peers) * node_rows * rows * width,
    )
    return dict(zip(peers, out))


def sum_kernel(count, *refs):
    refs[-1][...] = total_of(refs[:count])


def sum_all(parts, name, after=(), flops=0):
    kernel = functools.partial(sum_kernel, len(parts))
    return call(kernel, name, (*parts, *after), (vmem(*parts[0].shape),), flops=flops)[0]


def hand_over_kernel(value_ref, *refs):
    refs[-1][...] = value_ref[...]


def hand_over(value, after):
    return call(hand_over_kernel, "hand_over", (value, *after), (hbm(*value.shape),))[0]


def finish_kernel(parts, *refs):
    total = total_of(refs[:parts])
    grads = total_of(refs[parts:-4])
    scale_ref, out_ref, weight_ref, bias_ref = refs[-4:]
    row = lax.axis_index("row")
    width, node_rows = total.shape
    own_tiles = node_rows // TILE
    for t in range(own_tiles):
        part = total[:, t * TILE : (t + 1) * TILE] * scale_ref[pl.ds(row * own_tiles + t, 1), :]
        out_ref[pl.ds(t * TILE, TILE), :] = part.T
    weight_ref[...] = grads[:width, :]
    bias_ref[...] = grads[width : width + 1, :]


def finish(parts, grads, scale):
    width, node_rows = parts[0].shape
    return call(
        functools.partial(finish_kernel, len(parts)),
        "finish",
        (*parts, *grads, scale),
        (hbm(node_rows, width), hbm(width, width), hbm(1, width)),
    )


def swap(value, axis, mask):
    count = lax.axis_size(axis)
    return lax.ppermute(value, axis, [(i, i ^ mask) for i in range(count)])


def local(features, weight, bias_vector, out_grad, adj_tiles, tile_slots, tile_counts):
    row_count = lax.axis_size("row")
    col_count = lax.axis_size("col")
    node_rows, width = features.shape
    tile_rows = node_rows * col_count // TILE
    tile_cols = node_rows * row_count // TILE
    top = row_count // 2
    near, far = list(range(top)), list(range(top, row_count))
    even, odd = list(range(0, col_count, 2)), list(range(1, col_count, 2))

    blocks = [None] * row_count
    blocks[0] = features
    blocks[top] = swap(features, "row", top)
    for m in near[1:]:
        blocks[m] = swap(features, "row", m)
    dense, col_sums = densify(tile_slots[0], tile_counts, adj_tiles[0, 0], tile_rows, tile_cols)
    sent = message(blocks[top], col_sums, swap(col_sums, "row", top), blocks[1:top])
    row_sums = row_totals(dense)
    blocks[top:] = [sent] + [swap(sent, "row", m) for m in near[1:]]
    wide, scale = source_scales(blocks[top:], node_rows)

    given, rhs = forward_first(odd, dense, row_sums, wide, blocks)
    got = swap(given, "col", 1)
    kept = forward_second(even, dense, row_sums, rhs, node_rows)
    paired = pair_sums(kept, got)
    others = [swap(part, "col", m) for m, part in zip(even[1:], paired)]
    activated, back, aggregated, pre_grad = node_step(
        kept, got, others, out_grad, weight, bias_vector[None, :]
    )

    backs = [None] * col_count
    for m in even[1:]:
        backs[m] = swap(back, "col", m)
    backs[0] = weight_parts(back, aggregated, pre_grad)
    for m in even:
        backs[m | 1] = swap(backs[m], "col", 1)
    chunks, lhs, grads = backward_first(far, dense, backs, width)
    ahead = [chunks[top]] + [swap(chunks[top | m], "row", m) for m in near[1:]]
    chunks = backward_second(near, dense, lhs, node_rows)
    mine = [chunks[0]] + [swap(chunks[m], "row", m) for m in near[1:]]
    ahead = sum_all(ahead, "ahead_sums", (), HINT)
    passed = swap(ahead, "row", top)

    rounds = [("col", 1 << b) for b in range(1, col_count.bit_length() - 1)]
    rounds += [("row", top)] + [("row", 1 << b) for b in range(top.bit_length() - 1)]
    grads = sum_all([grads], "held_grads", (lhs,))
    for step, (axis, mask) in enumerate(rounds[:-1]):
        after = (ahead,) if (axis, mask) == ("row", top) else ()
        grads = sum_all([grads, swap(grads, axis, mask)], f"{axis}{mask}_grads", after)
        if step == len(rounds) - 3:
            activated = hand_over(activated, (grads,))
    mine = sum_all(mine, "mine_sums", (grads,), HINT // 4)
    mine = sum_all([mine, passed], "last_sums", (), HINT)
    axis, mask = rounds[-1]
    feature_grad, weight_grad, bias_grad = finish(
        [mine], [grads, swap(grads, axis, mask)], scale
    )
    return activated, feature_grad, weight_grad, bias_grad[0]


def solution(mesh):
    return jax.shard_map(
        local,
        mesh=mesh,
        in_specs=(
            P(("col", "row"), None),
            P(),
            P(),
            P(("row", "col"), None),
            P("row", "col", None, None, None),
            P("row", "col", None),
            P("row", "col"),
        ),
        out_specs=(P(("row", "col"), None), P(("col", "row"), None), P(), P()),
        check_vma=False,
    )
```

```python
import functools

import jax
import jax.numpy as jnp
from jax import lax
from jax.experimental import pallas as pl
from jax.experimental.pallas import tpu as pltpu
from jax.sharding import PartitionSpec as P

TILE = 128
PAD = 8
F32 = jnp.float32
BF16 = jnp.bfloat16
HIGHEST = lax.Precision.HIGHEST
MIB = 1024 * 1024
HINT = 2 * 10**9


def nt_dot(lhs, rhs, **kw):
    return lax.dot_general(lhs, rhs, (((1,), (1,)), ((), ())), preferred_element_type=F32, **kw)


def tn_dot(lhs, rhs, **kw):
    return lax.dot_general(lhs, rhs, (((0,), (0,)), ((), ())), preferred_element_type=F32, **kw)


def split(value):
    high = value.astype(BF16)
    low = (value - high.astype(F32)).astype(BF16)
    return high, low


def total_of(refs):
    total = refs[0][...]
    for ref in refs[1:]:
        total = total + ref[...]
    return total


def vmem(*shape, dtype=F32):
    return pltpu.VMEM(shape, dtype)


def hbm(*shape, dtype=F32):
    return jax.ShapeDtypeStruct(shape, dtype)


def call(kernel, name, args, outs, flops=0, room=4, scratch=(), before=(), before_specs=()):
    spec = pl.BlockSpec(memory_space=pltpu.VMEM)
    return pl.pallas_call(
        kernel,
        out_shape=tuple(outs),
        in_specs=list(before_specs) + [spec] * len(args),
        out_specs=(spec,) * len(outs),
        scratch_shapes=list(scratch),
        compiler_params=pltpu.CompilerParams(vmem_limit_bytes=room * MIB),
        cost_estimate=pl.CostEstimate(
            flops=int(flops), bytes_accessed=sum(4 * arg.size for arg in args), transcendentals=0
        ),
        name=name,
    )(*before, *[pltpu.with_memory_space_constraint(arg, pltpu.VMEM) for arg in args])


def densify_kernel(
    tile_cols, pieces, slots_hbm, counts_hbm, tiles_hbm, dense_ref, col_ref,
    tiles, col_acc, slots, counts, sems, slot_sem, count_sem,
):
    slot_total = tiles.shape[0]
    piece = slot_total // pieces
    slot_copy = pltpu.make_async_copy(slots_hbm.at[0], slots, slot_sem)
    count_copy = pltpu.make_async_copy(counts_hbm, counts, count_sem)
    slot_copy.start()
    count_copy.start()
    copies = [
        pltpu.make_async_copy(
            tiles_hbm.at[pl.ds(p * piece, piece)], tiles.at[pl.ds(p * piece, piece)], sems.at[p]
        )
        for p in range(pieces)
    ]
    for copy in copies:
        copy.start()
    if slot_total * TILE * TILE < dense_ref.shape[0] * dense_ref.shape[1]:
        dense_ref[...] = jnp.zeros_like(dense_ref)
    col_acc[...] = jnp.zeros_like(col_acc)
    slot_copy.wait()
    count_copy.wait()
    live = counts[0, 0]

    def place(k, carry):
        slot = slots[k]
        r = slot // tile_cols
        c = slot % tile_cols
        keep = jnp.where(k < live, 1.0, 0.0)
        tile = (tiles[k].astype(F32) * keep).astype(BF16)
        dense_ref[
            pl.ds(pl.multiple_of(r * TILE, TILE), TILE), pl.ds(pl.multiple_of(c * TILE, TILE), TILE)
        ] = tile
        col_acc[c] += jnp.sum(tile.reshape(TILE // 16, 16, TILE), axis=0, dtype=BF16).astype(F32)
        return carry

    for p in range(pieces):
        copies[p].wait()
        lax.fori_loop(p * piece, (p + 1) * piece, place, 0, unroll=4)
    col_ref[...] = jnp.sum(col_acc[...], axis=1)


def densify(slots, counts, tiles, tile_rows, tile_cols):
    pieces = 8
    return call(
        functools.partial(densify_kernel, tile_cols, pieces),
        "densify",
        (),
        (vmem(tile_rows * TILE, tile_cols * TILE, dtype=BF16), vmem(tile_cols, TILE)),
        flops=tiles.size * 400,
        room=16,
        scratch=(
            vmem(*tiles.shape, dtype=jnp.int32),
            vmem(tile_cols, 16, TILE),
            pltpu.SMEM(slots.shape[1:], jnp.int32),
            pltpu.SMEM(counts.shape, jnp.int32),
            pltpu.SemaphoreType.DMA((pieces,)),
            pltpu.SemaphoreType.DMA,
            pltpu.SemaphoreType.DMA,
        ),
        before=(
            pltpu.with_memory_space_constraint(slots, pltpu.HBM),
            counts,
            pltpu.with_memory_space_constraint(tiles, pltpu.HBM),
        ),
        before_specs=[pl.BlockSpec(memory_space=pl.ANY)] * 3,
    )


def row_kernel(dense_ref, row_ref):
    ones = jnp.ones((8, TILE), BF16)
    tile_rows = row_ref.shape[0]
    for r in range(tile_rows):
        total = dense_ref[pl.ds(r * TILE, TILE), pl.ds(0, TILE)].astype(F32)
        for c in range(1, dense_ref.shape[1] // TILE):
            total += dense_ref[pl.ds(r * TILE, TILE), pl.ds(c * TILE, TILE)].astype(F32)
        row_ref[pl.ds(r, 1), :] = nt_dot(ones, total.astype(BF16))[0:1, :]


def row_totals(dense):
    return call(row_kernel, "row_totals", (dense,), (vmem(dense.shape[0] // TILE, TILE),))[0]


def message_kernel(block_ref, own_ref, got_ref, *refs):
    out_ref = refs[-1]
    node_rows = block_ref.shape[0]
    out_ref[pl.ds(0, node_rows), :] = block_ref[...]
    out_ref[pl.ds(node_rows, own_ref.shape[0]), :] = own_ref[...] + got_ref[...]


def message(block, own, got, after):
    rows = block.shape[0] + own.shape[0]
    return call(
        message_kernel, "message", (block, own, got, *after), (vmem(rows, block.shape[1]),)
    )[0]


def scales_kernel(skip, *refs):
    parts, (wide_ref, scale_ref) = refs[:-2], refs[-2:]
    total = parts[0][skip:, :]
    for ref in parts[1:]:
        total = total + ref[skip:, :]
    scale = lax.rsqrt(1.0 + total)
    for c in range(scale.shape[0]):
        wide_ref[pl.ds(c * TILE, TILE), :] = jnp.broadcast_to(scale[c : c + 1, :], (TILE, TILE)).T
    scale_ref[...] = scale


def source_scales(parts, skip):
    tile_cols = parts[0].shape[0] - skip
    return call(
        functools.partial(scales_kernel, skip),
        "source_scales",
        parts,
        (vmem(tile_cols * TILE, TILE), vmem(tile_cols, TILE)),
    )


def forward_chunks(peers, dense_ref, row_ref, rhs, out_ref):
    col = lax.axis_index("col")
    node_rows, width = out_ref.shape[1] - PAD, out_ref.shape[2]
    own_tiles = node_rows // TILE
    for h, m in enumerate(peers):
        peer = col ^ m
        start = pl.multiple_of(peer * node_rows, node_rows)
        both = jnp.dot(dense_ref[pl.ds(start, node_rows), :], rhs[...], preferred_element_type=F32)
        out_ref[h, pl.ds(0, node_rows), :] = both[:, :width] + both[:, width:]
        out_ref[h, pl.ds(node_rows, PAD), :] = jnp.zeros((PAD, width), F32)
        for t in range(own_tiles):
            out_ref[h, pl.ds(node_rows + t, 1), :] = row_ref[pl.ds(peer * own_tiles + t, 1), :]


def forward_first_kernel(peers, row_count, *refs):
    dense_ref, row_ref, wide_ref = refs[:3]
    blocks = refs[3 : 3 + row_count]
    out_ref, rhs = refs[3 + row_count :]
    row = lax.axis_index("row")
    node_rows, width = blocks[0].shape
    for m in range(row_count):
        start = pl.multiple_of((row ^ m) * node_rows, node_rows)
        block = blocks[m][pl.ds(0, node_rows), :]
        high, low = split(block * wide_ref[pl.ds(start, node_rows), :])
        rhs[pl.ds(start, node_rows), :width] = high
        rhs[pl.ds(start, node_rows), width:] = low
    forward_chunks(peers, dense_ref, row_ref, rhs, out_ref)


def forward_second_kernel(peers, dense_ref, row_ref, rhs, out_ref):
    forward_chunks(peers, dense_ref, row_ref, rhs, out_ref)


def forward_first(peers, dense, row_sums, wide, blocks):
    node_rows, width = blocks[0].shape
    cols = dense.shape[1]
    return call(
        functools.partial(forward_first_kernel, peers, len(blocks)),
        "forward_first",
        (dense, row_sums, wide, *blocks),
        (vmem(len(peers), node_rows + PAD, width), vmem(cols, 2 * width, dtype=BF16)),
        flops=4 * len(peers) * node_rows * cols * width,
    )


def forward_second(peers, dense, row_sums, rhs, node_rows):
    cols = dense.shape[1]
    width = rhs.shape[1] // 2
    return call(
        functools.partial(forward_second_kernel, peers),
        "forward_second",
        (dense, row_sums, rhs),
        (vmem(len(peers), node_rows + PAD, width),),
        flops=4 * len(peers) * node_rows * cols * width,
    )[0]


def pair_kernel(kept_ref, got_ref, *outs):
    for h, out_ref in enumerate(outs):
        out_ref[...] = kept_ref[h + 1] + got_ref[h + 1]


def pair_sums(kept, got):
    return call(
        pair_kernel, "pair_sums", (kept, got), [vmem(*kept.shape[1:])] * (kept.shape[0] - 1)
    )


def node_kernel(*refs):
    kept_ref, got_ref = refs[:2]
    others = refs[2:-7]
    cot_ref, weight_ref, bias_ref, act_ref, back_ref, agg_ref, pre_ref = refs[-7:]
    node_rows, width = cot_ref.shape
    total = kept_ref[0] + got_ref[0]
    for ref in others:
        total = total + ref[...]
    own_tiles = node_rows // TILE
    scale = lax.rsqrt(1.0 + total[node_rows:, :])
    wide = jnp.concatenate(
        [jnp.broadcast_to(scale[t : t + 1, :], (TILE, TILE)).T for t in range(own_tiles)], axis=0
    )
    flat = jnp.concatenate([scale[t : t + 1, :] for t in range(own_tiles)], axis=1)
    weight = weight_ref[...]
    aggregated = total[:node_rows, :] * wide
    preact = (
        jnp.dot(aggregated, weight, precision=HIGHEST, preferred_element_type=F32) + bias_ref[...]
    )
    logistic = jax.nn.sigmoid(preact)
    act_ref[...] = preact * logistic
    pre_grad = cot_ref[...] * logistic * (1.0 + preact * (1.0 - logistic))
    back_ref[...] = nt_dot(weight, pre_grad, precision=HIGHEST) * flat
    agg_ref[...] = aggregated
    pre_ref[...] = pre_grad


def node_step(kept, got, others, cotangent, weight, bias):
    node_rows, width = cotangent.shape
    return call(
        node_kernel,
        "node_step",
        (kept, got, *others, cotangent, weight, bias),
        (
            vmem(node_rows, width),
            vmem(width, node_rows),
            vmem(node_rows, width),
            vmem(node_rows, width),
        ),
        flops=24 * node_rows * width * width,
    )


def folds(rows, width, node_rows):
    step = -(-rows * width // node_rows // 8) * 8
    return [(at, min(step, rows - at)) for at in range(0, rows, step)], step


def grads_kernel(back_ref, agg_ref, pre_ref, out_ref, sums):
    width, node_rows = back_ref.shape
    pre_grad = pre_ref[...]
    out_ref[pl.ds(0, width), :] = back_ref[...]
    sums[pl.ds(0, width), :] = tn_dot(agg_ref[...], pre_grad, precision=HIGHEST)
    sums[pl.ds(width, PAD), :] = jnp.broadcast_to(
        jnp.sum(pre_grad, axis=0, keepdims=True), (PAD, width)
    )
    parts, step = folds(width + PAD, width, node_rows)
    out_ref[pl.ds(width, step), :] = jnp.zeros((step, node_rows), F32)
    for j, (at, size) in enumerate(parts):
        out_ref[pl.ds(width, size), pl.ds(j * width, width)] = sums[pl.ds(at, size), :]


def weight_parts(back, aggregated, pre_grad):
    node_rows, width = aggregated.shape
    step = folds(width + PAD, width, node_rows)[1]
    return call(
        grads_kernel,
        "weight_parts",
        (back, aggregated, pre_grad),
        (vmem(width + step, node_rows),),
        flops=12 * node_rows * width * width,
        scratch=(vmem(width + PAD, width),),
    )[0]


def backward_chunks(peers, dense_ref, lhs, outs):
    row = lax.axis_index("row")
    width, node_rows = outs[0].shape
    for m, out_ref in zip(peers, outs):
        start = pl.multiple_of((row ^ m) * node_rows, node_rows)
        both = jnp.dot(lhs[...], dense_ref[:, pl.ds(start, node_rows)], preferred_element_type=F32)
        out_ref[...] = both[:width, :] + both[width:, :]


def backward_first_kernel(peers, col_count, *refs):
    outs, lhs = refs[-1 - len(peers) : -1], refs[-1]
    dense_ref, blocks = refs[0], refs[1 : 1 + col_count]
    col = lax.axis_index("col")
    width, node_rows = outs[0].shape
    for m, block in enumerate(blocks):
        start = pl.multiple_of((col ^ m) * node_rows, node_rows)
        high, low = split(block[pl.ds(0, width), :])
        lhs[:width, pl.ds(start, node_rows)] = high
        lhs[width:, pl.ds(start, node_rows)] = low
    backward_chunks(peers, dense_ref, lhs, outs)


def unfold_kernel(own_ref, got_ref, out_ref):
    rows, width = out_ref.shape
    for j, (at, size) in enumerate(folds(rows, width, own_ref.shape[1])[0]):
        part = pl.ds(width, size), pl.ds(j * width, width)
        out_ref[pl.ds(at, size), :] = own_ref[part] + got_ref[part]


def unfold_sums(own, got, width):
    return call(unfold_kernel, "core_grads", (own, got), (vmem(width + PAD, width),))[0]


def backward_second_kernel(peers, dense_ref, lhs, *outs):
    backward_chunks(peers, dense_ref, lhs, outs)


def backward_first(peers, dense, blocks, width, after):
    rows = dense.shape[0]
    node_rows = blocks[0].shape[1]
    out = call(
        functools.partial(backward_first_kernel, peers, len(blocks)),
        "backward_first",
        (dense, *blocks, *after),
        [vmem(width, node_rows)] * len(peers) + [vmem(2 * width, rows, dtype=BF16)],
        flops=4 * len(peers) * node_rows * rows * width,
    )
    return dict(zip(peers, out)), out[-1]


def backward_second(peers, dense, lhs, node_rows):
    rows = dense.shape[0]
    width = lhs.shape[0] // 2
    out = call(
        functools.partial(backward_second_kernel, peers),
        "backward_second",
        (dense, lhs),
        [vmem(width, node_rows)] * len(peers),
        flops=4 * len(peers) * node_rows * rows * width,
    )
    return dict(zip(peers, out))


def sum_kernel(count, *refs):
    refs[-1][...] = total_of(refs[:count])


def sum_all(parts, name, after=(), flops=0):
    kernel = functools.partial(sum_kernel, len(parts))
    return call(kernel, name, (*parts, *after), (vmem(*parts[0].shape),), flops=flops)[0]


def hand_over_kernel(value_ref, *refs):
    refs[-1][...] = value_ref[...]


def hand_over(value, after):
    return call(hand_over_kernel, "hand_over", (value, *after), (hbm(*value.shape),))[0]


def finish_kernel(parts, *refs):
    total = total_of(refs[:parts])
    grads = total_of(refs[parts:-4])
    scale_ref, out_ref, weight_ref, bias_ref = refs[-4:]
    row = lax.axis_index("row")
    width, node_rows = total.shape
    own_tiles = node_rows // TILE
    for t in range(own_tiles):
        part = total[:, t * TILE : (t + 1) * TILE] * scale_ref[pl.ds(row * own_tiles + t, 1), :]
        out_ref[pl.ds(t * TILE, TILE), :] = part.T
    weight_ref[...] = grads[:width, :]
    bias_ref[...] = grads[width : width + 1, :]


def finish(parts, grads, scale):
    width, node_rows = parts[0].shape
    return call(
        functools.partial(finish_kernel, len(parts)),
        "finish",
        (*parts, *grads, scale),
        (hbm(node_rows, width), hbm(width, width), hbm(1, width)),
    )


def swap(value, axis, mask):
    count = lax.axis_size(axis)
    return lax.ppermute(value, axis, [(i, i ^ mask) for i in range(count)])


def local(features, weight, bias_vector, out_grad, adj_tiles, tile_slots, tile_counts):
    row_count = lax.axis_size("row")
    col_count = lax.axis_size("col")
    node_rows, width = features.shape
    tile_rows = node_rows * col_count // TILE
    tile_cols = node_rows * row_count // TILE
    top = row_count // 2
    near, far = list(range(top)), list(range(top, row_count))
    even, odd = list(range(0, col_count, 2)), list(range(1, col_count, 2))

    blocks = [None] * row_count
    blocks[0] = features
    blocks[top] = swap(features, "row", top)
    for m in near[1:]:
        blocks[m] = swap(features, "row", m)
    dense, col_sums = densify(tile_slots[0], tile_counts, adj_tiles[0, 0], tile_rows, tile_cols)
    sent = message(blocks[top], col_sums, swap(col_sums, "row", top), blocks[1:top])
    row_sums = row_totals(dense)
    blocks[top:] = [sent] + [swap(sent, "row", m) for m in near[1:]]
    wide, scale = source_scales(blocks[top:], node_rows)

    given, rhs = forward_first(odd, dense, row_sums, wide, blocks)
    got = swap(given, "col", 1)
    kept = forward_second(even, dense, row_sums, rhs, node_rows)
    paired = pair_sums(kept, got)
    others = [swap(part, "col", m) for m, part in zip(even[1:], paired)]
    activated, back, aggregated, pre_grad = node_step(
        kept, got, others, out_grad, weight, bias_vector[None, :]
    )

    backs = [None] * col_count
    for m in even[1:]:
        backs[m] = swap(back, "col", m)
    backs[0] = weight_parts(back, aggregated, pre_grad)
    for m in even:
        backs[m | 1] = swap(backs[m], "col", 1)
    grads = unfold_sums(backs[0], backs[1], width)
    grads = sum_all([grads, swap(grads, "row", top)], "top_grads", (), HINT)
    chunks, lhs = backward_first(far, dense, backs, width, (grads,))
    ahead = [chunks[top]] + [swap(chunks[top | m], "row", m) for m in near[1:]]
    chunks = backward_second(near, dense, lhs, node_rows)
    mine = [chunks[0]] + [swap(chunks[m], "row", m) for m in near[1:]]
    ahead = sum_all(ahead, "ahead_sums", (), HINT)
    passed = swap(ahead, "row", top)

    rounds = [("col", 1 << b) for b in range(1, col_count.bit_length() - 1)]
    rounds = [("row", 1)] * (top > 1) + rounds
    rounds += [("row", 1 << b) for b in range(1, top.bit_length() - 1)]
    grads = sum_all([grads], "held_grads", (lhs,))
    for step, (axis, mask) in enumerate(rounds[:-1]):
        after = (ahead,) if False else ()
        grads = sum_all([grads, swap(grads, axis, mask)], f"{axis}{mask}_grads", after)
        if step == len(rounds) - 3:
            activated = hand_over(activated, (grads,))
    mine = sum_all(mine, "mine_sums", (grads,), HINT // 4)
    mine = sum_all([mine, passed], "last_sums", (), HINT)
    axis, mask = rounds[-1]
    feature_grad, weight_grad, bias_grad = finish(
        [mine], [grads, swap(grads, axis, mask)], scale
    )
    return activated, feature_grad, weight_grad, bias_grad[0]


def solution(mesh):
    return jax.shard_map(
        local,
        mesh=mesh,
        in_specs=(
            P(("col", "row"), None),
            P(),
            P(),
            P(("row", "col"), None),
            P("row", "col", None, None, None),
            P("row", "col", None),
            P("row", "col"),
        ),
        out_specs=(P(("row", "col"), None), P(("col", "row"), None), P(), P()),
        check_vma=False,
    )
```

```python
import functools

import jax
import jax.numpy as jnp
from jax import lax
from jax.experimental import pallas as pl
from jax.experimental.pallas import tpu as pltpu
from jax.sharding import PartitionSpec as P

TILE = 128
PAD = 8
F32 = jnp.float32
BF16 = jnp.bfloat16
HIGHEST = lax.Precision.HIGHEST
MIB = 1024 * 1024
HINT = 2 * 10**9


def nt_dot(lhs, rhs, **kw):
    return lax.dot_general(lhs, rhs, (((1,), (1,)), ((), ())), preferred_element_type=F32, **kw)


def tn_dot(lhs, rhs, **kw):
    return lax.dot_general(lhs, rhs, (((0,), (0,)), ((), ())), preferred_element_type=F32, **kw)


def split(value):
    high = value.astype(BF16)
    low = (value - high.astype(F32)).astype(BF16)
    return high, low


def total_of(refs):
    total = refs[0][...]
    for ref in refs[1:]:
        total = total + ref[...]
    return total


def vmem(*shape, dtype=F32):
    return pltpu.VMEM(shape, dtype)


def hbm(*shape, dtype=F32):
    return jax.ShapeDtypeStruct(shape, dtype)


def call(kernel, name, args, outs, flops=0, room=4, scratch=(), before=(), before_specs=()):
    spec = pl.BlockSpec(memory_space=pltpu.VMEM)
    return pl.pallas_call(
        kernel,
        out_shape=tuple(outs),
        in_specs=list(before_specs) + [spec] * len(args),
        out_specs=(spec,) * len(outs),
        scratch_shapes=list(scratch),
        compiler_params=pltpu.CompilerParams(vmem_limit_bytes=room * MIB),
        cost_estimate=pl.CostEstimate(
            flops=int(flops), bytes_accessed=sum(4 * arg.size for arg in args), transcendentals=0
        ),
        name=name,
    )(*before, *[pltpu.with_memory_space_constraint(arg, pltpu.VMEM) for arg in args])


def densify_kernel(
    tile_cols, pieces, slots_hbm, counts_hbm, tiles_hbm, dense_ref, col_ref,
    tiles, col_acc, slots, counts, sems, slot_sem, count_sem,
):
    slot_total = tiles.shape[0]
    piece = slot_total // pieces
    slot_copy = pltpu.make_async_copy(slots_hbm.at[0], slots, slot_sem)
    count_copy = pltpu.make_async_copy(counts_hbm, counts, count_sem)
    slot_copy.start()
    count_copy.start()
    copies = [
        pltpu.make_async_copy(
            tiles_hbm.at[pl.ds(p * piece, piece)], tiles.at[pl.ds(p * piece, piece)], sems.at[p]
        )
        for p in range(pieces)
    ]
    for copy in copies:
        copy.start()
    if slot_total * TILE * TILE < dense_ref.shape[0] * dense_ref.shape[1]:
        dense_ref[...] = jnp.zeros_like(dense_ref)
    col_acc[...] = jnp.zeros_like(col_acc)
    slot_copy.wait()
    count_copy.wait()
    live = counts[0, 0]

    def place(k, carry):
        slot = slots[k]
        r = slot // tile_cols
        c = slot % tile_cols
        keep = jnp.where(k < live, 1.0, 0.0)
        tile = (tiles[k].astype(F32) * keep).astype(BF16)
        dense_ref[
            pl.ds(pl.multiple_of(r * TILE, TILE), TILE), pl.ds(pl.multiple_of(c * TILE, TILE), TILE)
        ] = tile
        col_acc[c] += jnp.sum(tile.reshape(TILE // 16, 16, TILE), axis=0, dtype=BF16).astype(F32)
        return carry

    for p in range(pieces):
        copies[p].wait()
        lax.fori_loop(p * piece, (p + 1) * piece, place, 0, unroll=4)
    col_ref[...] = jnp.sum(col_acc[...], axis=1)


def densify(slots, counts, tiles, tile_rows, tile_cols):
    pieces = 8
    return call(
        functools.partial(densify_kernel, tile_cols, pieces),
        "densify",
        (),
        (vmem(tile_rows * TILE, tile_cols * TILE, dtype=BF16), vmem(tile_cols, TILE)),
        flops=tiles.size * 400,
        room=16,
        scratch=(
            vmem(*tiles.shape, dtype=jnp.int32),
            vmem(tile_cols, 16, TILE),
            pltpu.SMEM(slots.shape[1:], jnp.int32),
            pltpu.SMEM(counts.shape, jnp.int32),
            pltpu.SemaphoreType.DMA((pieces,)),
            pltpu.SemaphoreType.DMA,
            pltpu.SemaphoreType.DMA,
        ),
        before=(
            pltpu.with_memory_space_constraint(slots, pltpu.HBM),
            counts,
            pltpu.with_memory_space_constraint(tiles, pltpu.HBM),
        ),
        before_specs=[pl.BlockSpec(memory_space=pl.ANY)] * 3,
    )


def row_kernel(dense_ref, row_ref):
    ones = jnp.ones((8, TILE), BF16)
    tile_rows = row_ref.shape[0]
    for r in range(tile_rows):
        total = dense_ref[pl.ds(r * TILE, TILE), pl.ds(0, TILE)].astype(F32)
        for c in range(1, dense_ref.shape[1] // TILE):
            total += dense_ref[pl.ds(r * TILE, TILE), pl.ds(c * TILE, TILE)].astype(F32)
        row_ref[pl.ds(r, 1), :] = nt_dot(ones, total.astype(BF16))[0:1, :]


def row_totals(dense):
    return call(row_kernel, "row_totals", (dense,), (vmem(dense.shape[0] // TILE, TILE),))[0]


def message_kernel(block_ref, own_ref, got_ref, *refs):
    out_ref = refs[-1]
    node_rows = block_ref.shape[0]
    out_ref[pl.ds(0, node_rows), :] = block_ref[...]
    out_ref[pl.ds(node_rows, own_ref.shape[0]), :] = own_ref[...] + got_ref[...]


def message(block, own, got, after):
    rows = block.shape[0] + own.shape[0]
    return call(
        message_kernel, "message", (block, own, got, *after), (vmem(rows, block.shape[1]),)
    )[0]


def scales_kernel(skip, *refs):
    parts, (wide_ref, scale_ref) = refs[:-2], refs[-2:]
    total = parts[0][skip:, :]
    for ref in parts[1:]:
        total = total + ref[skip:, :]
    scale = lax.rsqrt(1.0 + total)
    for c in range(scale.shape[0]):
        wide_ref[pl.ds(c * TILE, TILE), :] = jnp.broadcast_to(scale[c : c + 1, :], (TILE, TILE)).T
    scale_ref[...] = scale


def source_scales(parts, skip):
    tile_cols = parts[0].shape[0] - skip
    return call(
        functools.partial(scales_kernel, skip),
        "source_scales",
        parts,
        (vmem(tile_cols * TILE, TILE), vmem(tile_cols, TILE)),
    )


def forward_chunks(peers, dense_ref, row_ref, rhs, out_ref):
    col = lax.axis_index("col")
    node_rows, width = out_ref.shape[1] - PAD, out_ref.shape[2]
    own_tiles = node_rows // TILE
    for h, m in enumerate(peers):
        peer = col ^ m
        start = pl.multiple_of(peer * node_rows, node_rows)
        both = jnp.dot(dense_ref[pl.ds(start, node_rows), :], rhs[...], preferred_element_type=F32)
        out_ref[h, pl.ds(0, node_rows), :] = both[:, :width] + both[:, width:]
        out_ref[h, pl.ds(node_rows, PAD), :] = jnp.zeros((PAD, width), F32)
        for t in range(own_tiles):
            out_ref[h, pl.ds(node_rows + t, 1), :] = row_ref[pl.ds(peer * own_tiles + t, 1), :]


def forward_first_kernel(peers, row_count, *refs):
    dense_ref, row_ref, wide_ref = refs[:3]
    blocks = refs[3 : 3 + row_count]
    out_ref, rhs = refs[3 + row_count :]
    row = lax.axis_index("row")
    node_rows, width = blocks[0].shape
    for m in range(row_count):
        start = pl.multiple_of((row ^ m) * node_rows, node_rows)
        block = blocks[m][pl.ds(0, node_rows), :]
        high, low = split(block * wide_ref[pl.ds(start, node_rows), :])
        rhs[pl.ds(start, node_rows), :width] = high
        rhs[pl.ds(start, node_rows), width:] = low
    forward_chunks(peers, dense_ref, row_ref, rhs, out_ref)


def forward_second_kernel(peers, dense_ref, row_ref, rhs, out_ref):
    forward_chunks(peers, dense_ref, row_ref, rhs, out_ref)


def forward_first(peers, dense, row_sums, wide, blocks):
    node_rows, width = blocks[0].shape
    cols = dense.shape[1]
    return call(
        functools.partial(forward_first_kernel, peers, len(blocks)),
        "forward_first",
        (dense, row_sums, wide, *blocks),
        (vmem(len(peers), node_rows + PAD, width), vmem(cols, 2 * width, dtype=BF16)),
        flops=4 * len(peers) * node_rows * cols * width,
    )


def forward_second(peers, dense, row_sums, rhs, node_rows):
    cols = dense.shape[1]
    width = rhs.shape[1] // 2
    return call(
        functools.partial(forward_second_kernel, peers),
        "forward_second",
        (dense, row_sums, rhs),
        (vmem(len(peers), node_rows + PAD, width),),
        flops=4 * len(peers) * node_rows * cols * width,
    )[0]


def pair_kernel(kept_ref, got_ref, *outs):
    for h, out_ref in enumerate(outs):
        out_ref[...] = kept_ref[h + 1] + got_ref[h + 1]


def pair_sums(kept, got):
    return call(
        pair_kernel, "pair_sums", (kept, got), [vmem(*kept.shape[1:])] * (kept.shape[0] - 1)
    )


def node_kernel(*refs):
    kept_ref, got_ref = refs[:2]
    others = refs[2:-7]
    cot_ref, weight_ref, bias_ref, act_ref, back_ref, agg_ref, pre_ref = refs[-7:]
    node_rows, width = cot_ref.shape
    total = kept_ref[0] + got_ref[0]
    for ref in others:
        total = total + ref[...]
    own_tiles = node_rows // TILE
    scale = lax.rsqrt(1.0 + total[node_rows:, :])
    wide = jnp.concatenate(
        [jnp.broadcast_to(scale[t : t + 1, :], (TILE, TILE)).T for t in range(own_tiles)], axis=0
    )
    flat = jnp.concatenate([scale[t : t + 1, :] for t in range(own_tiles)], axis=1)
    weight = weight_ref[...]
    aggregated = total[:node_rows, :] * wide
    preact = (
        jnp.dot(aggregated, weight, precision=HIGHEST, preferred_element_type=F32) + bias_ref[...]
    )
    logistic = jax.nn.sigmoid(preact)
    act_ref[...] = preact * logistic
    pre_grad = cot_ref[...] * logistic * (1.0 + preact * (1.0 - logistic))
    back_ref[...] = nt_dot(weight, pre_grad, precision=HIGHEST) * flat
    agg_ref[...] = aggregated
    pre_ref[...] = pre_grad


def node_step(kept, got, others, cotangent, weight, bias):
    node_rows, width = cotangent.shape
    return call(
        node_kernel,
        "node_step",
        (kept, got, *others, cotangent, weight, bias),
        (
            vmem(node_rows, width),
            vmem(width, node_rows),
            vmem(node_rows, width),
            vmem(node_rows, width),
        ),
        flops=24 * node_rows * width * width,
    )


def folds(rows, width, node_rows):
    step = -(-rows * width // node_rows // 8) * 8
    return [(at, min(step, rows - at)) for at in range(0, rows, step)], step


def grads_kernel(back_ref, agg_ref, pre_ref, out_ref, sums):
    width, node_rows = back_ref.shape
    pre_grad = pre_ref[...]
    out_ref[pl.ds(0, width), :] = back_ref[...]
    sums[pl.ds(0, width), :] = tn_dot(agg_ref[...], pre_grad, precision=HIGHEST)
    sums[pl.ds(width, PAD), :] = jnp.broadcast_to(
        jnp.sum(pre_grad, axis=0, keepdims=True), (PAD, width)
    )
    parts, step = folds(width + PAD, width, node_rows)
    out_ref[pl.ds(width, step), :] = jnp.zeros((step, node_rows), F32)
    for j, (at, size) in enumerate(parts):
        out_ref[pl.ds(width, size), pl.ds(j * width, width)] = sums[pl.ds(at, size), :]


def weight_parts(back, aggregated, pre_grad):
    node_rows, width = aggregated.shape
    step = folds(width + PAD, width, node_rows)[1]
    return call(
        grads_kernel,
        "weight_parts",
        (back, aggregated, pre_grad),
        (vmem(width + step, node_rows),),
        flops=12 * node_rows * width * width,
        scratch=(vmem(width + PAD, width),),
    )[0]


def backward_chunks(peers, dense_ref, lhs, outs):
    row = lax.axis_index("row")
    width, node_rows = outs[0].shape
    for m, out_ref in zip(peers, outs):
        start = pl.multiple_of((row ^ m) * node_rows, node_rows)
        both = jnp.dot(lhs[...], dense_ref[:, pl.ds(start, node_rows)], preferred_element_type=F32)
        out_ref[...] = both[:width, :] + both[width:, :]


def backward_first_kernel(peers, col_count, *refs):
    outs, lhs = refs[-1 - len(peers) : -1], refs[-1]
    dense_ref, blocks = refs[0], refs[1 : 1 + col_count]
    col = lax.axis_index("col")
    width, node_rows = outs[0].shape
    for m, block in enumerate(blocks):
        start = pl.multiple_of((col ^ m) * node_rows, node_rows)
        high, low = split(block[pl.ds(0, width), :])
        lhs[:width, pl.ds(start, node_rows)] = high
        lhs[width:, pl.ds(start, node_rows)] = low
    backward_chunks(peers, dense_ref, lhs, outs)


def unfold_kernel(own_ref, got_ref, out_ref):
    rows, width = out_ref.shape
    for j, (at, size) in enumerate(folds(rows, width, own_ref.shape[1])[0]):
        part = pl.ds(width, size), pl.ds(j * width, width)
        out_ref[pl.ds(at, size), :] = own_ref[part] + got_ref[part]


def unfold_sums(own, got, width):
    return call(unfold_kernel, "core_grads", (own, got), (vmem(width + PAD, width),))[0]


def backward_second_kernel(peers, dense_ref, lhs, *outs):
    backward_chunks(peers, dense_ref, lhs, outs)


def backward_first(peers, dense, blocks, width, after):
    rows = dense.shape[0]
    node_rows = blocks[0].shape[1]
    out = call(
        functools.partial(backward_first_kernel, peers, len(blocks)),
        "backward_first",
        (dense, *blocks, *after),
        [vmem(width, node_rows)] * len(peers) + [vmem(2 * width, rows, dtype=BF16)],
        flops=4 * len(peers) * node_rows * rows * width,
    )
    return dict(zip(peers, out)), out[-1]


def backward_second(peers, dense, lhs, node_rows):
    rows = dense.shape[0]
    width = lhs.shape[0] // 2
    out = call(
        functools.partial(backward_second_kernel, peers),
        "backward_second",
        (dense, lhs),
        [vmem(width, node_rows)] * len(peers),
        flops=4 * len(peers) * node_rows * rows * width,
    )
    return dict(zip(peers, out))


def sum_kernel(count, *refs):
    refs[-1][...] = total_of(refs[:count])


def sum_all(parts, name, after=(), flops=0):
    kernel = functools.partial(sum_kernel, len(parts))
    return call(kernel, name, (*parts, *after), (vmem(*parts[0].shape),), flops=flops)[0]


def hand_over_kernel(value_ref, *refs):
    refs[-1][...] = value_ref[...]


def hand_over(value, after):
    return call(hand_over_kernel, "hand_over", (value, *after), (hbm(*value.shape),))[0]


def finish_kernel(parts, *refs):
    total = total_of(refs[:parts])
    grads = total_of(refs[parts:-4])
    scale_ref, out_ref, weight_ref, bias_ref = refs[-4:]
    row = lax.axis_index("row")
    width, node_rows = total.shape
    own_tiles = node_rows // TILE
    for t in range(own_tiles):
        part = total[:, t * TILE : (t + 1) * TILE] * scale_ref[pl.ds(row * own_tiles + t, 1), :]
        out_ref[pl.ds(t * TILE, TILE), :] = part.T
    weight_ref[...] = grads[:width, :]
    bias_ref[...] = grads[width : width + 1, :]


def finish(parts, grads, scale):
    width, node_rows = parts[0].shape
    return call(
        functools.partial(finish_kernel, len(parts)),
        "finish",
        (*parts, *grads, scale),
        (hbm(node_rows, width), hbm(width, width), hbm(1, width)),
    )


def swap(value, axis, mask):
    count = lax.axis_size(axis)
    return lax.ppermute(value, axis, [(i, i ^ mask) for i in range(count)])


def local(features, weight, bias_vector, out_grad, adj_tiles, tile_slots, tile_counts):
    row_count = lax.axis_size("row")
    col_count = lax.axis_size("col")
    node_rows, width = features.shape
    tile_rows = node_rows * col_count // TILE
    tile_cols = node_rows * row_count // TILE
    top = row_count // 2
    near, far = list(range(top)), list(range(top, row_count))
    even, odd = list(range(0, col_count, 2)), list(range(1, col_count, 2))

    blocks = [None] * row_count
    blocks[0] = features
    blocks[top] = swap(features, "row", top)
    for m in near[1:]:
        blocks[m] = swap(features, "row", m)
    dense, col_sums = densify(tile_slots[0], tile_counts, adj_tiles[0, 0], tile_rows, tile_cols)
    sent = message(blocks[top], col_sums, swap(col_sums, "row", top), blocks[1:top])
    row_sums = row_totals(dense)
    blocks[top:] = [sent] + [swap(sent, "row", m) for m in near[1:]]
    wide, scale = source_scales(blocks[top:], node_rows)

    given, rhs = forward_first(odd, dense, row_sums, wide, blocks)
    got = swap(given, "col", 1)
    kept = forward_second(even, dense, row_sums, rhs, node_rows)
    paired = pair_sums(kept, got)
    others = [swap(part, "col", m) for m, part in zip(even[1:], paired)]
    activated, back, aggregated, pre_grad = node_step(
        kept, got, others, out_grad, weight, bias_vector[None, :]
    )

    backs = [None] * col_count
    for m in even[1:]:
        backs[m] = swap(back, "col", m)
    backs[0] = weight_parts(back, aggregated, pre_grad)
    for m in even:
        backs[m | 1] = swap(backs[m], "col", 1)
    grads = unfold_sums(backs[0], backs[1], width)
    grads = sum_all([grads, swap(grads, "row", top)], "top_grads", (), HINT)
    chunks, lhs = backward_first(far, dense, backs, width, ())
    ahead = [chunks[top]] + [swap(chunks[top | m], "row", m) for m in near[1:]]
    chunks = backward_second(near, dense, lhs, node_rows)
    mine = [chunks[0]] + [swap(chunks[m], "row", m) for m in near[1:]]
    ahead = sum_all(ahead, "ahead_sums", (), HINT)
    passed = swap(ahead, "row", top)

    rounds = [("col", 1 << b) for b in range(1, col_count.bit_length() - 1)]
    rounds = [("row", 1)] * (top > 1) + rounds
    rounds += [("row", 1 << b) for b in range(1, top.bit_length() - 1)]
    grads = sum_all([grads], "held_grads", (lhs,))
    for step, (axis, mask) in enumerate(rounds[:-1]):
        after = (ahead,) if (axis, mask) == ("row", 1) else ()
        grads = sum_all([grads, swap(grads, axis, mask)], f"{axis}{mask}_grads", after)
        if step == len(rounds) - 3:
            activated = hand_over(activated, (grads,))
    mine = sum_all(mine, "mine_sums", (grads,), HINT // 4)
    mine = sum_all([mine, passed], "last_sums", (), HINT)
    axis, mask = rounds[-1]
    feature_grad, weight_grad, bias_grad = finish(
        [mine], [grads, swap(grads, axis, mask)], scale
    )
    return activated, feature_grad, weight_grad, bias_grad[0]


def solution(mesh):
    return jax.shard_map(
        local,
        mesh=mesh,
        in_specs=(
            P(("col", "row"), None),
            P(),
            P(),
            P(("row", "col"), None),
            P("row", "col", None, None, None),
            P("row", "col", None),
            P("row", "col"),
        ),
        out_specs=(P(("row", "col"), None), P(("col", "row"), None), P(), P()),
        check_vma=False,
    )
```

```python
import functools

import jax
import jax.numpy as jnp
from jax import lax
from jax.experimental import pallas as pl
from jax.experimental.pallas import tpu as pltpu
from jax.sharding import PartitionSpec as P

TILE = 128
PAD = 8
F32 = jnp.float32
BF16 = jnp.bfloat16
HIGHEST = lax.Precision.HIGHEST
MIB = 1024 * 1024
HINT = 2 * 10**9


def nt_dot(lhs, rhs, **kw):
    return lax.dot_general(lhs, rhs, (((1,), (1,)), ((), ())), preferred_element_type=F32, **kw)


def tn_dot(lhs, rhs, **kw):
    return lax.dot_general(lhs, rhs, (((0,), (0,)), ((), ())), preferred_element_type=F32, **kw)


def split(value):
    high = value.astype(BF16)
    low = (value - high.astype(F32)).astype(BF16)
    return high, low


def total_of(refs):
    total = refs[0][...]
    for ref in refs[1:]:
        total = total + ref[...]
    return total


def vmem(*shape, dtype=F32):
    return pltpu.VMEM(shape, dtype)


def hbm(*shape, dtype=F32):
    return jax.ShapeDtypeStruct(shape, dtype)


def call(kernel, name, args, outs, flops=0, room=4, scratch=(), before=(), before_specs=()):
    spec = pl.BlockSpec(memory_space=pltpu.VMEM)
    return pl.pallas_call(
        kernel,
        out_shape=tuple(outs),
        in_specs=list(before_specs) + [spec] * len(args),
        out_specs=(spec,) * len(outs),
        scratch_shapes=list(scratch),
        compiler_params=pltpu.CompilerParams(vmem_limit_bytes=room * MIB),
        cost_estimate=pl.CostEstimate(
            flops=int(flops), bytes_accessed=sum(4 * arg.size for arg in args), transcendentals=0
        ),
        name=name,
    )(*before, *[pltpu.with_memory_space_constraint(arg, pltpu.VMEM) for arg in args])


def densify_kernel(
    tile_cols, pieces, slots_hbm, counts_hbm, tiles_hbm, dense_ref, col_ref,
    tiles, col_acc, slots, counts, sems, slot_sem, count_sem,
):
    slot_total = tiles.shape[0]
    piece = slot_total // pieces
    slot_copy = pltpu.make_async_copy(slots_hbm.at[0], slots, slot_sem)
    count_copy = pltpu.make_async_copy(counts_hbm, counts, count_sem)
    slot_copy.start()
    count_copy.start()
    copies = [
        pltpu.make_async_copy(
            tiles_hbm.at[pl.ds(p * piece, piece)], tiles.at[pl.ds(p * piece, piece)], sems.at[p]
        )
        for p in range(pieces)
    ]
    for copy in copies:
        copy.start()
    if slot_total * TILE * TILE < dense_ref.shape[0] * dense_ref.shape[1]:
        dense_ref[...] = jnp.zeros_like(dense_ref)
    col_acc[...] = jnp.zeros_like(col_acc)
    slot_copy.wait()
    count_copy.wait()
    live = counts[0, 0]

    def place(k, carry):
        slot = slots[k]
        r = slot // tile_cols
        c = slot % tile_cols
        keep = jnp.where(k < live, 1.0, 0.0)
        tile = (tiles[k].astype(F32) * keep).astype(BF16)
        dense_ref[
            pl.ds(pl.multiple_of(r * TILE, TILE), TILE), pl.ds(pl.multiple_of(c * TILE, TILE), TILE)
        ] = tile
        col_acc[c] += jnp.sum(tile.reshape(TILE // 16, 16, TILE), axis=0, dtype=BF16).astype(F32)
        return carry

    for p in range(pieces):
        copies[p].wait()
        lax.fori_loop(p * piece, (p + 1) * piece, place, 0, unroll=4)
    col_ref[...] = jnp.sum(col_acc[...], axis=1)


def densify(slots, counts, tiles, tile_rows, tile_cols):
    pieces = 8
    return call(
        functools.partial(densify_kernel, tile_cols, pieces),
        "densify",
        (),
        (vmem(tile_rows * TILE, tile_cols * TILE, dtype=BF16), vmem(tile_cols, TILE)),
        flops=tiles.size * 400,
        room=16,
        scratch=(
            vmem(*tiles.shape, dtype=jnp.int32),
            vmem(tile_cols, 16, TILE),
            pltpu.SMEM(slots.shape[1:], jnp.int32),
            pltpu.SMEM(counts.shape, jnp.int32),
            pltpu.SemaphoreType.DMA((pieces,)),
            pltpu.SemaphoreType.DMA,
            pltpu.SemaphoreType.DMA,
        ),
        before=(
            pltpu.with_memory_space_constraint(slots, pltpu.HBM),
            counts,
            pltpu.with_memory_space_constraint(tiles, pltpu.HBM),
        ),
        before_specs=[pl.BlockSpec(memory_space=pl.ANY)] * 3,
    )


def row_kernel(dense_ref, row_ref):
    ones = jnp.ones((8, TILE), BF16)
    tile_rows = row_ref.shape[0]
    for r in range(tile_rows):
        total = dense_ref[pl.ds(r * TILE, TILE), pl.ds(0, TILE)].astype(F32)
        for c in range(1, dense_ref.shape[1] // TILE):
            total += dense_ref[pl.ds(r * TILE, TILE), pl.ds(c * TILE, TILE)].astype(F32)
        row_ref[pl.ds(r, 1), :] = nt_dot(ones, total.astype(BF16))[0:1, :]


def row_totals(dense):
    return call(row_kernel, "row_totals", (dense,), (vmem(dense.shape[0] // TILE, TILE),))[0]


def message_kernel(block_ref, own_ref, got_ref, *refs):
    out_ref = refs[-1]
    node_rows = block_ref.shape[0]
    out_ref[pl.ds(0, node_rows), :] = block_ref[...]
    out_ref[pl.ds(node_rows, own_ref.shape[0]), :] = own_ref[...] + got_ref[...]


def message(block, own, got, after):
    rows = block.shape[0] + own.shape[0]
    return call(
        message_kernel, "message", (block, own, got, *after), (vmem(rows, block.shape[1]),)
    )[0]


def scales_kernel(skip, *refs):
    parts, (wide_ref, scale_ref) = refs[:-2], refs[-2:]
    total = parts[0][skip:, :]
    for ref in parts[1:]:
        total = total + ref[skip:, :]
    scale = lax.rsqrt(1.0 + total)
    for c in range(scale.shape[0]):
        wide_ref[pl.ds(c * TILE, TILE), :] = jnp.broadcast_to(scale[c : c + 1, :], (TILE, TILE)).T
    scale_ref[...] = scale


def source_scales(parts, skip):
    tile_cols = parts[0].shape[0] - skip
    return call(
        functools.partial(scales_kernel, skip),
        "source_scales",
        parts,
        (vmem(tile_cols * TILE, TILE), vmem(tile_cols, TILE)),
    )


def forward_chunks(peers, dense_ref, row_ref, rhs, out_ref):
    col = lax.axis_index("col")
    node_rows, width = out_ref.shape[1] - PAD, out_ref.shape[2]
    own_tiles = node_rows // TILE
    for h, m in enumerate(peers):
        peer = col ^ m
        start = pl.multiple_of(peer * node_rows, node_rows)
        both = jnp.dot(dense_ref[pl.ds(start, node_rows), :], rhs[...], preferred_element_type=F32)
        out_ref[h, pl.ds(0, node_rows), :] = both[:, :width] + both[:, width:]
        out_ref[h, pl.ds(node_rows, PAD), :] = jnp.zeros((PAD, width), F32)
        for t in range(own_tiles):
            out_ref[h, pl.ds(node_rows + t, 1), :] = row_ref[pl.ds(peer * own_tiles + t, 1), :]


def forward_first_kernel(peers, row_count, *refs):
    dense_ref, row_ref, wide_ref = refs[:3]
    blocks = refs[3 : 3 + row_count]
    out_ref, rhs = refs[3 + row_count :]
    row = lax.axis_index("row")
    node_rows, width = blocks[0].shape
    for m in range(row_count):
        start = pl.multiple_of((row ^ m) * node_rows, node_rows)
        block = blocks[m][pl.ds(0, node_rows), :]
        high, low = split(block * wide_ref[pl.ds(start, node_rows), :])
        rhs[pl.ds(start, node_rows), :width] = high
        rhs[pl.ds(start, node_rows), width:] = low
    forward_chunks(peers, dense_ref, row_ref, rhs, out_ref)


def forward_second_kernel(peers, dense_ref, row_ref, rhs, out_ref):
    forward_chunks(peers, dense_ref, row_ref, rhs, out_ref)


def forward_first(peers, dense, row_sums, wide, blocks):
    node_rows, width = blocks[0].shape
    cols = dense.shape[1]
    return call(
        functools.partial(forward_first_kernel, peers, len(blocks)),
        "forward_first",
        (dense, row_sums, wide, *blocks),
        (vmem(len(peers), node_rows + PAD, width), vmem(cols, 2 * width, dtype=BF16)),
        flops=4 * len(peers) * node_rows * cols * width,
    )


def forward_second(peers, dense, row_sums, rhs, node_rows):
    cols = dense.shape[1]
    width = rhs.shape[1] // 2
    return call(
        functools.partial(forward_second_kernel, peers),
        "forward_second",
        (dense, row_sums, rhs),
        (vmem(len(peers), node_rows + PAD, width),),
        flops=4 * len(peers) * node_rows * cols * width,
    )[0]


def pair_kernel(kept_ref, got_ref, *outs):
    for h, out_ref in enumerate(outs):
        out_ref[...] = kept_ref[h + 1] + got_ref[h + 1]


def pair_sums(kept, got):
    return call(
        pair_kernel, "pair_sums", (kept, got), [vmem(*kept.shape[1:])] * (kept.shape[0] - 1)
    )


def node_kernel(*refs):
    kept_ref, got_ref = refs[:2]
    others = refs[2:-7]
    cot_ref, weight_ref, bias_ref, act_ref, back_ref, agg_ref, pre_ref = refs[-7:]
    node_rows, width = cot_ref.shape
    total = kept_ref[0] + got_ref[0]
    for ref in others:
        total = total + ref[...]
    own_tiles = node_rows // TILE
    scale = lax.rsqrt(1.0 + total[node_rows:, :])
    wide = jnp.concatenate(
        [jnp.broadcast_to(scale[t : t + 1, :], (TILE, TILE)).T for t in range(own_tiles)], axis=0
    )
    flat = jnp.concatenate([scale[t : t + 1, :] for t in range(own_tiles)], axis=1)
    weight = weight_ref[...]
    aggregated = total[:node_rows, :] * wide
    preact = (
        jnp.dot(aggregated, weight, precision=HIGHEST, preferred_element_type=F32) + bias_ref[...]
    )
    logistic = jax.nn.sigmoid(preact)
    act_ref[...] = preact * logistic
    pre_grad = cot_ref[...] * logistic * (1.0 + preact * (1.0 - logistic))
    back_ref[...] = nt_dot(weight, pre_grad, precision=HIGHEST) * flat
    agg_ref[...] = aggregated
    pre_ref[...] = pre_grad


def node_step(kept, got, others, cotangent, weight, bias):
    node_rows, width = cotangent.shape
    return call(
        node_kernel,
        "node_step",
        (kept, got, *others, cotangent, weight, bias),
        (
            vmem(node_rows, width),
            vmem(width, node_rows),
            vmem(node_rows, width),
            vmem(node_rows, width),
        ),
        flops=24 * node_rows * width * width,
    )


def folds(rows, width, node_rows):
    step = -(-rows * width // node_rows // 8) * 8
    return [(at, min(step, rows - at)) for at in range(0, rows, step)], step


def grads_kernel(back_ref, agg_ref, pre_ref, out_ref, sums):
    width, node_rows = back_ref.shape
    pre_grad = pre_ref[...]
    out_ref[pl.ds(0, width), :] = back_ref[...]
    sums[pl.ds(0, width), :] = tn_dot(agg_ref[...], pre_grad, precision=HIGHEST)
    sums[pl.ds(width, PAD), :] = jnp.broadcast_to(
        jnp.sum(pre_grad, axis=0, keepdims=True), (PAD, width)
    )
    parts, step = folds(width + PAD, width, node_rows)
    out_ref[pl.ds(width, step), :] = jnp.zeros((step, node_rows), F32)
    for j, (at, size) in enumerate(parts):
        out_ref[pl.ds(width, size), pl.ds(j * width, width)] = sums[pl.ds(at, size), :]


def weight_parts(back, aggregated, pre_grad):
    node_rows, width = aggregated.shape
    step = folds(width + PAD, width, node_rows)[1]
    return call(
        grads_kernel,
        "weight_parts",
        (back, aggregated, pre_grad),
        (vmem(width + step, node_rows),),
        flops=12 * node_rows * width * width,
        scratch=(vmem(width + PAD, width),),
    )[0]


def backward_chunks(peers, dense_ref, lhs, outs):
    row = lax.axis_index("row")
    width, node_rows = outs[0].shape
    for m, out_ref in zip(peers, outs):
        start = pl.multiple_of((row ^ m) * node_rows, node_rows)
        both = jnp.dot(lhs[...], dense_ref[:, pl.ds(start, node_rows)], preferred_element_type=F32)
        out_ref[...] = both[:width, :] + both[width:, :]


def backward_first_kernel(peers, col_count, *refs):
    outs, lhs = refs[-1 - len(peers) : -1], refs[-1]
    dense_ref, blocks = refs[0], refs[1 : 1 + col_count]
    col = lax.axis_index("col")
    width, node_rows = outs[0].shape
    for m, block in enumerate(blocks):
        start = pl.multiple_of((col ^ m) * node_rows, node_rows)
        high, low = split(block[pl.ds(0, width), :])
        lhs[:width, pl.ds(start, node_rows)] = high
        lhs[width:, pl.ds(start, node_rows)] = low
    backward_chunks(peers, dense_ref, lhs, outs)


def unfold_kernel(own_ref, got_ref, out_ref):
    rows, width = out_ref.shape
    for j, (at, size) in enumerate(folds(rows, width, own_ref.shape[1])[0]):
        part = pl.ds(width, size), pl.ds(j * width, width)
        out_ref[pl.ds(at, size), :] = own_ref[part] + got_ref[part]


def unfold_sums(own, got, width):
    return call(unfold_kernel, "core_grads", (own, got), (vmem(width + PAD, width),))[0]


def backward_second_kernel(peers, dense_ref, lhs, *refs):
    backward_chunks(peers, dense_ref, lhs, refs[-len(peers) :])


def backward_first(peers, dense, blocks, width, after):
    rows = dense.shape[0]
    node_rows = blocks[0].shape[1]
    out = call(
        functools.partial(backward_first_kernel, peers, len(blocks)),
        "backward_first",
        (dense, *blocks, *after),
        [vmem(width, node_rows)] * len(peers) + [vmem(2 * width, rows, dtype=BF16)],
        flops=4 * len(peers) * node_rows * rows * width,
    )
    return dict(zip(peers, out)), out[-1]


def backward_second(peers, dense, lhs, node_rows, after):
    rows = dense.shape[0]
    width = lhs.shape[0] // 2
    out = call(
        functools.partial(backward_second_kernel, peers),
        "backward_second",
        (dense, lhs, *after),
        [vmem(width, node_rows)] * len(peers),
        flops=4 * len(peers) * node_rows * rows * width,
    )
    return dict(zip(peers, out))


def sum_kernel(count, *refs):
    refs[-1][...] = total_of(refs[:count])


def sum_all(parts, name, after=(), flops=0):
    kernel = functools.partial(sum_kernel, len(parts))
    return call(kernel, name, (*parts, *after), (vmem(*parts[0].shape),), flops=flops)[0]


def hand_over_kernel(value_ref, *refs):
    refs[-1][...] = value_ref[...]


def hand_over(value, after):
    return call(hand_over_kernel, "hand_over", (value, *after), (hbm(*value.shape),))[0]


def finish_kernel(parts, *refs):
    total = total_of(refs[:parts])
    grads = total_of(refs[parts:-4])
    scale_ref, out_ref, weight_ref, bias_ref = refs[-4:]
    row = lax.axis_index("row")
    width, node_rows = total.shape
    own_tiles = node_rows // TILE
    for t in range(own_tiles):
        part = total[:, t * TILE : (t + 1) * TILE] * scale_ref[pl.ds(row * own_tiles + t, 1), :]
        out_ref[pl.ds(t * TILE, TILE), :] = part.T
    weight_ref[...] = grads[:width, :]
    bias_ref[...] = grads[width : width + 1, :]


def finish(parts, grads, scale):
    width, node_rows = parts[0].shape
    return call(
        functools.partial(finish_kernel, len(parts)),
        "finish",
        (*parts, *grads, scale),
        (hbm(node_rows, width), hbm(width, width), hbm(1, width)),
    )


def swap(value, axis, mask):
    count = lax.axis_size(axis)
    return lax.ppermute(value, axis, [(i, i ^ mask) for i in range(count)])


def local(features, weight, bias_vector, out_grad, adj_tiles, tile_slots, tile_counts):
    row_count = lax.axis_size("row")
    col_count = lax.axis_size("col")
    node_rows, width = features.shape
    tile_rows = node_rows * col_count // TILE
    tile_cols = node_rows * row_count // TILE
    top = row_count // 2
    near, far = list(range(top)), list(range(top, row_count))
    even, odd = list(range(0, col_count, 2)), list(range(1, col_count, 2))

    blocks = [None] * row_count
    blocks[0] = features
    blocks[top] = swap(features, "row", top)
    for m in near[1:]:
        blocks[m] = swap(features, "row", m)
    dense, col_sums = densify(tile_slots[0], tile_counts, adj_tiles[0, 0], tile_rows, tile_cols)
    sent = message(blocks[top], col_sums, swap(col_sums, "row", top), blocks[1:top])
    row_sums = row_totals(dense)
    blocks[top:] = [sent] + [swap(sent, "row", m) for m in near[1:]]
    wide, scale = source_scales(blocks[top:], node_rows)

    given, rhs = forward_first(odd, dense, row_sums, wide, blocks)
    got = swap(given, "col", 1)
    kept = forward_second(even, dense, row_sums, rhs, node_rows)
    paired = pair_sums(kept, got)
    others = [swap(part, "col", m) for m, part in zip(even[1:], paired)]
    activated, back, aggregated, pre_grad = node_step(
        kept, got, others, out_grad, weight, bias_vector[None, :]
    )

    backs = [None] * col_count
    for m in even[1:]:
        backs[m] = swap(back, "col", m)
    backs[0] = weight_parts(back, aggregated, pre_grad)
    for m in even:
        backs[m | 1] = swap(backs[m], "col", 1)
    grads = unfold_sums(backs[0], backs[1], width)
    grads = sum_all([grads, swap(grads, "row", top)], "top_grads", (), HINT)
    chunks, lhs = backward_first(far, dense, backs, width, ())
    ahead = [chunks[top]] + [swap(chunks[top | m], "row", m) for m in near[1:]]
    chunks = backward_second(near, dense, lhs, node_rows, (grads,))
    mine = [chunks[0]] + [swap(chunks[m], "row", m) for m in near[1:]]
    ahead = sum_all(ahead, "ahead_sums", (), HINT)
    passed = swap(ahead, "row", top)

    rounds = [("col", 1 << b) for b in range(1, col_count.bit_length() - 1)]
    rounds = [("row", 1)] * (top > 1) + rounds
    rounds += [("row", 1 << b) for b in range(1, top.bit_length() - 1)]
    grads = sum_all([grads], "held_grads", (lhs,))
    for step, (axis, mask) in enumerate(rounds[:-1]):
        after = (ahead,) if False else ()
        grads = sum_all([grads, swap(grads, axis, mask)], f"{axis}{mask}_grads", after)
        if step == len(rounds) - 3:
            activated = hand_over(activated, (grads,))
    mine = sum_all(mine, "mine_sums", (grads,), HINT // 4)
    mine = sum_all([mine, passed], "last_sums", (), HINT)
    axis, mask = rounds[-1]
    feature_grad, weight_grad, bias_grad = finish(
        [mine], [grads, swap(grads, axis, mask)], scale
    )
    return activated, feature_grad, weight_grad, bias_grad[0]


def solution(mesh):
    return jax.shard_map(
        local,
        mesh=mesh,
        in_specs=(
            P(("col", "row"), None),
            P(),
            P(),
            P(("row", "col"), None),
            P("row", "col", None, None, None),
            P("row", "col", None),
            P("row", "col"),
        ),
        out_specs=(P(("row", "col"), None), P(("col", "row"), None), P(), P()),
        check_vma=False,
    )
```

```python
import functools

import jax
import jax.numpy as jnp
from jax import lax
from jax.experimental import pallas as pl
from jax.experimental.pallas import tpu as pltpu
from jax.sharding import PartitionSpec as P

TILE = 128
PAD = 8
F32 = jnp.float32
BF16 = jnp.bfloat16
HIGHEST = lax.Precision.HIGHEST
MIB = 1024 * 1024
HINT = 2 * 10**9


def nt_dot(lhs, rhs, **kw):
    return lax.dot_general(lhs, rhs, (((1,), (1,)), ((), ())), preferred_element_type=F32, **kw)


def tn_dot(lhs, rhs, **kw):
    return lax.dot_general(lhs, rhs, (((0,), (0,)), ((), ())), preferred_element_type=F32, **kw)


def split(value):
    high = value.astype(BF16)
    low = (value - high.astype(F32)).astype(BF16)
    return high, low


def total_of(refs):
    total = refs[0][...]
    for ref in refs[1:]:
        total = total + ref[...]
    return total


def vmem(*shape, dtype=F32):
    return pltpu.VMEM(shape, dtype)


def hbm(*shape, dtype=F32):
    return jax.ShapeDtypeStruct(shape, dtype)


def call(kernel, name, args, outs, flops=0, room=4, scratch=(), before=(), before_specs=()):
    spec = pl.BlockSpec(memory_space=pltpu.VMEM)
    return pl.pallas_call(
        kernel,
        out_shape=tuple(outs),
        in_specs=list(before_specs) + [spec] * len(args),
        out_specs=(spec,) * len(outs),
        scratch_shapes=list(scratch),
        compiler_params=pltpu.CompilerParams(vmem_limit_bytes=room * MIB),
        cost_estimate=pl.CostEstimate(
            flops=int(flops), bytes_accessed=sum(4 * arg.size for arg in args), transcendentals=0
        ),
        name=name,
    )(*before, *[pltpu.with_memory_space_constraint(arg, pltpu.VMEM) for arg in args])


def densify_kernel(
    tile_cols, pieces, slots_hbm, counts_hbm, tiles_hbm, dense_ref, col_ref,
    tiles, col_acc, slots, counts, sems, slot_sem, count_sem,
):
    slot_total = tiles.shape[0]
    piece = slot_total // pieces
    slot_copy = pltpu.make_async_copy(slots_hbm.at[0], slots, slot_sem)
    count_copy = pltpu.make_async_copy(counts_hbm, counts, count_sem)
    slot_copy.start()
    count_copy.start()
    copies = [
        pltpu.make_async_copy(
            tiles_hbm.at[pl.ds(p * piece, piece)], tiles.at[pl.ds(p * piece, piece)], sems.at[p]
        )
        for p in range(pieces)
    ]
    for copy in copies:
        copy.start()
    if slot_total * TILE * TILE < dense_ref.shape[0] * dense_ref.shape[1]:
        dense_ref[...] = jnp.zeros_like(dense_ref)
    col_acc[...] = jnp.zeros_like(col_acc)
    slot_copy.wait()
    count_copy.wait()
    live = counts[0, 0]

    def place(k, carry):
        slot = slots[k]
        r = slot // tile_cols
        c = slot % tile_cols
        keep = jnp.where(k < live, 1.0, 0.0)
        tile = (tiles[k].astype(F32) * keep).astype(BF16)
        dense_ref[
            pl.ds(pl.multiple_of(r * TILE, TILE), TILE), pl.ds(pl.multiple_of(c * TILE, TILE), TILE)
        ] = tile
        col_acc[c] += jnp.sum(tile.reshape(TILE // 16, 16, TILE), axis=0, dtype=BF16).astype(F32)
        return carry

    for p in range(pieces):
        copies[p].wait()
        lax.fori_loop(p * piece, (p + 1) * piece, place, 0, unroll=4)
    col_ref[...] = jnp.sum(col_acc[...], axis=1)


def densify(slots, counts, tiles, tile_rows, tile_cols):
    pieces = 8
    return call(
        functools.partial(densify_kernel, tile_cols, pieces),
        "densify",
        (),
        (vmem(tile_rows * TILE, tile_cols * TILE, dtype=BF16), vmem(tile_cols, TILE)),
        flops=tiles.size * 400,
        room=16,
        scratch=(
            vmem(*tiles.shape, dtype=jnp.int32),
            vmem(tile_cols, 16, TILE),
            pltpu.SMEM(slots.shape[1:], jnp.int32),
            pltpu.SMEM(counts.shape, jnp.int32),
            pltpu.SemaphoreType.DMA((pieces,)),
            pltpu.SemaphoreType.DMA,
            pltpu.SemaphoreType.DMA,
        ),
        before=(
            pltpu.with_memory_space_constraint(slots, pltpu.HBM),
            counts,
            pltpu.with_memory_space_constraint(tiles, pltpu.HBM),
        ),
        before_specs=[pl.BlockSpec(memory_space=pl.ANY)] * 3,
    )


def row_kernel(dense_ref, row_ref):
    ones = jnp.ones((8, TILE), BF16)
    tile_rows = row_ref.shape[0]
    for r in range(tile_rows):
        total = dense_ref[pl.ds(r * TILE, TILE), pl.ds(0, TILE)].astype(F32)
        for c in range(1, dense_ref.shape[1] // TILE):
            total += dense_ref[pl.ds(r * TILE, TILE), pl.ds(c * TILE, TILE)].astype(F32)
        row_ref[pl.ds(r, 1), :] = nt_dot(ones, total.astype(BF16))[0:1, :]


def row_totals(dense):
    return call(row_kernel, "row_totals", (dense,), (vmem(dense.shape[0] // TILE, TILE),))[0]


def message_kernel(block_ref, own_ref, got_ref, *refs):
    out_ref = refs[-1]
    node_rows = block_ref.shape[0]
    out_ref[pl.ds(0, node_rows), :] = block_ref[...]
    out_ref[pl.ds(node_rows, own_ref.shape[0]), :] = own_ref[...] + got_ref[...]


def message(block, own, got, after):
    rows = block.shape[0] + own.shape[0]
    return call(
        message_kernel, "message", (block, own, got, *after), (vmem(rows, block.shape[1]),)
    )[0]


def scales_kernel(skip, *refs):
    parts, (wide_ref, scale_ref) = refs[:-2], refs[-2:]
    total = parts[0][skip:, :]
    for ref in parts[1:]:
        total = total + ref[skip:, :]
    scale = lax.rsqrt(1.0 + total)
    for c in range(scale.shape[0]):
        wide_ref[pl.ds(c * TILE, TILE), :] = jnp.broadcast_to(scale[c : c + 1, :], (TILE, TILE)).T
    scale_ref[...] = scale


def source_scales(parts, skip):
    tile_cols = parts[0].shape[0] - skip
    return call(
        functools.partial(scales_kernel, skip),
        "source_scales",
        parts,
        (vmem(tile_cols * TILE, TILE), vmem(tile_cols, TILE)),
    )


def forward_chunks(peers, dense_ref, row_ref, rhs, out_ref):
    col = lax.axis_index("col")
    node_rows, width = out_ref.shape[1] - PAD, out_ref.shape[2]
    own_tiles = node_rows // TILE
    for h, m in enumerate(peers):
        peer = col ^ m
        start = pl.multiple_of(peer * node_rows, node_rows)
        both = jnp.dot(dense_ref[pl.ds(start, node_rows), :], rhs[...], preferred_element_type=F32)
        out_ref[h, pl.ds(0, node_rows), :] = both[:, :width] + both[:, width:]
        out_ref[h, pl.ds(node_rows, PAD), :] = jnp.zeros((PAD, width), F32)
        for t in range(own_tiles):
            out_ref[h, pl.ds(node_rows + t, 1), :] = row_ref[pl.ds(peer * own_tiles + t, 1), :]


def forward_first_kernel(peers, row_count, *refs):
    dense_ref, row_ref, wide_ref = refs[:3]
    blocks = refs[3 : 3 + row_count]
    out_ref, rhs = refs[3 + row_count :]
    row = lax.axis_index("row")
    node_rows, width = blocks[0].shape
    for m in range(row_count):
        start = pl.multiple_of((row ^ m) * node_rows, node_rows)
        block = blocks[m][pl.ds(0, node_rows), :]
        high, low = split(block * wide_ref[pl.ds(start, node_rows), :])
        rhs[pl.ds(start, node_rows), :width] = high
        rhs[pl.ds(start, node_rows), width:] = low
    forward_chunks(peers, dense_ref, row_ref, rhs, out_ref)


def forward_second_kernel(peers, dense_ref, row_ref, rhs, out_ref):
    forward_chunks(peers, dense_ref, row_ref, rhs, out_ref)


def forward_first(peers, dense, row_sums, wide, blocks):
    node_rows, width = blocks[0].shape
    cols = dense.shape[1]
    return call(
        functools.partial(forward_first_kernel, peers, len(blocks)),
        "forward_first",
        (dense, row_sums, wide, *blocks),
        (vmem(len(peers), node_rows + PAD, width), vmem(cols, 2 * width, dtype=BF16)),
        flops=4 * len(peers) * node_rows * cols * width,
    )


def forward_second(peers, dense, row_sums, rhs, node_rows):
    cols = dense.shape[1]
    width = rhs.shape[1] // 2
    return call(
        functools.partial(forward_second_kernel, peers),
        "forward_second",
        (dense, row_sums, rhs),
        (vmem(len(peers), node_rows + PAD, width),),
        flops=4 * len(peers) * node_rows * cols * width,
    )[0]


def pair_kernel(kept_ref, got_ref, *outs):
    for h, out_ref in enumerate(outs):
        out_ref[...] = kept_ref[h + 1] + got_ref[h + 1]


def pair_sums(kept, got):
    return call(
        pair_kernel, "pair_sums", (kept, got), [vmem(*kept.shape[1:])] * (kept.shape[0] - 1)
    )


def node_kernel(*refs):
    kept_ref, got_ref = refs[:2]
    others = refs[2:-7]
    cot_ref, weight_ref, bias_ref, act_ref, back_ref, agg_ref, pre_ref = refs[-7:]
    node_rows, width = cot_ref.shape
    total = kept_ref[0] + got_ref[0]
    for ref in others:
        total = total + ref[...]
    own_tiles = node_rows // TILE
    scale = lax.rsqrt(1.0 + total[node_rows:, :])
    wide = jnp.concatenate(
        [jnp.broadcast_to(scale[t : t + 1, :], (TILE, TILE)).T for t in range(own_tiles)], axis=0
    )
    flat = jnp.concatenate([scale[t : t + 1, :] for t in range(own_tiles)], axis=1)
    weight = weight_ref[...]
    aggregated = total[:node_rows, :] * wide
    preact = (
        jnp.dot(aggregated, weight, precision=HIGHEST, preferred_element_type=F32) + bias_ref[...]
    )
    logistic = jax.nn.sigmoid(preact)
    act_ref[...] = preact * logistic
    pre_grad = cot_ref[...] * logistic * (1.0 + preact * (1.0 - logistic))
    back_ref[...] = nt_dot(weight, pre_grad, precision=HIGHEST) * flat
    agg_ref[...] = aggregated
    pre_ref[...] = pre_grad


def node_step(kept, got, others, cotangent, weight, bias):
    node_rows, width = cotangent.shape
    return call(
        node_kernel,
        "node_step",
        (kept, got, *others, cotangent, weight, bias),
        (
            vmem(node_rows, width),
            vmem(width, node_rows),
            vmem(node_rows, width),
            vmem(node_rows, width),
        ),
        flops=24 * node_rows * width * width,
    )


def folds(rows, width, node_rows):
    step = -(-rows * width // node_rows // 8) * 8
    return [(at, min(step, rows - at)) for at in range(0, rows, step)], step


def grads_kernel(back_ref, agg_ref, pre_ref, out_ref, sums):
    width, node_rows = back_ref.shape
    pre_grad = pre_ref[...]
    out_ref[pl.ds(0, width), :] = back_ref[...]
    sums[pl.ds(0, width), :] = tn_dot(agg_ref[...], pre_grad, precision=HIGHEST)
    sums[pl.ds(width, PAD), :] = jnp.broadcast_to(
        jnp.sum(pre_grad, axis=0, keepdims=True), (PAD, width)
    )
    parts, step = folds(width + PAD, width, node_rows)
    out_ref[pl.ds(width, step), :] = jnp.zeros((step, node_rows), F32)
    for j, (at, size) in enumerate(parts):
        out_ref[pl.ds(width, size), pl.ds(j * width, width)] = sums[pl.ds(at, size), :]


def weight_parts(back, aggregated, pre_grad):
    node_rows, width = aggregated.shape
    step = folds(width + PAD, width, node_rows)[1]
    return call(
        grads_kernel,
        "weight_parts",
        (back, aggregated, pre_grad),
        (vmem(width + step, node_rows),),
        flops=12 * node_rows * width * width,
        scratch=(vmem(width + PAD, width),),
    )[0]


def backward_chunks(peers, dense_ref, lhs, outs):
    row = lax.axis_index("row")
    width, node_rows = outs[0].shape
    for m, out_ref in zip(peers, outs):
        start = pl.multiple_of((row ^ m) * node_rows, node_rows)
        both = jnp.dot(lhs[...], dense_ref[:, pl.ds(start, node_rows)], preferred_element_type=F32)
        out_ref[...] = both[:width, :] + both[width:, :]


def backward_first_kernel(peers, col_count, *refs):
    outs, lhs = refs[-1 - len(peers) : -1], refs[-1]
    dense_ref, blocks = refs[0], refs[1 : 1 + col_count]
    col = lax.axis_index("col")
    width, node_rows = outs[0].shape
    for m, block in enumerate(blocks):
        start = pl.multiple_of((col ^ m) * node_rows, node_rows)
        high, low = split(block[pl.ds(0, width), :])
        lhs[:width, pl.ds(start, node_rows)] = high
        lhs[width:, pl.ds(start, node_rows)] = low
    backward_chunks(peers, dense_ref, lhs, outs)


def unfold_kernel(own_ref, got_ref, out_ref):
    rows, width = out_ref.shape
    for j, (at, size) in enumerate(folds(rows, width, own_ref.shape[1])[0]):
        part = pl.ds(width, size), pl.ds(j * width, width)
        out_ref[pl.ds(at, size), :] = own_ref[part] + got_ref[part]


def unfold_sums(own, got, width):
    return call(unfold_kernel, "core_grads", (own, got), (vmem(width + PAD, width),))[0]


def backward_second_kernel(peers, dense_ref, lhs, *refs):
    backward_chunks(peers, dense_ref, lhs, refs[-len(peers) :])


def backward_first(peers, dense, blocks, width, after):
    rows = dense.shape[0]
    node_rows = blocks[0].shape[1]
    out = call(
        functools.partial(backward_first_kernel, peers, len(blocks)),
        "backward_first",
        (dense, *blocks, *after),
        [vmem(width, node_rows)] * len(peers) + [vmem(2 * width, rows, dtype=BF16)],
        flops=4 * len(peers) * node_rows * rows * width,
    )
    return dict(zip(peers, out)), out[-1]


def backward_second(peers, dense, lhs, node_rows, after):
    rows = dense.shape[0]
    width = lhs.shape[0] // 2
    out = call(
        functools.partial(backward_second_kernel, peers),
        "backward_second",
        (dense, lhs, *after),
        [vmem(width, node_rows)] * len(peers),
        flops=4 * len(peers) * node_rows * rows * width,
    )
    return dict(zip(peers, out))


def sum_kernel(count, *refs):
    refs[-1][...] = total_of(refs[:count])


def sum_all(parts, name, after=(), flops=0):
    kernel = functools.partial(sum_kernel, len(parts))
    return call(kernel, name, (*parts, *after), (vmem(*parts[0].shape),), flops=flops)[0]


def hand_over_kernel(value_ref, *refs):
    refs[-1][...] = value_ref[...]


def hand_over(value, after):
    return call(hand_over_kernel, "hand_over", (value, *after), (hbm(*value.shape),))[0]


def finish_kernel(parts, *refs):
    total = total_of(refs[:parts])
    grads = total_of(refs[parts:-4])
    scale_ref, out_ref, weight_ref, bias_ref = refs[-4:]
    row = lax.axis_index("row")
    width, node_rows = total.shape
    own_tiles = node_rows // TILE
    for t in range(own_tiles):
        part = total[:, t * TILE : (t + 1) * TILE] * scale_ref[pl.ds(row * own_tiles + t, 1), :]
        out_ref[pl.ds(t * TILE, TILE), :] = part.T
    weight_ref[...] = grads[:width, :]
    bias_ref[...] = grads[width : width + 1, :]


def finish(parts, grads, scale):
    width, node_rows = parts[0].shape
    return call(
        functools.partial(finish_kernel, len(parts)),
        "finish",
        (*parts, *grads, scale),
        (hbm(node_rows, width), hbm(width, width), hbm(1, width)),
    )


def swap(value, axis, mask):
    count = lax.axis_size(axis)
    return lax.ppermute(value, axis, [(i, i ^ mask) for i in range(count)])


def local(features, weight, bias_vector, out_grad, adj_tiles, tile_slots, tile_counts):
    row_count = lax.axis_size("row")
    col_count = lax.axis_size("col")
    node_rows, width = features.shape
    tile_rows = node_rows * col_count // TILE
    tile_cols = node_rows * row_count // TILE
    top = row_count // 2
    near, far = list(range(top)), list(range(top, row_count))
    even, odd = list(range(0, col_count, 2)), list(range(1, col_count, 2))

    blocks = [None] * row_count
    blocks[0] = features
    blocks[top] = swap(features, "row", top)
    for m in near[1:]:
        blocks[m] = swap(features, "row", m)
    dense, col_sums = densify(tile_slots[0], tile_counts, adj_tiles[0, 0], tile_rows, tile_cols)
    sent = message(blocks[top], col_sums, swap(col_sums, "row", top), blocks[1:top])
    row_sums = row_totals(dense)
    blocks[top:] = [sent] + [swap(sent, "row", m) for m in near[1:]]
    wide, scale = source_scales(blocks[top:], node_rows)

    given, rhs = forward_first(odd, dense, row_sums, wide, blocks)
    got = swap(given, "col", 1)
    kept = forward_second(even, dense, row_sums, rhs, node_rows)
    paired = pair_sums(kept, got)
    others = [swap(part, "col", m) for m, part in zip(even[1:], paired)]
    activated, back, aggregated, pre_grad = node_step(
        kept, got, others, out_grad, weight, bias_vector[None, :]
    )

    backs = [None] * col_count
    for m in even[1:]:
        backs[m] = swap(back, "col", m)
    backs[0] = weight_parts(back, aggregated, pre_grad)
    for m in even:
        backs[m | 1] = swap(backs[m], "col", 1)
    grads = unfold_sums(backs[0], backs[1], width)
    grads = sum_all([grads, swap(grads, "row", top)], "top_grads", (), HINT)
    chunks, lhs = backward_first(far, dense, backs, width, ())
    ahead = [chunks[top]] + [swap(chunks[top | m], "row", m) for m in near[1:]]
    chunks = backward_second(near, dense, lhs, node_rows, (grads,))
    mine = [chunks[0]] + [swap(chunks[m], "row", m) for m in near[1:]]
    ahead = sum_all(ahead, "ahead_sums", (), HINT)
    passed = swap(ahead, "row", top)

    rounds = [("col", 1 << b) for b in range(1, col_count.bit_length() - 1)]
    row_rounds = [("row", 1 << b) for b in range(top.bit_length() - 1)]
    rounds = row_rounds[-1:] + rounds + row_rounds[:-1]
    grads = sum_all([grads], "held_grads", (lhs,))
    for step, (axis, mask) in enumerate(rounds[:-1]):
        after = (ahead,) if False else ()
        grads = sum_all([grads, swap(grads, axis, mask)], f"{axis}{mask}_grads", after)
        if step == len(rounds) - 3:
            activated = hand_over(activated, (grads,))
    mine = sum_all(mine, "mine_sums", (grads,), HINT // 4)
    mine = sum_all([mine, passed], "last_sums", (), HINT)
    axis, mask = rounds[-1]
    feature_grad, weight_grad, bias_grad = finish(
        [mine], [grads, swap(grads, axis, mask)], scale
    )
    return activated, feature_grad, weight_grad, bias_grad[0]


def solution(mesh):
    return jax.shard_map(
        local,
        mesh=mesh,
        in_specs=(
            P(("col", "row"), None),
            P(),
            P(),
            P(("row", "col"), None),
            P("row", "col", None, None, None),
            P("row", "col", None),
            P("row", "col"),
        ),
        out_specs=(P(("row", "col"), None), P(("col", "row"), None), P(), P()),
        check_vma=False,
    )
```

```python
import functools

import jax
import jax.numpy as jnp
from jax import lax
from jax.experimental import pallas as pl
from jax.experimental.pallas import tpu as pltpu
from jax.sharding import PartitionSpec as P

TILE = 128
PAD = 8
F32 = jnp.float32
BF16 = jnp.bfloat16
HIGHEST = lax.Precision.HIGHEST
MIB = 1024 * 1024
HINT = 2 * 10**9


def nt_dot(lhs, rhs, **kw):
    return lax.dot_general(lhs, rhs, (((1,), (1,)), ((), ())), preferred_element_type=F32, **kw)


def tn_dot(lhs, rhs, **kw):
    return lax.dot_general(lhs, rhs, (((0,), (0,)), ((), ())), preferred_element_type=F32, **kw)


def split(value):
    high = value.astype(BF16)
    low = (value - high.astype(F32)).astype(BF16)
    return high, low


def total_of(refs):
    total = refs[0][...]
    for ref in refs[1:]:
        total = total + ref[...]
    return total


def vmem(*shape, dtype=F32):
    return pltpu.VMEM(shape, dtype)


def hbm(*shape, dtype=F32):
    return jax.ShapeDtypeStruct(shape, dtype)


def call(kernel, name, args, outs, flops=0, room=4, scratch=(), before=(), before_specs=()):
    spec = pl.BlockSpec(memory_space=pltpu.VMEM)
    return pl.pallas_call(
        kernel,
        out_shape=tuple(outs),
        in_specs=list(before_specs) + [spec] * len(args),
        out_specs=(spec,) * len(outs),
        scratch_shapes=list(scratch),
        compiler_params=pltpu.CompilerParams(vmem_limit_bytes=room * MIB),
        cost_estimate=pl.CostEstimate(
            flops=int(flops), bytes_accessed=sum(4 * arg.size for arg in args), transcendentals=0
        ),
        name=name,
    )(*before, *[pltpu.with_memory_space_constraint(arg, pltpu.VMEM) for arg in args])


def densify_kernel(
    tile_cols, pieces, slots_hbm, counts_hbm, tiles_hbm, dense_ref, col_ref,
    tiles, col_acc, slots, counts, sems, slot_sem, count_sem,
):
    slot_total = tiles.shape[0]
    piece = slot_total // pieces
    slot_copy = pltpu.make_async_copy(slots_hbm.at[0], slots, slot_sem)
    count_copy = pltpu.make_async_copy(counts_hbm, counts, count_sem)
    slot_copy.start()
    count_copy.start()
    copies = [
        pltpu.make_async_copy(
            tiles_hbm.at[pl.ds(p * piece, piece)], tiles.at[pl.ds(p * piece, piece)], sems.at[p]
        )
        for p in range(pieces)
    ]
    for copy in copies:
        copy.start()
    if slot_total * TILE * TILE < dense_ref.shape[0] * dense_ref.shape[1]:
        dense_ref[...] = jnp.zeros_like(dense_ref)
    col_acc[...] = jnp.zeros_like(col_acc)
    slot_copy.wait()
    count_copy.wait()
    live = counts[0, 0]

    def place(k, carry):
        slot = slots[k]
        r = slot // tile_cols
        c = slot % tile_cols
        keep = jnp.where(k < live, 1.0, 0.0)
        tile = (tiles[k].astype(F32) * keep).astype(BF16)
        dense_ref[
            pl.ds(pl.multiple_of(r * TILE, TILE), TILE), pl.ds(pl.multiple_of(c * TILE, TILE), TILE)
        ] = tile
        col_acc[c] += jnp.sum(tile.reshape(TILE // 16, 16, TILE), axis=0, dtype=BF16).astype(F32)
        return carry

    for p in range(pieces):
        copies[p].wait()
        lax.fori_loop(p * piece, (p + 1) * piece, place, 0, unroll=8)
    col_ref[...] = jnp.sum(col_acc[...], axis=1)


def densify(slots, counts, tiles, tile_rows, tile_cols):
    pieces = 8
    return call(
        functools.partial(densify_kernel, tile_cols, pieces),
        "densify",
        (),
        (vmem(tile_rows * TILE, tile_cols * TILE, dtype=BF16), vmem(tile_cols, TILE)),
        flops=tiles.size * 400,
        room=16,
        scratch=(
            vmem(*tiles.shape, dtype=jnp.int32),
            vmem(tile_cols, 16, TILE),
            pltpu.SMEM(slots.shape[1:], jnp.int32),
            pltpu.SMEM(counts.shape, jnp.int32),
            pltpu.SemaphoreType.DMA((pieces,)),
            pltpu.SemaphoreType.DMA,
            pltpu.SemaphoreType.DMA,
        ),
        before=(
            pltpu.with_memory_space_constraint(slots, pltpu.HBM),
            counts,
            pltpu.with_memory_space_constraint(tiles, pltpu.HBM),
        ),
        before_specs=[pl.BlockSpec(memory_space=pl.ANY)] * 3,
    )


def row_kernel(dense_ref, row_ref):
    ones = jnp.ones((8, TILE), BF16)
    tile_rows = row_ref.shape[0]
    for r in range(tile_rows):
        total = dense_ref[pl.ds(r * TILE, TILE), pl.ds(0, TILE)].astype(F32)
        for c in range(1, dense_ref.shape[1] // TILE):
            total += dense_ref[pl.ds(r * TILE, TILE), pl.ds(c * TILE, TILE)].astype(F32)
        row_ref[pl.ds(r, 1), :] = nt_dot(ones, total.astype(BF16))[0:1, :]


def row_totals(dense):
    return call(row_kernel, "row_totals", (dense,), (vmem(dense.shape[0] // TILE, TILE),))[0]


def message_kernel(block_ref, own_ref, got_ref, *refs):
    out_ref = refs[-1]
    node_rows = block_ref.shape[0]
    out_ref[pl.ds(0, node_rows), :] = block_ref[...]
    out_ref[pl.ds(node_rows, own_ref.shape[0]), :] = own_ref[...] + got_ref[...]


def message(block, own, got, after):
    rows = block.shape[0] + own.shape[0]
    return call(
        message_kernel, "message", (block, own, got, *after), (vmem(rows, block.shape[1]),)
    )[0]


def scales_kernel(skip, *refs):
    parts, (wide_ref, scale_ref) = refs[:-2], refs[-2:]
    total = parts[0][skip:, :]
    for ref in parts[1:]:
        total = total + ref[skip:, :]
    scale = lax.rsqrt(1.0 + total)
    for c in range(scale.shape[0]):
        wide_ref[pl.ds(c * TILE, TILE), :] = jnp.broadcast_to(scale[c : c + 1, :], (TILE, TILE)).T
    scale_ref[...] = scale


def source_scales(parts, skip):
    tile_cols = parts[0].shape[0] - skip
    return call(
        functools.partial(scales_kernel, skip),
        "source_scales",
        parts,
        (vmem(tile_cols * TILE, TILE), vmem(tile_cols, TILE)),
    )


def forward_chunks(peers, dense_ref, row_ref, rhs, out_ref):
    col = lax.axis_index("col")
    node_rows, width = out_ref.shape[1] - PAD, out_ref.shape[2]
    own_tiles = node_rows // TILE
    for h, m in enumerate(peers):
        peer = col ^ m
        start = pl.multiple_of(peer * node_rows, node_rows)
        both = jnp.dot(dense_ref[pl.ds(start, node_rows), :], rhs[...], preferred_element_type=F32)
        out_ref[h, pl.ds(0, node_rows), :] = both[:, :width] + both[:, width:]
        out_ref[h, pl.ds(node_rows, PAD), :] = jnp.zeros((PAD, width), F32)
        for t in range(own_tiles):
            out_ref[h, pl.ds(node_rows + t, 1), :] = row_ref[pl.ds(peer * own_tiles + t, 1), :]


def forward_first_kernel(peers, row_count, *refs):
    dense_ref, row_ref, wide_ref = refs[:3]
    blocks = refs[3 : 3 + row_count]
    out_ref, rhs = refs[3 + row_count :]
    row = lax.axis_index("row")
    node_rows, width = blocks[0].shape
    for m in range(row_count):
        start = pl.multiple_of((row ^ m) * node_rows, node_rows)
        block = blocks[m][pl.ds(0, node_rows), :]
        high, low = split(block * wide_ref[pl.ds(start, node_rows), :])
        rhs[pl.ds(start, node_rows), :width] = high
        rhs[pl.ds(start, node_rows), width:] = low
    forward_chunks(peers, dense_ref, row_ref, rhs, out_ref)


def forward_second_kernel(peers, dense_ref, row_ref, rhs, out_ref):
    forward_chunks(peers, dense_ref, row_ref, rhs, out_ref)


def forward_first(peers, dense, row_sums, wide, blocks):
    node_rows, width = blocks[0].shape
    cols = dense.shape[1]
    return call(
        functools.partial(forward_first_kernel, peers, len(blocks)),
        "forward_first",
        (dense, row_sums, wide, *blocks),
        (vmem(len(peers), node_rows + PAD, width), vmem(cols, 2 * width, dtype=BF16)),
        flops=4 * len(peers) * node_rows * cols * width,
    )


def forward_second(peers, dense, row_sums, rhs, node_rows):
    cols = dense.shape[1]
    width = rhs.shape[1] // 2
    return call(
        functools.partial(forward_second_kernel, peers),
        "forward_second",
        (dense, row_sums, rhs),
        (vmem(len(peers), node_rows + PAD, width),),
        flops=4 * len(peers) * node_rows * cols * width,
    )[0]


def pair_kernel(kept_ref, got_ref, *outs):
    for h, out_ref in enumerate(outs):
        out_ref[...] = kept_ref[h + 1] + got_ref[h + 1]


def pair_sums(kept, got):
    return call(
        pair_kernel, "pair_sums", (kept, got), [vmem(*kept.shape[1:])] * (kept.shape[0] - 1)
    )


def node_kernel(*refs):
    kept_ref, got_ref = refs[:2]
    others = refs[2:-7]
    cot_ref, weight_ref, bias_ref, act_ref, back_ref, agg_ref, pre_ref = refs[-7:]
    node_rows, width = cot_ref.shape
    total = kept_ref[0] + got_ref[0]
    for ref in others:
        total = total + ref[...]
    own_tiles = node_rows // TILE
    scale = lax.rsqrt(1.0 + total[node_rows:, :])
    wide = jnp.concatenate(
        [jnp.broadcast_to(scale[t : t + 1, :], (TILE, TILE)).T for t in range(own_tiles)], axis=0
    )
    flat = jnp.concatenate([scale[t : t + 1, :] for t in range(own_tiles)], axis=1)
    weight = weight_ref[...]
    aggregated = total[:node_rows, :] * wide
    preact = (
        jnp.dot(aggregated, weight, precision=HIGHEST, preferred_element_type=F32) + bias_ref[...]
    )
    logistic = jax.nn.sigmoid(preact)
    act_ref[...] = preact * logistic
    pre_grad = cot_ref[...] * logistic * (1.0 + preact * (1.0 - logistic))
    back_ref[...] = nt_dot(weight, pre_grad, precision=HIGHEST) * flat
    agg_ref[...] = aggregated
    pre_ref[...] = pre_grad


def node_step(kept, got, others, cotangent, weight, bias):
    node_rows, width = cotangent.shape
    return call(
        node_kernel,
        "node_step",
        (kept, got, *others, cotangent, weight, bias),
        (
            vmem(node_rows, width),
            vmem(width, node_rows),
            vmem(node_rows, width),
            vmem(node_rows, width),
        ),
        flops=24 * node_rows * width * width,
    )


def folds(rows, width, node_rows):
    step = -(-rows * width // node_rows // 8) * 8
    return [(at, min(step, rows - at)) for at in range(0, rows, step)], step


def grads_kernel(back_ref, agg_ref, pre_ref, out_ref, sums):
    width, node_rows = back_ref.shape
    pre_grad = pre_ref[...]
    out_ref[pl.ds(0, width), :] = back_ref[...]
    sums[pl.ds(0, width), :] = tn_dot(agg_ref[...], pre_grad, precision=HIGHEST)
    sums[pl.ds(width, PAD), :] = jnp.broadcast_to(
        jnp.sum(pre_grad, axis=0, keepdims=True), (PAD, width)
    )
    parts, step = folds(width + PAD, width, node_rows)
    out_ref[pl.ds(width, step), :] = jnp.zeros((step, node_rows), F32)
    for j, (at, size) in enumerate(parts):
        out_ref[pl.ds(width, size), pl.ds(j * width, width)] = sums[pl.ds(at, size), :]


def weight_parts(back, aggregated, pre_grad):
    node_rows, width = aggregated.shape
    step = folds(width + PAD, width, node_rows)[1]
    return call(
        grads_kernel,
        "weight_parts",
        (back, aggregated, pre_grad),
        (vmem(width + step, node_rows),),
        flops=12 * node_rows * width * width,
        scratch=(vmem(width + PAD, width),),
    )[0]


def backward_chunks(peers, dense_ref, lhs, outs):
    row = lax.axis_index("row")
    width, node_rows = outs[0].shape
    for m, out_ref in zip(peers, outs):
        start = pl.multiple_of((row ^ m) * node_rows, node_rows)
        both = jnp.dot(lhs[...], dense_ref[:, pl.ds(start, node_rows)], preferred_element_type=F32)
        out_ref[...] = both[:width, :] + both[width:, :]


def backward_first_kernel(peers, col_count, *refs):
    outs, lhs = refs[-1 - len(peers) : -1], refs[-1]
    dense_ref, blocks = refs[0], refs[1 : 1 + col_count]
    col = lax.axis_index("col")
    width, node_rows = outs[0].shape
    for m, block in enumerate(blocks):
        start = pl.multiple_of((col ^ m) * node_rows, node_rows)
        high, low = split(block[pl.ds(0, width), :])
        lhs[:width, pl.ds(start, node_rows)] = high
        lhs[width:, pl.ds(start, node_rows)] = low
    backward_chunks(peers, dense_ref, lhs, outs)


def unfold_kernel(own_ref, got_ref, out_ref):
    rows, width = out_ref.shape
    for j, (at, size) in enumerate(folds(rows, width, own_ref.shape[1])[0]):
        part = pl.ds(width, size), pl.ds(j * width, width)
        out_ref[pl.ds(at, size), :] = own_ref[part] + got_ref[part]


def unfold_sums(own, got, width):
    return call(unfold_kernel, "core_grads", (own, got), (vmem(width + PAD, width),))[0]


def backward_second_kernel(peers, dense_ref, lhs, *refs):
    backward_chunks(peers, dense_ref, lhs, refs[-len(peers) :])


def backward_first(peers, dense, blocks, width, after):
    rows = dense.shape[0]
    node_rows = blocks[0].shape[1]
    out = call(
        functools.partial(backward_first_kernel, peers, len(blocks)),
        "backward_first",
        (dense, *blocks, *after),
        [vmem(width, node_rows)] * len(peers) + [vmem(2 * width, rows, dtype=BF16)],
        flops=4 * len(peers) * node_rows * rows * width,
    )
    return dict(zip(peers, out)), out[-1]


def backward_second(peers, dense, lhs, node_rows, after):
    rows = dense.shape[0]
    width = lhs.shape[0] // 2
    out = call(
        functools.partial(backward_second_kernel, peers),
        "backward_second",
        (dense, lhs, *after),
        [vmem(width, node_rows)] * len(peers),
        flops=4 * len(peers) * node_rows * rows * width,
    )
    return dict(zip(peers, out))


def sum_kernel(count, *refs):
    refs[-1][...] = total_of(refs[:count])


def sum_all(parts, name, after=(), flops=0):
    kernel = functools.partial(sum_kernel, len(parts))
    return call(kernel, name, (*parts, *after), (vmem(*parts[0].shape),), flops=flops)[0]


def hand_over_kernel(value_ref, *refs):
    refs[-1][...] = value_ref[...]


def hand_over(value, after):
    return call(hand_over_kernel, "hand_over", (value, *after), (hbm(*value.shape),))[0]


def finish_kernel(parts, *refs):
    total = total_of(refs[:parts])
    grads = total_of(refs[parts:-4])
    scale_ref, out_ref, weight_ref, bias_ref = refs[-4:]
    row = lax.axis_index("row")
    width, node_rows = total.shape
    own_tiles = node_rows // TILE
    for t in range(own_tiles):
        part = total[:, t * TILE : (t + 1) * TILE] * scale_ref[pl.ds(row * own_tiles + t, 1), :]
        out_ref[pl.ds(t * TILE, TILE), :] = part.T
    weight_ref[...] = grads[:width, :]
    bias_ref[...] = grads[width : width + 1, :]


def finish(parts, grads, scale):
    width, node_rows = parts[0].shape
    return call(
        functools.partial(finish_kernel, len(parts)),
        "finish",
        (*parts, *grads, scale),
        (hbm(node_rows, width), hbm(width, width), hbm(1, width)),
    )


def swap(value, axis, mask):
    count = lax.axis_size(axis)
    return lax.ppermute(value, axis, [(i, i ^ mask) for i in range(count)])


def local(features, weight, bias_vector, out_grad, adj_tiles, tile_slots, tile_counts):
    row_count = lax.axis_size("row")
    col_count = lax.axis_size("col")
    node_rows, width = features.shape
    tile_rows = node_rows * col_count // TILE
    tile_cols = node_rows * row_count // TILE
    top = row_count // 2
    near, far = list(range(top)), list(range(top, row_count))
    even, odd = list(range(0, col_count, 2)), list(range(1, col_count, 2))

    blocks = [None] * row_count
    blocks[0] = features
    blocks[top] = swap(features, "row", top)
    for m in near[1:]:
        blocks[m] = swap(features, "row", m)
    dense, col_sums = densify(tile_slots[0], tile_counts, adj_tiles[0, 0], tile_rows, tile_cols)
    sent = message(blocks[top], col_sums, swap(col_sums, "row", top), blocks[1:top])
    row_sums = row_totals(dense)
    blocks[top:] = [sent] + [swap(sent, "row", m) for m in near[1:]]
    wide, scale = source_scales(blocks[top:], node_rows)

    given, rhs = forward_first(odd, dense, row_sums, wide, blocks)
    got = swap(given, "col", 1)
    kept = forward_second(even, dense, row_sums, rhs, node_rows)
    paired = pair_sums(kept, got)
    others = [swap(part, "col", m) for m, part in zip(even[1:], paired)]
    activated, back, aggregated, pre_grad = node_step(
        kept, got, others, out_grad, weight, bias_vector[None, :]
    )

    backs = [None] * col_count
    for m in even[1:]:
        backs[m] = swap(back, "col", m)
    backs[0] = weight_parts(back, aggregated, pre_grad)
    for m in even:
        backs[m | 1] = swap(backs[m], "col", 1)
    grads = unfold_sums(backs[0], backs[1], width)
    grads = sum_all([grads, swap(grads, "row", top)], "top_grads", (), HINT)
    chunks, lhs = backward_first(far, dense, backs, width, ())
    ahead = [chunks[top]] + [swap(chunks[top | m], "row", m) for m in near[1:]]
    chunks = backward_second(near, dense, lhs, node_rows, (grads,))
    mine = [chunks[0]] + [swap(chunks[m], "row", m) for m in near[1:]]
    ahead = sum_all(ahead, "ahead_sums", (), HINT)
    passed = swap(ahead, "row", top)

    rounds = [("col", 1 << b) for b in range(1, col_count.bit_length() - 1)]
    row_rounds = [("row", 1 << b) for b in range(top.bit_length() - 1)]
    rounds = row_rounds[-1:] + rounds + row_rounds[:-1]
    grads = sum_all([grads], "held_grads", (lhs,))
    for step, (axis, mask) in enumerate(rounds[:-1]):
        after = (ahead,) if False else ()
        grads = sum_all([grads, swap(grads, axis, mask)], f"{axis}{mask}_grads", after)
        if step == len(rounds) - 3:
            activated = hand_over(activated, (grads,))
    mine = sum_all(mine, "mine_sums", (grads,), HINT // 4)
    mine = sum_all([mine, passed], "last_sums", (), HINT)
    axis, mask = rounds[-1]
    feature_grad, weight_grad, bias_grad = finish(
        [mine], [grads, swap(grads, axis, mask)], scale
    )
    return activated, feature_grad, weight_grad, bias_grad[0]


def solution(mesh):
    return jax.shard_map(
        local,
        mesh=mesh,
        in_specs=(
            P(("col", "row"), None),
            P(),
            P(),
            P(("row", "col"), None),
            P("row", "col", None, None, None),
            P("row", "col", None),
            P("row", "col"),
        ),
        out_specs=(P(("row", "col"), None), P(("col", "row"), None), P(), P()),
        check_vma=False,
    )
```
